32 devices in a mesh: seq: 8 (over z, y), tp: 4 (over x, core).
Axes of the slice: x: 2, y: 2, z: 4, core: 2. Of those that a mesh axis runs over, the one named last changes fastest.
Arguments:
- tokens: bfloat16 [2, 3072, 1536], P(None, 'seq'), may hold values from -6 to 6
- mix_gain: float32 [1536], replicated, may hold values from 0.1 to 1.9
- proj_b: bfloat16 [1536, 1536], P(None, 'tp'), may hold values from -0.15625 to 0.15625
- proj_c: bfloat16 [1536, 1536], P(None, 'tp'), may hold values from -0.15625 to 0.15625
- proj_x: bfloat16 [1536, 1536], P(None, 'tp'), may hold values from -0.15625 to 0.15625
- conv_taps: bfloat16 [3, 1536], P(None, 'tp'), may hold values from -3.5 to 3.5
- proj_out: bfloat16 [1536, 1536], P('tp'), may hold values from -0.15625 to 0.15625
- ffn_gain: float32 [1536], replicated, may hold values from 0.1 to 1.9
- w_gate: bfloat16 [1536, 6912], P(None, 'tp'), may hold values from -0.15625 to 0.15625
- w_up: bfloat16 [1536, 6912], P(None, 'tp'), may hold values from -0.15625 to 0.15625
- w_down: bfloat16 [6912, 1536], P('tp'), may hold values from -0.109375 to 0.109375
- cotangent: bfloat16 [2, 3072, 1536], P(None, 'seq'), may hold values from -6 to 6
- seq_lengths: int32 [2, 6], replicated, may hold values from 1 to 2048, 3072 in all within a row
- span_order: int32 [2, 24], replicated, may hold values from 0 to 23, as said below
- keep_mask: int32 [2, 3072], P(None, 'seq'), may hold values 0 or 1
Outputs:
- block_out: bfloat16 [2, 3072, 1536], P(None, 'seq')
- d_tokens: bfloat16 [2, 3072, 1536], P(None, 'seq')
- d_mixgain: float32 [1536], replicated
- d_projb: float32 [1536, 1536], P('seq', 'tp')
- d_projc: float32 [1536, 1536], P('seq', 'tp')
- d_projx: float32 [1536, 1536], P('seq', 'tp')
- d_convtaps: float32 [3, 1536], P(None, 'tp')
- d_projout: float32 [1536, 1536], P('tp', 'seq')
- d_ffngain: float32 [1536], replicated
- d_gate: float32 [1536, 6912], P('seq', 'tp')
- d_up: float32 [1536, 6912], P('seq', 'tp')
- d_down: float32 [6912, 1536], P('tp', 'seq')
The draws below stay inside these ranges and needn't reach their ends.
Inputs may be any that keep to these rules, and one draw needn't show every extreme that they name: Each row of seq_lengths sums to 3072; its longest sequence has exactly 2048 tokens. `span_order`: each row is a permutation of the 24 stream blocks; slot s lies on index s // 3 of seq, and stream block c + 1 always lies on the seq index after that of block c, cyclically.
All inputs are finite; a program needn't handle non-finite values. No bound on the sum of `keep_mask` on one device may be relied on, other than what follows from the above.
Results may differ from the reference program's by a relative error of at most 0.011.
Values may be sent and summed in bfloat16 or wider, within the bound.
A program may use at most 192 MiB of HBM per device.

```python
import math
import jax
import jax.numpy as jnp
import numpy as np
from jax import lax

D = 1536
FF = 6912
KW = 3
SPAN = 128
TOK_DEV = 384
MICRO = 2
NDOC = 6
TOKENS_MB = 3072
SPANS = 24
SEQ_MAX = 2048


def draw_span_order(key, part):
    per_dev = TOK_DEV // SPAN
    ndev = SPANS // per_dev

    def single(sub):
        first, second = jax.random.split(sub)
        shift_by = jax.random.randint(first, (), 0, ndev)
        orders = jax.vmap(lambda kk: jax.random.permutation(kk, per_dev))(jax.random.split(second, ndev))
        devices = jnp.arange(ndev, dtype=jnp.int32)
        base = jnp.mod(devices - shift_by, ndev).astype(jnp.int32)
        return (base[:, None] + ndev * orders.astype(jnp.int32)).reshape(ndev * per_dev)
    return jax.vmap(single)(jax.random.split(key, MICRO)).astype(jnp.int32)


def touch_ends(values, stream_key, low, largest):
    place = [jax.random.randint(jax.random.fold_in(stream_key, axis), (), 0, length) for axis, length in enumerate(values.shape)]
    widest = values.shape.index(max(values.shape))
    next_to = place[:widest] + [(place[widest] + 1) % values.shape[widest]] + place[widest + 1:]
    return values.at[tuple(place)].set(low).at[tuple(next_to)].set(largest)


def level_of(key, dims, cuts, least, largest):
    level = 1.0
    for axis_at, parts in cuts:
        draws = jax.random.uniform(jax.random.fold_in(jax.random.fold_in(key, 6), axis_at), (parts,), jnp.float32, least / len(cuts), largest / len(cuts))
        level = level * jnp.repeat(jnp.exp(draws), dims[axis_at] // parts).reshape((-1,) + (1,) * (len(dims) - 1 - axis_at))
    return level


def profile(number_of, total, bound, slope):
    portions = [(1 << 20) // math.isqrt(grade ** slope) + 1 for grade in range(2, number_of + 1)]
    surplus, given = total - bound - (number_of - 1), [1] * (number_of - 1)
    while surplus > 0:
        candidates = [i for i in range(number_of - 1) if given[i] < bound]
        mass, left = sum([portions[i] for i in candidates]), surplus
        for i in candidates:
            more = min(bound - given[i], max(1, left * portions[i] // mass), surplus)
            given[i] = given[i] + more
            surplus = surplus - more
    return np.array([bound] + given)


def uneven_parts(stream_key, count, total, reach, skew):
    if count == 2:
        one = jax.random.randint(stream_key, (), max(1, total - reach), min(reach, total - 1) + 1)
        return jnp.stack([one, total - one])
    sizes = jnp.asarray(profile(count, total, reach, skew), jnp.int32)
    pairs = (count - 1) // 2
    source_of, receiver = sizes[1:1 + 2 * pairs:2], sizes[2:2 + 2 * pairs:2]
    slack = jnp.minimum(source_of - 1, reach - receiver)
    shifted = jax.random.randint(jax.random.fold_in(stream_key, 1), (pairs,), 0, 1 << 20) % (slack + 1)
    sizes = sizes.at[1:1 + 2 * pairs:2].set(source_of - shifted).at[2:2 + 2 * pairs:2].set(receiver + shifted)
    return sizes[jax.random.permutation(jax.random.fold_in(stream_key, 2), count)]


def gaussian(key, extent, deviation, limit, cuts=(), held_as=jnp.bfloat16):
    loudness = level_of(key, extent, cuts, -0.22, 0.18) if cuts else 1.0
    values = jax.random.normal(key, extent, jnp.float32) * deviation * loudness
    return jnp.minimum(jnp.maximum(values, -limit), limit).astype(held_as)


def setup_inputs(seed: int = 0) -> dict:
    arg_keys = jax.random.split(jax.random.key(seed), 16)
    return {
        "tokens": gaussian(arg_keys[0], (MICRO, TOKENS_MB, D), 1.0, 6.0, ((1, 8),)),
        "mix_gain": jnp.clip(1.0 + 0.18 * jax.random.normal(arg_keys[1], (D,), jnp.float32), 0.1, 1.9),
        "proj_b": gaussian(arg_keys[2], (D, D), D ** -0.5, 0.15625, ((1, 4),)),
        "proj_c": gaussian(arg_keys[3], (D, D), D ** -0.5, 0.15625, ((1, 4),)),
        "proj_x": gaussian(arg_keys[4], (D, D), D ** -0.5, 0.15625, ((1, 4),)),
        "conv_taps": gaussian(arg_keys[5], (KW, D), KW ** -0.5, 3.5, ((1, 4),)),
        "proj_out": gaussian(arg_keys[6], (D, D), D ** -0.5, 0.15625, ((0, 4),)),
        "ffn_gain": jnp.clip(1.0 + 0.18 * jax.random.normal(arg_keys[7], (D,), jnp.float32), 0.1, 1.9),
        "w_gate": gaussian(arg_keys[8], (D, FF), D ** -0.5, 0.15625, ((1, 4),)),
        "w_up": gaussian(arg_keys[9], (D, FF), D ** -0.5, 0.15625, ((1, 4),)),
        "w_down": gaussian(arg_keys[10], (FF, D), (FF // 2) ** -0.5, 0.109375, ((0, 4),)),
        "cotangent": gaussian(arg_keys[11], (MICRO, TOKENS_MB, D), 1.0, 6.0, ((1, 8),)),
        "seq_lengths": jax.vmap(lambda own: uneven_parts(own, NDOC, TOKENS_MB, SEQ_MAX, 2))(jax.random.split(arg_keys[12], MICRO)).reshape((MICRO, NDOC)).astype(jnp.int32),
        "span_order": draw_span_order(jax.random.fold_in(arg_keys[15], 71), 0),
        "keep_mask": touch_ends((jax.random.randint(arg_keys[14], (MICRO, TOKENS_MB), 0, 8) < 7).astype(jnp.int32), jax.random.fold_in(arg_keys[14], 1), 0, 1),
    }


EPSILON = 1e-05

@jax.custom_vjp
def low(v):
    return lax.optimization_barrier(v.astype(jnp.bfloat16)).astype(jnp.float32)

@jax.custom_vjp
def low_back(v):
    return v

def low_keep(v):
    return (low(v), None)

def low_pass(kept, grad):
    return (grad,)

def back_keep(v):
    return (v, None)

def back_low(kept, grad):
    return (low(grad),)
low.defvjp(low_keep, low_pass)
low_back.defvjp(back_keep, back_low)

def matmul_hi(left, right):
    return jnp.dot(left, right, precision=lax.Precision.HIGHEST, preferred_element_type=jnp.float32)

def rms_norm(values, gain):
    return values * lax.rsqrt(lax.optimization_barrier(jnp.mean(values * values, axis=-1, keepdims=True)) + EPSILON) * gain

def forward(valid_far, valid_near, tokens, mix_gain, proj_b, proj_c, proj_x, conv_taps, proj_out, ffn_gain, w_gate, w_up, w_down):
    normed = low(rms_norm(tokens, mix_gain))
    gate_b = low_back(matmul_hi(normed, proj_b))
    gate_c = low_back(matmul_hi(normed, proj_c))
    values = low_back(matmul_hi(normed, proj_x))
    product = low(gate_b * values)
    padded = jnp.concatenate([jnp.zeros((2, product.shape[1]), jnp.float32), product], axis=0)
    convolved = conv_taps[0] * padded[:-2] * valid_far[:, None] + conv_taps[1] * padded[1:-1] * valid_near[:, None] + conv_taps[2] * padded[2:]
    mixed = low(gate_c * convolved)
    branch = low_back(matmul_hi(mixed, proj_out))
    middle = tokens + branch
    second = low(rms_norm(middle, ffn_gain))
    gate_h = low_back(matmul_hi(second, w_gate))
    up_h = low_back(matmul_hi(second, w_up))
    hidden = low(jax.nn.silu(gate_h) * up_h)
    return middle + matmul_hi(hidden, w_down)

def reference(tokens, mix_gain, proj_b, proj_c, proj_x, conv_taps, proj_out, ffn_gain, w_gate, w_up, w_down, cotangent, seq_lengths, span_order, keep_mask):
    weights = [mix_gain.astype(jnp.float32), proj_b.astype(jnp.float32), proj_c.astype(jnp.float32), proj_x.astype(jnp.float32), conv_taps.astype(jnp.float32), proj_out.astype(jnp.float32), ffn_gain.astype(jnp.float32), w_gate.astype(jnp.float32), w_up.astype(jnp.float32), w_down.astype(jnp.float32)]
    totals = [jnp.zeros(w.shape, jnp.float32) for w in weights]
    outputs = []
    input_grads = []
    for batch_idx in range(MICRO):
        order = span_order[batch_idx].astype(jnp.int32)
        inverse = jnp.zeros((SPANS,), jnp.int32).at[order].set(jnp.arange(SPANS, dtype=jnp.int32))

        def to_logical(array):
            return array.reshape((SPANS, SPAN) + array.shape[1:])[inverse].reshape(array.shape)

        def to_stored(array):
            return array.reshape((SPANS, SPAN) + array.shape[1:])[order].reshape(array.shape)
        lengths = seq_lengths[batch_idx].astype(jnp.int32)
        starts = (jnp.cumsum(lengths) - lengths).astype(jnp.int32)
        position = jnp.arange(TOKENS_MB, dtype=jnp.int32)
        doc_start = lax.optimization_barrier(jnp.max(jnp.where(starts[None, :] <= position[:, None], starts[None, :], 0), axis=1)).astype(jnp.int32)
        offset = position - doc_start
        valid_far = (offset >= 2).astype(jnp.float32)
        valid_near = (offset >= 1).astype(jnp.float32)
        inputs = to_logical(tokens[batch_idx].astype(jnp.float32))
        cotan = to_logical(cotangent[batch_idx].astype(jnp.float32) * keep_mask[batch_idx].astype(jnp.float32)[:, None])
        result, pullback = jax.vjp(lambda *params: forward(valid_far, valid_near, *params), inputs, *weights)
        grads = pullback(cotan)
        outputs.append(to_stored(result).astype(jnp.bfloat16))
        input_grads.append(to_stored(grads[0]).astype(jnp.bfloat16))
        totals = [acc + grad for acc, grad in zip(totals, grads[1:])]
    return (jnp.stack(outputs), jnp.stack(input_grads), totals[0], totals[1], totals[2], totals[3], totals[4], totals[5], totals[6], totals[7], totals[8], totals[9])
```

```python
import jax
import jax.numpy as jnp
from jax import lax
from jax.sharding import PartitionSpec as P

SPAN = 128
MICRO = 2


EPSILON = 1e-05


def passed_along(block, axis, distance):
    devices = range(lax.axis_size(axis))
    route = [((i - distance) % len(devices), i) for i in devices]
    return lax.ppermute(block, axis, route)


def body(
    tokens,
    mix_gain,
    proj_b,
    proj_c,
    proj_x,
    conv_taps,
    proj_out,
    ffn_gain,
    w_gate,
    w_up,
    w_down,
    cotangent,
    seq_lengths,
    span_order,
    keep_mask,
):
    f32 = jnp.float32
    bf16 = jnp.bfloat16
    seq_count = lax.axis_size("seq")
    device = lax.axis_index("seq")
    tok_local = tokens.shape[1]
    per_device = tok_local // SPAN
    chan_local = proj_b.shape[1]
    taps = conv_taps.astype(f32)
    gain_one = jnp.zeros(mix_gain.shape, f32)
    gain_two = jnp.zeros(ffn_gain.shape, f32)
    taps_grad = jnp.zeros(taps.shape, f32)
    pending = None
    sharded = None
    outputs = []
    input_grads = []
    for batch_idx in range(MICRO):
        order = span_order[batch_idx]
        mine = lax.dynamic_slice_in_dim(order, device * per_device, per_device)
        lengths = seq_lengths[batch_idx]
        starts = jnp.cumsum(lengths) - lengths
        position = mine[:, None] * SPAN + jnp.arange(SPAN, dtype=jnp.int32)[None, :]
        doc_start = jnp.max(
            jnp.where(starts[None, None, :] <= position[:, :, None], starts[None, None, :], 0),
            axis=2,
        )
        offset = position - doc_start
        valid_far = (offset >= 2).astype(f32)[:, :, None]
        valid_near = (offset >= 1).astype(f32)[:, :, None]
        inputs = tokens[batch_idx].astype(f32)
        scale_one = lax.rsqrt(jnp.mean(inputs * inputs, axis=-1, keepdims=True) + EPSILON)
        normal_one = inputs * scale_one
        normed = (normal_one * mix_gain).astype(bf16)
        gate_b = jnp.dot(normed, proj_b, preferred_element_type=f32)
        gate_c = jnp.dot(normed, proj_c, preferred_element_type=f32)
        values = jnp.dot(normed, proj_x, preferred_element_type=f32)
        product = (gate_b * values).astype(bf16).reshape(per_device, SPAN, chan_local)
        tails = product[:, SPAN - 2 :, :]
        before = passed_along(tails, "seq", 1)
        left_order = lax.dynamic_slice_in_dim(
            order, jnp.mod(device - 1, seq_count) * per_device, per_device
        )
        select = (left_order[None, :] == (mine - 1)[:, None]).astype(bf16)
        prior = jnp.einsum("ak,kjc->ajc", select, before, preferred_element_type=f32).astype(bf16)
        extended = jnp.concatenate([prior, product], axis=1).astype(f32)
        far_term = extended[:, :-2] * valid_far
        near_term = extended[:, 1:-1] * valid_near
        here_term = extended[:, 2:]
        convolved = (taps[0] * far_term + taps[1] * near_term + taps[2] * here_term).reshape(
            tok_local, chan_local
        )
        mixed = (gate_c * convolved).astype(bf16)
        branch_terms = jnp.dot(mixed, proj_out, preferred_element_type=f32)
        middle = inputs + lax.psum(branch_terms.astype(bf16), "tp").astype(f32)
        scale_two = lax.rsqrt(jnp.mean(middle * middle, axis=-1, keepdims=True) + EPSILON)
        normal_two = middle * scale_two
        second_rows = (normal_two * ffn_gain).astype(bf16)
        gate_h = jnp.dot(second_rows, w_gate, preferred_element_type=f32)
        up_h = jnp.dot(second_rows, w_up, preferred_element_type=f32)
        sigma = jax.nn.sigmoid(gate_h)
        silu_h = gate_h * sigma
        hidden = (silu_h * up_h).astype(bf16)
        feed_terms = jnp.dot(hidden, w_down, preferred_element_type=f32)
        outputs.append((middle + lax.psum(feed_terms.astype(bf16), "tp").astype(f32)).astype(bf16))
        grad_out = cotangent[batch_idx] * keep_mask[batch_idx].astype(bf16)[:, None]
        grad_down = jnp.einsum("tf,td->fd", hidden, grad_out, preferred_element_type=f32)
        grad_hidden = jnp.einsum("td,fd->tf", grad_out, w_down, preferred_element_type=f32)
        grad_gate = (grad_hidden * up_h * sigma * (1.0 + gate_h * (1.0 - sigma))).astype(bf16)
        grad_up = (grad_hidden * silu_h).astype(bf16)
        grad_wgate = jnp.einsum("td,tf->df", second_rows, grad_gate, preferred_element_type=f32)
        grad_wup = jnp.einsum("td,tf->df", second_rows, grad_up, preferred_element_type=f32)
        partial_second = jnp.einsum(
            "tf,df->td", grad_gate, w_gate, preferred_element_type=f32
        ) + jnp.einsum("tf,df->td", grad_up, w_up, preferred_element_type=f32)
        grad_second = lax.psum(partial_second.astype(bf16), "tp").astype(f32)
        out_rows = grad_out.astype(f32)
        gain_two = gain_two + jnp.sum(grad_second * normal_two, axis=0)
        weighted_two = grad_second * ffn_gain
        grad_middle = out_rows + scale_two * (
            weighted_two - normal_two * jnp.mean(weighted_two * normal_two, axis=-1, keepdims=True)
        )
        branch_rows = grad_middle.astype(bf16)
        grad_wout = jnp.einsum("tc,td->cd", mixed, branch_rows, preferred_element_type=f32)
        grad_mixed = jnp.einsum("td,cd->tc", branch_rows, proj_out, preferred_element_type=f32)
        grad_c = (grad_mixed * convolved).astype(bf16)
        grad_conv = (grad_mixed * gate_c).reshape(per_device, SPAN, chan_local)
        taps_grad = taps_grad + jnp.stack(
            [
                jnp.sum(grad_conv * far_term, axis=(0, 1)),
                jnp.sum(grad_conv * near_term, axis=(0, 1)),
                jnp.sum(grad_conv * here_term, axis=(0, 1)),
            ]
        )
        grad_ext = (
            jnp.pad(taps[0] * valid_far * grad_conv, ((0, 0), (0, 2), (0, 0)))
            + jnp.pad(taps[1] * valid_near * grad_conv, ((0, 0), (1, 1), (0, 0)))
            + jnp.pad(taps[2] * grad_conv, ((0, 0), (2, 0), (0, 0)))
        )
        outgoing = grad_ext[:, :2, :]
        arrived = passed_along(outgoing, "seq", -1)
        right_order = lax.dynamic_slice_in_dim(
            order, jnp.mod(device + 1, seq_count) * per_device, per_device
        )
        route = (right_order[None, :] == (mine + 1)[:, None]).astype(f32)
        incoming = jnp.einsum(
            "ak,kjc->ajc",
            route,
            arrived,
            precision=lax.Precision.HIGHEST,
            preferred_element_type=f32,
        )
        grad_product = (
            grad_ext[:, 2:, :] + jnp.pad(incoming, ((0, 0), (SPAN - 2, 0), (0, 0)))
        ).reshape(tok_local, chan_local)
        grad_b = (grad_product * values).astype(bf16)
        grad_x = (grad_product * gate_b).astype(bf16)
        grad_wb = jnp.einsum("td,tc->dc", normed, grad_b, preferred_element_type=f32)
        grad_wc = jnp.einsum("td,tc->dc", normed, grad_c, preferred_element_type=f32)
        grad_wx = jnp.einsum("td,tc->dc", normed, grad_x, preferred_element_type=f32)
        partial_first = (
            jnp.einsum("tc,dc->td", grad_b, proj_b, preferred_element_type=f32)
            + jnp.einsum("tc,dc->td", grad_c, proj_c, preferred_element_type=f32)
            + jnp.einsum("tc,dc->td", grad_x, proj_x, preferred_element_type=f32)
        )
        grad_first = lax.psum(partial_first.astype(bf16), "tp").astype(f32)
        gain_one = gain_one + jnp.sum(grad_first * normal_one, axis=0)
        weighted_one = grad_first * mix_gain
        grad_input = grad_middle + scale_one * (
            weighted_one - normal_one * jnp.mean(weighted_one * normal_one, axis=-1, keepdims=True)
        )
        input_rows = grad_input.astype(bf16)
        input_grads.append(input_rows)
        local_grads = (grad_wb, grad_wc, grad_wx, grad_wout, grad_wgate, grad_wup, grad_down)
        pending = (
            local_grads
            if pending is None
            else jax.tree.map(lambda left, right: left + right, pending, local_grads)
        )
    sharded = (
        lax.psum_scatter(pending[0].astype(bf16), "seq", scatter_dimension=0, tiled=True).astype(f32),
        lax.psum_scatter(pending[1].astype(bf16), "seq", scatter_dimension=0, tiled=True).astype(f32),
        lax.psum_scatter(pending[2].astype(bf16), "seq", scatter_dimension=0, tiled=True).astype(f32),
        lax.psum_scatter(pending[3].astype(bf16), "seq", scatter_dimension=1, tiled=True).astype(f32),
        lax.psum_scatter(pending[4].astype(bf16), "seq", scatter_dimension=0, tiled=True).astype(f32),
        lax.psum_scatter(pending[5].astype(bf16), "seq", scatter_dimension=0, tiled=True).astype(f32),
        lax.psum_scatter(pending[6].astype(bf16), "seq", scatter_dimension=1, tiled=True).astype(f32),
    )
    small = lax.psum((gain_one, gain_two, taps_grad), "seq")
    return (
        jnp.stack(outputs),
        jnp.stack(input_grads),
        small[0],
        sharded[0],
        sharded[1],
        sharded[2],
        small[2],
        sharded[3],
        small[1],
        sharded[4],
        sharded[5],
        sharded[6],
    )


def solution(mesh):
    placed = (
        P(None, "seq", None),
        P(),
        P(None, "tp"),
        P(None, "tp"),
        P(None, "tp"),
        P(None, "tp"),
        P("tp", None),
        P(),
        P(None, "tp"),
        P(None, "tp"),
        P("tp", None),
        P(None, "seq", None),
        P(),
        P(),
        P(None, "seq"),
    )
    return jax.shard_map(
        body,
        mesh=mesh,
        in_specs=placed,
        out_specs=(
            P(None, "seq", None),
            P(None, "seq", None),
            P(),
            P("seq", "tp"),
            P("seq", "tp"),
            P("seq", "tp"),
            P(None, "tp"),
            P("tp", "seq"),
            P(),
            P("seq", "tp"),
            P("seq", "tp"),
            P("tp", "seq"),
        ),
        check_vma=False,
    )
```

```python
import functools
import jax
import jax.numpy as jnp
from jax import lax
from jax.experimental import pallas as pl
from jax.experimental.pallas import tpu as pltpu
from jax.sharding import PartitionSpec as P

SPAN = 128
MICRO = 2
EPSILON = 1e-05
MESH = pl.DeviceIdType.MESH
TILE = 256
f32 = jnp.float32
bf16 = jnp.bfloat16


def dot_nn(a, b):
    return jnp.dot(a, b, preferred_element_type=f32)


def dot_nt(a, b):
    return lax.dot_general(a, b, (((1,), (1,)), ((), ())), preferred_element_type=f32)


def dot_tn(a, b):
    return lax.dot_general(a, b, (((0,), (0,)), ((), ())), preferred_element_type=f32)


def send_to(src, dst, send_sem, recv_sem, device):
    return pltpu.make_async_remote_copy(
        src_ref=src,
        dst_ref=dst,
        send_sem=send_sem,
        recv_sem=recv_sem,
        device_id=device,
        device_id_type=MESH,
    )


class Scatter:
    def __init__(self, n_tiles, line, rows, ffn_tiles, refs):
        self.n = n_tiles
        self.line = line
        self.rows = rows
        self.ffn_tiles = ffn_tiles
        (
            self.sbuf,
            self.obuf,
            self.out,
            self.stage,
            self.yrecv,
            self.zup,
            self.zdn,
            self.fetch,
            self.final,
            self.stage_sem,
            self.ysend_sem,
            self.yrecv_sem,
            self.zsend_sem,
            self.zup_sem,
            self.zdn_sem,
            self.fetch_sem,
            self.final_sem,
        ) = refs
        self.slots = self.zup.shape[0]
        s = lax.axis_index("seq")
        self.t = lax.axis_index("tp")
        self.a = lax.div(s, 2)
        self.b = lax.rem(s, 2)
        self.pair = (self.a * 2 + 1 - self.b, self.t)
        self.up = (lax.rem(self.a + 1, line) * 2 + self.b, self.t)
        self.down = (lax.rem(self.a + line - 1, line) * 2 + self.b, self.t)

    @staticmethod
    def scratch(n_tiles, line, rows):
        slots = min(n_tiles, line + 2)
        return [
            pltpu.VMEM((2, 2, line, rows, TILE), bf16),
            pltpu.VMEM((n_tiles, line, rows, TILE), bf16),
            pltpu.VMEM((slots, line, rows, TILE), bf16),
            pltpu.VMEM((slots, line, rows, TILE), bf16),
            pltpu.VMEM((3, line, rows, TILE), bf16),
            pltpu.VMEM((2, rows, TILE), f32),
            pltpu.SemaphoreType.DMA((2, 2)),
            pltpu.SemaphoreType.DMA((n_tiles,)),
            pltpu.SemaphoreType.DMA((n_tiles,)),
            pltpu.SemaphoreType.DMA((3, line)),
            pltpu.SemaphoreType.DMA((slots, line)),
            pltpu.SemaphoreType.DMA((slots, line)),
            pltpu.SemaphoreType.DMA((3, line)),
            pltpu.SemaphoreType.DMA((2,)),
        ]

    def local(self, k):
        slot = lax.rem(k, 2)
        return (
            pltpu.make_async_copy(
                self.stage.at[slot, 1 - self.b], self.sbuf.at[k], self.stage_sem.at[slot, 0]
            ),
            pltpu.make_async_copy(
                self.stage.at[slot, self.b], self.obuf.at[k], self.stage_sem.at[slot, 1]
            ),
        )

    def swap(self, k):
        return send_to(
            self.sbuf.at[k], self.yrecv.at[k], self.ysend_sem.at[k], self.yrecv_sem.at[k], self.pair
        )

    def flush(self, k):
        for copy in self.local(k):
            copy.wait()
        self.swap(k).start()

    def produce(self, k, parts):
        @pl.when(k >= 1)
        def _():
            self.flush(k - 1)

        slot = lax.rem(k, 2)
        for offset, value in parts:
            width = value.shape[1]
            for c in range(self.line):
                for half in range(2):
                    row = (2 * c + half) * self.rows
                    self.stage[slot, half, c, :, offset : offset + width] = value[
                        row : row + self.rows
                    ].astype(bf16)
        for copy in self.local(k):
            copy.start()

    def lag(self, c):
        return jnp.where(
            c > self.a, self.a, jnp.where(c < self.a, self.line - 1 - self.a, self.line - 1)
        )

    def fetching(self, i, c):
        slot = lax.rem(i, 3)
        k = jnp.clip(i - self.lag(c), 0, self.n - 1)
        return pltpu.make_async_copy(
            self.obuf.at[k, c], self.fetch.at[slot, c], self.fetch_sem.at[slot, c]
        )

    def onward(self, i, c, upward):
        slot = lax.rem(i, 3)
        k = jnp.clip(i - self.lag(c), 0, self.n - 1)
        zslot = lax.rem(k, self.slots)
        inbox, sem, device = (
            (self.zup, self.zup_sem, self.up) if upward else (self.zdn, self.zdn_sem, self.down)
        )
        return send_to(
            self.fetch.at[slot, c],
            inbox.at[zslot, c],
            self.zsend_sem.at[slot, c],
            sem.at[zslot, c],
            device,
        )

    def valid(self, i, c):
        k = i - self.lag(c)
        return jnp.logical_and(k >= 0, k < self.n)

    def prefetch(self, i):
        @pl.loop(0, self.line)
        def _(c):
            @pl.when(self.valid(i, c))
            def _():
                self.fetching(i, c).start()

    def drain(self, i):
        @pl.loop(0, self.line)
        def _(c):
            @pl.when(jnp.logical_and(self.valid(i, c), c != self.a))
            def _():
                self.onward(i, c, True).wait_send()

    def storing(self, k):
        slot = lax.rem(k, 2)
        ffn = k < self.ffn_tiles
        kind = jnp.where(ffn, lax.rem(k, 3), 3)
        column = jnp.where(ffn, lax.div(k, 3), k - self.ffn_tiles)
        return pltpu.make_async_copy(
            self.final.at[slot],
            self.out.at[kind, :, pl.ds(pl.multiple_of(column * TILE, TILE), TILE)],
            self.final_sem.at[slot],
        )

    def advance(self, i):
        line, a = self.line, self.a

        @pl.when(i >= 2)
        def _():
            self.drain(i - 2)

        self.prefetch(i + 1)
        first = i - jnp.minimum(a, line - 1 - a)

        @pl.when(jnp.logical_and(first >= 0, first < self.n))
        def _():
            self.swap(first).wait_recv()

        slot = lax.rem(i, 3)

        @pl.loop(0, line)
        def _(c):
            @pl.when(self.valid(i, c))
            def _():
                k = i - self.lag(c)
                zslot = lax.rem(k, self.slots)
                below = jnp.logical_and(c >= a, a > 0)
                above = jnp.logical_and(c <= a, a < line - 1)
                self.fetching(i, c).wait()

                @pl.when(below)
                def _():
                    send_to(
                        self.fetch.at[slot, c],
                        self.zup.at[zslot, c],
                        self.zsend_sem.at[slot, c],
                        self.zup_sem.at[zslot, c],
                        self.down,
                    ).wait_recv()

                @pl.when(above)
                def _():
                    send_to(
                        self.fetch.at[slot, c],
                        self.zdn.at[zslot, c],
                        self.zsend_sem.at[slot, c],
                        self.zdn_sem.at[zslot, c],
                        self.up,
                    ).wait_recv()

                def base():
                    return self.fetch[slot, c].astype(f32) + self.yrecv[k, c].astype(f32)

                @pl.when(c != a)
                def _():
                    @pl.when(jnp.logical_and(c > a, a > 0))
                    def _():
                        self.fetch[slot, c] = (base() + self.zup[zslot, c].astype(f32)).astype(bf16)

                    @pl.when(jnp.logical_and(c < a, a < line - 1))
                    def _():
                        self.fetch[slot, c] = (base() + self.zdn[zslot, c].astype(f32)).astype(bf16)

                    @pl.when(
                        jnp.logical_or(
                            jnp.logical_and(c > a, a == 0),
                            jnp.logical_and(c < a, a == line - 1),
                        )
                    )
                    def _():
                        self.fetch[slot, c] = base().astype(bf16)

                    @pl.when(c > a)
                    def _():
                        self.onward(i, c, True).start()

                    @pl.when(c < a)
                    def _():
                        self.onward(i, c, False).start()

                @pl.when(c == a)
                def _():
                    fslot = lax.rem(k, 2)

                    @pl.when(k >= 2)
                    def _():
                        self.storing(k - 2).wait()

                    @pl.when(jnp.logical_and(a > 0, a < line - 1))
                    def _():
                        self.final[fslot] = (
                            base() + self.zup[zslot, c].astype(f32) + self.zdn[zslot, c].astype(f32)
                        )

                    @pl.when(a == 0)
                    def _():
                        self.final[fslot] = base() + self.zdn[zslot, c].astype(f32)

                    @pl.when(a == line - 1)
                    def _():
                        self.final[fslot] = base() + self.zup[zslot, c].astype(f32)

                    self.storing(k).start()

    def finish(self):
        steps = self.n + self.line - 1
        self.drain(steps - 2)
        self.drain(steps - 1)
        self.storing(self.n - 2).wait()
        self.storing(self.n - 1).wait()

        @pl.loop(0, self.n)
        def _(k):
            self.swap(k).wait_send()


def ffn_kernel(
    line,
    rows,
    n_ffn,
    n2,
    g,
    wg,
    wu,
    wd,
    wg_rest,
    wu_rest,
    o_out,
    d_out,
    grads,
    sbuf,
    obuf,
    oacc,
    dacc,
    wgb,
    wub,
    wdb,
    gs,
    us,
    ds,
    hb,
    dgb,
    dub,
    wsem,
    *rs_refs,
):
    units = wd.shape[0]
    full = units // TILE
    rest = units - full * TILE
    rs = Scatter(3 * n_ffn, line, rows, 3 * n_ffn, (sbuf, obuf, grads) + rs_refs)

    barrier = pltpu.get_barrier_semaphore()
    for device in (rs.pair, rs.up, rs.down):
        pl.semaphore_signal(barrier, inc=1, device_id=device, device_id_type=MESH)

    def weights(j, slot):
        cols = pl.ds(pl.multiple_of(j * TILE, TILE), TILE)
        return (
            pltpu.make_async_copy(wg.at[:, cols], wgb.at[slot], wsem.at[slot, 0]),
            pltpu.make_async_copy(wu.at[:, cols], wub.at[slot], wsem.at[slot, 1]),
            pltpu.make_async_copy(wd.at[cols, :], wdb.at[slot], wsem.at[slot, 2]),
        )

    def rest_weights(slot):
        return (
            pltpu.make_async_copy(wg_rest, wgb.at[slot], wsem.at[slot, 0]),
            pltpu.make_async_copy(wu_rest, wub.at[slot], wsem.at[slot, 1]),
            pltpu.make_async_copy(
                wd.at[full * TILE :, :], wdb.at[slot, 0:rest, :], wsem.at[slot, 2]
            ),
        )

    for copy in weights(0, 0):
        copy.start()
    oacc[...] = jnp.zeros_like(oacc)
    dacc[...] = jnp.zeros_like(dacc)
    pl.semaphore_wait(barrier, 3)

    @pl.loop(0, n_ffn)
    def _(j):
        slot = lax.rem(j, 2)

        @pl.when(j < full)
        def _():
            for copy in weights(j, slot):
                copy.wait()

        if rest:

            @pl.when(j == full)
            def _():
                for copy in rest_weights(full % 2):
                    copy.wait()

        @pl.when(j + 1 < full)
        def _():
            for copy in weights(j + 1, 1 - slot):
                copy.start()

        if rest:

            @pl.when(j + 1 == full)
            def _():
                wdb[full % 2, rest:, :] = jnp.zeros((TILE - rest, wdb.shape[2]), bf16)
                for copy in rest_weights(full % 2):
                    copy.start()

        gs[...] = dot_nn(n2[...], wgb[slot])
        us[...] = dot_nn(n2[...], wub[slot])
        ds[...] = dot_nt(g[...], wdb[slot])

        @pl.loop(0, gs.shape[0] // 64)
        def _(r):
            at = pl.ds(pl.multiple_of(r * 64, 64), 64)
            gate, up, back = gs[at, :], us[at, :], ds[at, :]
            sigma = jax.nn.sigmoid(gate)
            silu = gate * sigma
            hb[at, :] = (silu * up).astype(bf16)
            dgb[at, :] = (back * up * sigma * (1.0 + gate * (1.0 - sigma))).astype(bf16)
            dub[at, :] = (back * silu).astype(bf16)

        rs.produce(3 * j, [(0, dot_tn(g[...], hb[...]))])
        rs.produce(3 * j + 1, [(0, dot_tn(n2[...], dgb[...]))])
        rs.produce(3 * j + 2, [(0, dot_tn(n2[...], dub[...]))])
        oacc[...] += dot_nn(hb[...], wdb[slot])
        dacc[...] += dot_nt(dgb[...], wgb[slot])
        dacc[...] += dot_nt(dub[...], wub[slot])

    rs.flush(rs.n - 1)
    o_out[...] = oacc[...].astype(bf16)
    d_out[...] = dacc[...].astype(bf16)
    rs.prefetch(0)

    @pl.loop(0, rs.n + line - 1)
    def _(i):
        rs.advance(i)

    rs.finish()


def ffn(n2, g, w_gate, w_up, w_down, seq_count):
    tokens, width = n2.shape
    units = w_gate.shape[1]
    n_ffn = pl.cdiv(units, TILE)
    full = units // TILE
    line = seq_count // 2
    rows = width // seq_count
    n_tiles = 3 * n_ffn

    def tail(w):
        return jnp.pad(w[:, full * TILE :], ((0, 0), (0, n_ffn * TILE - units)))

    vmem = pl.BlockSpec(memory_space=pltpu.VMEM)
    hbm = pl.BlockSpec(memory_space=pl.ANY)
    return pl.pallas_call(
        functools.partial(ffn_kernel, line, rows, n_ffn),
        out_shape=(
            jax.ShapeDtypeStruct((tokens, width), bf16),
            jax.ShapeDtypeStruct((tokens, width), bf16),
            jax.ShapeDtypeStruct((4, rows, n_ffn * TILE), f32),
            jax.ShapeDtypeStruct((n_tiles, line, rows, TILE), bf16),
            jax.ShapeDtypeStruct((n_tiles, line, rows, TILE), bf16),
        ),
        in_specs=[vmem, vmem, hbm, hbm, hbm, hbm, hbm],
        out_specs=(vmem, vmem, hbm, hbm, hbm),
        scratch_shapes=[
            pltpu.VMEM((tokens, width), f32),
            pltpu.VMEM((tokens, width), f32),
            pltpu.VMEM((2, width, TILE), bf16),
            pltpu.VMEM((2, width, TILE), bf16),
            pltpu.VMEM((2, TILE, width), bf16),
            pltpu.VMEM((tokens, TILE), f32),
            pltpu.VMEM((tokens, TILE), f32),
            pltpu.VMEM((tokens, TILE), f32),
            pltpu.VMEM((tokens, TILE), bf16),
            pltpu.VMEM((tokens, TILE), bf16),
            pltpu.VMEM((tokens, TILE), bf16),
            pltpu.SemaphoreType.DMA((2, 3)),
        ]
        + Scatter.scratch(n_tiles, line, rows),
        compiler_params=pltpu.CompilerParams(
            collective_id=0, has_side_effects=True, vmem_limit_bytes=60 * 2**20
        ),
    )(n2, g, w_gate, w_up, w_down, tail(w_gate), tail(w_up))[:3]


def passed_along(block, axis, distance):
    devices = range(lax.axis_size(axis))
    route = [((i - distance) % len(devices), i) for i in devices]
    return lax.ppermute(block, axis, route)


def body(
    tokens,
    mix_gain,
    proj_b,
    proj_c,
    proj_x,
    conv_taps,
    proj_out,
    ffn_gain,
    w_gate,
    w_up,
    w_down,
    cotangent,
    seq_lengths,
    span_order,
    keep_mask,
):
    seq_count = lax.axis_size("seq")
    device = lax.axis_index("seq")
    tok_local = tokens.shape[1]
    per_device = tok_local // SPAN
    chan_local = proj_b.shape[1]
    taps = conv_taps.astype(f32)
    gain_one = jnp.zeros(mix_gain.shape, f32)
    gain_two = jnp.zeros(ffn_gain.shape, f32)
    taps_grad = jnp.zeros(taps.shape, f32)
    pending = None
    sharded = None
    outputs = []
    saved = []
    input_grads = []
    for batch_idx in range(MICRO):
        order = span_order[batch_idx]
        mine = lax.dynamic_slice_in_dim(order, device * per_device, per_device)
        lengths = seq_lengths[batch_idx]
        starts = jnp.cumsum(lengths) - lengths
        position = mine[:, None] * SPAN + jnp.arange(SPAN, dtype=jnp.int32)[None, :]
        doc_start = jnp.max(
            jnp.where(starts[None, None, :] <= position[:, :, None], starts[None, None, :], 0),
            axis=2,
        )
        offset = position - doc_start
        valid_far = (offset >= 2).astype(f32)[:, :, None]
        valid_near = (offset >= 1).astype(f32)[:, :, None]
        inputs = tokens[batch_idx].astype(f32)
        scale_one = lax.rsqrt(jnp.mean(inputs * inputs, axis=-1, keepdims=True) + EPSILON)
        normal_one = inputs * scale_one
        normed = (normal_one * mix_gain).astype(bf16)
        gate_b = jnp.dot(normed, proj_b, preferred_element_type=f32)
        gate_c = jnp.dot(normed, proj_c, preferred_element_type=f32)
        values = jnp.dot(normed, proj_x, preferred_element_type=f32)
        product = (gate_b * values).astype(bf16).reshape(per_device, SPAN, chan_local)
        tails = product[:, SPAN - 2 :, :]
        before = passed_along(tails, "seq", 1)
        left_order = lax.dynamic_slice_in_dim(
            order, jnp.mod(device - 1, seq_count) * per_device, per_device
        )
        select = (left_order[None, :] == (mine - 1)[:, None]).astype(bf16)
        prior = jnp.einsum("ak,kjc->ajc", select, before, preferred_element_type=f32).astype(bf16)
        extended = jnp.concatenate([prior, product], axis=1).astype(f32)
        far_term = extended[:, :-2] * valid_far
        near_term = extended[:, 1:-1] * valid_near
        here_term = extended[:, 2:]
        convolved = (taps[0] * far_term + taps[1] * near_term + taps[2] * here_term).reshape(
            tok_local, chan_local
        )
        mixed = (gate_c * convolved).astype(bf16)
        branch_terms = jnp.dot(mixed, proj_out, preferred_element_type=f32)
        middle = inputs + lax.psum(branch_terms.astype(bf16), "tp").astype(f32)
        scale_two = lax.rsqrt(jnp.mean(middle * middle, axis=-1, keepdims=True) + EPSILON)
        normal_two = middle * scale_two
        second_rows = (normal_two * ffn_gain).astype(bf16)
        grad_out = cotangent[batch_idx] * keep_mask[batch_idx].astype(bf16)[:, None]
        saved.append(
            (
                inputs, scale_one, normal_one, normed, gate_b, gate_c, values, valid_far, valid_near,
                far_term, near_term, here_term, convolved, mixed, middle, scale_two, normal_two,
                second_rows, grad_out, order, mine,
            )
        )
    second_all = jnp.concatenate([one[17] for one in saved])
    grad_all = jnp.concatenate([one[18] for one in saved])
    feed_all, partial_all, ffn_grads = ffn(second_all, grad_all, w_gate, w_up, w_down, seq_count)
    feed_all = lax.psum(feed_all, "tp").astype(f32)
    partial_all = lax.psum(partial_all, "tp").astype(f32)
    units = w_gate.shape[1]
    for batch_idx in range(MICRO):
        (
            inputs, scale_one, normal_one, normed, gate_b, gate_c, values, valid_far, valid_near,
            far_term, near_term, here_term, convolved, mixed, middle, scale_two, normal_two,
            second_rows, grad_out, order, mine,
        ) = saved[batch_idx]
        part = slice(batch_idx * tok_local, (batch_idx + 1) * tok_local)
        outputs.append((middle + feed_all[part]).astype(bf16))
        grad_second = partial_all[part]
        out_rows = grad_out.astype(f32)
        gain_two = gain_two + jnp.sum(grad_second * normal_two, axis=0)
        weighted_two = grad_second * ffn_gain
        grad_middle = out_rows + scale_two * (
            weighted_two - normal_two * jnp.mean(weighted_two * normal_two, axis=-1, keepdims=True)
        )
        branch_rows = grad_middle.astype(bf16)
        grad_wout = jnp.einsum("tc,td->cd", mixed, branch_rows, preferred_element_type=f32)
        grad_mixed = jnp.einsum("td,cd->tc", branch_rows, proj_out, preferred_element_type=f32)
        grad_c = (grad_mixed * convolved).astype(bf16)
        grad_conv = (grad_mixed * gate_c).reshape(per_device, SPAN, chan_local)
        taps_grad = taps_grad + jnp.stack(
            [
                jnp.sum(grad_conv * far_term, axis=(0, 1)),
                jnp.sum(grad_conv * near_term, axis=(0, 1)),
                jnp.sum(grad_conv * here_term, axis=(0, 1)),
            ]
        )
        grad_ext = (
            jnp.pad(taps[0] * valid_far * grad_conv, ((0, 0), (0, 2), (0, 0)))
            + jnp.pad(taps[1] * valid_near * grad_conv, ((0, 0), (1, 1), (0, 0)))
            + jnp.pad(taps[2] * grad_conv, ((0, 0), (2, 0), (0, 0)))
        )
        outgoing = grad_ext[:, :2, :]
        arrived = passed_along(outgoing, "seq", -1)
        right_order = lax.dynamic_slice_in_dim(
            order, jnp.mod(device + 1, seq_count) * per_device, per_device
        )
        route = (right_order[None, :] == (mine + 1)[:, None]).astype(f32)
        incoming = jnp.einsum(
            "ak,kjc->ajc",
            route,
            arrived,
            precision=lax.Precision.HIGHEST,
            preferred_element_type=f32,
        )
        grad_product = (
            grad_ext[:, 2:, :] + jnp.pad(incoming, ((0, 0), (SPAN - 2, 0), (0, 0)))
        ).reshape(tok_local, chan_local)
        grad_b = (grad_product * values).astype(bf16)
        grad_x = (grad_product * gate_b).astype(bf16)
        grad_wb = jnp.einsum("td,tc->dc", normed, grad_b, preferred_element_type=f32)
        grad_wc = jnp.einsum("td,tc->dc", normed, grad_c, preferred_element_type=f32)
        grad_wx = jnp.einsum("td,tc->dc", normed, grad_x, preferred_element_type=f32)
        partial_first = (
            jnp.einsum("tc,dc->td", grad_b, proj_b, preferred_element_type=f32)
            + jnp.einsum("tc,dc->td", grad_c, proj_c, preferred_element_type=f32)
            + jnp.einsum("tc,dc->td", grad_x, proj_x, preferred_element_type=f32)
        )
        grad_first = lax.psum(partial_first.astype(bf16), "tp").astype(f32)
        gain_one = gain_one + jnp.sum(grad_first * normal_one, axis=0)
        weighted_one = grad_first * mix_gain
        grad_input = grad_middle + scale_one * (
            weighted_one - normal_one * jnp.mean(weighted_one * normal_one, axis=-1, keepdims=True)
        )
        input_rows = grad_input.astype(bf16)
        input_grads.append(input_rows)
        local_grads = (grad_wb, grad_wc, grad_wx, grad_wout)
        pending = (
            local_grads
            if pending is None
            else jax.tree.map(lambda left, right: left + right, pending, local_grads)
        )
    sharded = (
        lax.psum_scatter(pending[0].astype(bf16), "seq", scatter_dimension=0, tiled=True).astype(f32),
        lax.psum_scatter(pending[1].astype(bf16), "seq", scatter_dimension=0, tiled=True).astype(f32),
        lax.psum_scatter(pending[2].astype(bf16), "seq", scatter_dimension=0, tiled=True).astype(f32),
        lax.psum_scatter(pending[3].astype(bf16), "seq", scatter_dimension=1, tiled=True).astype(f32),
    )
    small = lax.psum((gain_one, gain_two, taps_grad), "seq")
    return (
        jnp.stack(outputs),
        jnp.stack(input_grads),
        small[0],
        sharded[0],
        sharded[1],
        sharded[2],
        small[2],
        sharded[3],
        small[1],
        ffn_grads[1, :, :units],
        ffn_grads[2, :, :units],
        ffn_grads[0, :, :units].T,
    )


def solution(mesh):
    placed = (
        P(None, "seq", None),
        P(),
        P(None, "tp"),
        P(None, "tp"),
        P(None, "tp"),
        P(None, "tp"),
        P("tp", None),
        P(),
        P(None, "tp"),
        P(None, "tp"),
        P("tp", None),
        P(None, "seq", None),
        P(),
        P(),
        P(None, "seq"),
    )
    return jax.shard_map(
        body,
        mesh=mesh,
        in_specs=placed,
        out_specs=(
            P(None, "seq", None),
            P(None, "seq", None),
            P(),
            P("seq", "tp"),
            P("seq", "tp"),
            P("seq", "tp"),
            P(None, "tp"),
            P("tp", "seq"),
            P(),
            P("seq", "tp"),
            P("seq", "tp"),
            P("tp", "seq"),
        ),
        check_vma=False,
    )
```

```python
import functools
import jax
import jax.numpy as jnp
from jax import lax
from jax.experimental import pallas as pl
from jax.experimental.pallas import tpu as pltpu
from jax.sharding import PartitionSpec as P

SPAN = 128
MICRO = 2
EPSILON = 1e-05
MESH = pl.DeviceIdType.MESH
TILE = 256
BLOCK = 32
f32 = jnp.float32
bf16 = jnp.bfloat16


def dot_nn(a, b):
    return jnp.dot(a, b, preferred_element_type=f32)


def dot_nt(a, b):
    return lax.dot_general(a, b, (((1,), (1,)), ((), ())), preferred_element_type=f32)


def dot_tn(a, b):
    return lax.dot_general(a, b, (((0,), (0,)), ((), ())), preferred_element_type=f32)


def send_to(src, dst, send_sem, recv_sem, device):
    return pltpu.make_async_remote_copy(
        src_ref=src,
        dst_ref=dst,
        send_sem=send_sem,
        recv_sem=recv_sem,
        device_id=device,
        device_id_type=MESH,
    )


def rows_at(start, size):
    return pl.ds(pl.multiple_of(start, 16), size)


class Place:
    def __init__(self, line):
        self.line = line
        self.s = lax.axis_index("seq")
        self.t = lax.axis_index("tp")
        self.a = lax.div(self.s, 2)
        self.b = lax.rem(self.s, 2)
        self.h = lax.rem(self.t, 2)
        count = 2 * line
        self.pair = (self.a * 2 + 1 - self.b, self.t)
        self.up = (lax.rem(self.a + 1, line) * 2 + self.b, self.t)
        self.down = (lax.rem(self.a + line - 1, line) * 2 + self.b, self.t)
        self.after = lax.rem(self.s + 1, count)
        self.before = lax.rem(self.s + count - 1, count)
        self.next = (self.after, self.t)
        self.last = (self.before, self.t)
        self.core = (self.s, self.t + 1 - 2 * self.h)
        self.across = (self.s, lax.rem(self.t + 2, 4))


class Scatter:
    NAMES = (
        "stage", "zin", "fetch", "yfetch", "final", "stage_sem", "ysend_sem", "yrecv_sem", "zsend_sem", "zin_sem",
        "fetch_sem", "yfetch_sem", "final_sem",
    )

    def __init__(self, place, n_tiles, ffn_tiles, rows, sbuf, obuf, ybuf, out, scratch):
        self.place, self.a, self.b, self.line = place, place.a, place.b, place.line
        self.n, self.ffn_tiles, self.rows = n_tiles, ffn_tiles, rows
        self.sbuf, self.obuf, self.ybuf, self.out = sbuf, obuf, ybuf, out
        for name, ref in zip(self.NAMES, scratch):
            setattr(self, name, ref)
        self.slots = self.zin.shape[0]

    @staticmethod
    def scratch(n_tiles, line, rows):
        slots = min(n_tiles, line + 1)
        dma = pltpu.SemaphoreType.DMA
        return [
            pltpu.VMEM((2, 2, line, rows, TILE), bf16),
            pltpu.VMEM((slots, line + 1, rows, TILE), bf16),
            pltpu.VMEM((2, line, rows, TILE), bf16),
            pltpu.VMEM((2, line, rows, TILE), bf16),
            pltpu.VMEM((2, rows, TILE), f32),
            dma((2, 2)),
            dma((n_tiles,)),
            dma((n_tiles,)),
            dma((2, line)),
            dma((slots, line + 1)),
            dma((2, line)),
            dma((2, line)),
            dma((2,)),
        ]

    def local(self, k):
        slot = lax.rem(k, 2)
        return (
            pltpu.make_async_copy(self.stage.at[slot, 1 - self.b], self.sbuf.at[k], self.stage_sem.at[slot, 0]),
            pltpu.make_async_copy(self.stage.at[slot, self.b], self.obuf.at[k], self.stage_sem.at[slot, 1]),
        )

    def swap(self, k):
        return send_to(
            self.sbuf.at[k], self.ybuf.at[k], self.ysend_sem.at[k], self.yrecv_sem.at[k], self.place.pair
        )

    def flush(self, k):
        for copy in self.local(k):
            copy.wait()
        self.swap(k).start()

    def produce(self, k, parts):
        @pl.when(jnp.logical_and(k != 0, k != self.ffn_tiles))
        def _():
            self.flush(k - 1)

        slot = lax.rem(k, 2)
        for offset, value in parts:
            width = value.shape[1]
            for c in range(self.line):
                for half in range(2):
                    row = (2 * c + half) * self.rows
                    self.stage[slot, half, c, :, offset : offset + width] = value[row : row + self.rows].astype(bf16)
        for copy in self.local(k):
            copy.start()

    def tile_of(self, i, c):
        lag = jnp.where(c > self.a, self.a, jnp.where(c < self.a, self.line - 1 - self.a, jnp.maximum(self.a, self.line - 1 - self.a)))
        return i - lag

    def valid(self, i, c):
        k = self.tile_of(i, c)
        return jnp.logical_and(k >= 0, k < self.n)

    def fetching(self, i, c):
        slot = lax.rem(i, 2)
        k = jnp.clip(self.tile_of(i, c), 0, self.n - 1)
        return (
            pltpu.make_async_copy(self.obuf.at[k, c], self.fetch.at[slot, c], self.fetch_sem.at[slot, c]),
            pltpu.make_async_copy(self.ybuf.at[k, c], self.yfetch.at[slot, c], self.yfetch_sem.at[slot, c]),
        )

    def onward(self, i, c, upward):
        slot = lax.rem(i, 2)
        k = jnp.clip(self.tile_of(i, c), 0, self.n - 1)
        at = lax.rem(k, self.slots)
        place = c + 1 if upward else c
        return send_to(
            self.fetch.at[slot, c],
            self.zin.at[at, place],
            self.zsend_sem.at[slot, c],
            self.zin_sem.at[at, place],
            self.place.up if upward else self.place.down,
        )

    def drain(self, i):
        @pl.loop(0, self.line)
        def _(c):
            @pl.when(jnp.logical_and(self.valid(i, c), c != self.a))
            def _():
                self.onward(i, c, False).wait_send()

    def storing(self, k):
        slot = lax.rem(k, 2)
        is_ffn = k < self.ffn_tiles
        kind = jnp.where(is_ffn, lax.rem(k, 3), 3)
        column = jnp.where(is_ffn, lax.div(k, 3), k - self.ffn_tiles)
        return pltpu.make_async_copy(
            self.final.at[slot],
            self.out.at[kind, :, pl.ds(pl.multiple_of(column * TILE, TILE), TILE)],
            self.final_sem.at[slot],
        )

    def advance(self, i):
        line, a = self.line, self.a

        @pl.when(i >= 2)
        def _():
            self.drain(i - 2)

        first = i - jnp.minimum(a, line - 1 - a)

        @pl.when(jnp.logical_and(first >= 0, first < self.n))
        def _():
            self.swap(first).wait_recv()

        @pl.loop(0, line)
        def _(c):
            @pl.when(self.valid(i, c))
            def _():
                for copy in self.fetching(i, c):
                    copy.start()

        slot = lax.rem(i, 2)

        @pl.loop(0, line)
        def _(c):
            @pl.when(self.valid(i, c))
            def _():
                k = self.tile_of(i, c)
                at = lax.rem(k, self.slots)

                def arrival(where, device):
                    send_to(
                        self.fetch.at[slot, c],
                        self.zin.at[at, where],
                        self.zsend_sem.at[slot, c],
                        self.zin_sem.at[at, where],
                        device,
                    ).wait_recv()

                for copy in self.fetching(i, c):
                    copy.wait()

                @pl.when(jnp.logical_and(c >= a, a > 0))
                def _():
                    arrival(c + 1, self.place.down)

                @pl.when(jnp.logical_and(c <= a, a < line - 1))
                def _():
                    arrival(c, self.place.up)

                def base():
                    return self.fetch[slot, c].astype(f32) + self.yfetch[slot, c].astype(f32)

                @pl.when(c != a)
                def _():
                    @pl.when(jnp.logical_and(c > a, a > 0))
                    def _():
                        self.fetch[slot, c] = (base() + self.zin[at, c + 1].astype(f32)).astype(bf16)

                    @pl.when(jnp.logical_and(c < a, a < line - 1))
                    def _():
                        self.fetch[slot, c] = (base() + self.zin[at, c].astype(f32)).astype(bf16)

                    @pl.when(
                        jnp.logical_or(jnp.logical_and(c > a, a == 0), jnp.logical_and(c < a, a == line - 1))
                    )
                    def _():
                        self.fetch[slot, c] = base().astype(bf16)

                    @pl.when(c > a)
                    def _():
                        self.onward(i, c, True).start()

                    @pl.when(c < a)
                    def _():
                        self.onward(i, c, False).start()

                @pl.when(c == a)
                def _():
                    fslot = lax.rem(k, 2)

                    @pl.when(k >= 2)
                    def _():
                        self.storing(k - 2).wait()

                    @pl.when(jnp.logical_and(a > 0, a < line - 1))
                    def _():
                        self.final[fslot] = base() + self.zin[at, c].astype(f32) + self.zin[at, c + 1].astype(f32)

                    @pl.when(a == 0)
                    def _():
                        self.final[fslot] = base() + self.zin[at, c].astype(f32)

                    @pl.when(a == line - 1)
                    def _():
                        self.final[fslot] = base() + self.zin[at, c + 1].astype(f32)

                    self.storing(k).start()

    def pump(self, low, high):
        @pl.loop(low, high)
        def _(i):
            self.advance(i)

    def finish(self):
        steps = self.n + self.line - 1
        self.drain(steps - 2)
        self.drain(steps - 1)
        self.storing(self.n - 2).wait()
        self.storing(self.n - 1).wait()

        @pl.loop(0, self.n)
        def _(k):
            self.swap(k).wait_send()


class Sum:
    def __init__(self, place, which, term, inbox, across, sems):
        self.place, self.which, self.term, self.inbox, self.across, self.sems = place, which, term, inbox, across, sems
        self.half = inbox.shape[1]

    def own(self, m):
        return rows_at((2 * m + self.place.h) * self.half, self.half)

    def other(self, m):
        return rows_at((2 * m + 1 - self.place.h) * self.half, self.half)

    def first(self, m):
        return send_to(
            self.term.at[self.other(m)], self.inbox.at[m], self.sems.at[self.which, m, 0], self.sems.at[self.which, m, 1],
            self.place.core,
        )

    def second(self, m):
        return send_to(
            self.term.at[self.own(m)], self.across.at[m], self.sems.at[self.which, m, 2], self.sems.at[self.which, m, 3],
            self.place.across,
        )

    def start(self, m):
        self.first(m).start()

    def relay(self, m):
        self.first(m).wait_recv()
        base = (2 * m + self.place.h) * self.half

        @pl.loop(0, self.half // BLOCK)
        def _(r):
            at = rows_at(base + r * BLOCK, BLOCK)
            took = self.inbox[m, rows_at(r * BLOCK, BLOCK), :].astype(f32)
            self.term[at, :] = (self.term[at, :].astype(f32) + took).astype(bf16)

        self.second(m).start()

    def ready(self, m):
        self.second(m).wait_recv()

    def total(self, m, r):
        at = rows_at((2 * m + self.place.h) * self.half + r * BLOCK, BLOCK)
        return self.term[at, :].astype(f32) + self.across[m, rows_at(r * BLOCK, BLOCK), :].astype(f32)

    def settle(self, m):
        self.first(m).wait_send()
        self.second(m).wait_send()

    def spread(self, m, buffer):
        at = self.own(m)
        return send_to(
            buffer.at[at], buffer.at[at], self.sems.at[self.which, m, 4], self.sems.at[self.which, m, 5], self.place.core
        )

    def publish(self, m, staged, out):
        at = rows_at(self.place.h * self.half, self.half)
        return (
            pltpu.make_async_copy(staged.at[m], out.at[m, at], self.sems.at[self.which, m, 6]),
            send_to(
                staged.at[m], out.at[m, at], self.sems.at[self.which, m, 4], self.sems.at[self.which, m, 5],
                self.place.core,
            ),
        )


def normal(values):
    scale = lax.rsqrt(jnp.mean(values * values, axis=-1, keepdims=True) + EPSILON)
    return scale, values * scale


def fold(values):
    return jnp.sum(values.reshape(values.shape[0] // 8, 8, values.shape[1]), axis=0)


def kernel(line, rows, n_ffn, names, *refs):
    v = dict(zip(names, refs))
    (lengths, order, mask, mix_gain, ffn_gain, taps_in) = (
        v[n] for n in ("lengths", "order", "mask", "mix_gain", "ffn_gain", "taps")
    )
    place = Place(line)
    n1, n2, g, term0, term1, r1h = (v[n] for n in ("n1", "n2", "g", "term0", "term1", "r1h"))
    inbox0, inbox1, across0, across1, across2 = (v[n] for n in ("inbox0", "inbox1", "across0", "across1", "across2"))
    pb, pc, px, po = (v[n] for n in ("pb", "pc", "px", "po"))
    bs, cs, xs, bx, ym, cat = (v[n] for n in ("bs", "cs", "xs", "bx", "ym", "cat"))
    sums, load = v["sums"], v["load"]
    tokens, width = n1.shape
    local = tokens // MICRO
    half = local // 2
    spans = local // SPAN
    chan = bs.shape[1]
    units = v["w_down"].shape[0]
    full = units // TILE
    rest = units - full * TILE
    docs = lengths.shape[1]
    rs = Scatter(
        place, 3 * n_ffn + 6, 3 * n_ffn, rows, v["sbuf"], v["obuf"], v["ybuf"], v["grads"],
        [v[n] for n in Scatter.NAMES],
    )
    branch = Sum(place, 0, term0, inbox0, across0, sums)
    second = Sum(place, 1, term1, inbox1, across1, sums)
    feed = Sum(place, 2, term0, inbox0, across2, sums)
    first = Sum(place, 3, term0, inbox1, across0, sums)

    barrier = pltpu.get_barrier_semaphore()
    for device in (place.pair, place.next, place.last, place.core, place.across):
        pl.semaphore_signal(barrier, inc=1, device_id=device, device_id_type=MESH)

    @pl.loop(0, line)
    def _(c):
        @pl.when(c != place.a)
        def _():
            pl.semaphore_signal(barrier, inc=1, device_id=(c * 2 + place.b, place.t), device_id_type=MESH)

    def loading(which, src, dst):
        return pltpu.make_async_copy(src, dst, load.at[which])

    projections = [
        loading(2, v["proj_b"], pb),
        loading(3, v["proj_x"], px),
        loading(4, v["proj_c"], pc),
        loading(5, v["proj_out"], po),
    ]
    cot_load = [loading(6 + m, v["cotangent"].at[m], g.at[m * local : (m + 1) * local]) for m in range(MICRO)]
    wgb, wub, wdb = v["wgb"], v["wub"], v["wdb"]

    def weights(j, slot):
        at = pl.ds(pl.multiple_of(j * TILE, TILE), TILE)
        return [
            pltpu.make_async_copy(v[src].at[at], dst.at[slot], v["wsem"].at[slot, q])
            for q, (src, dst) in enumerate((("w_gate", wgb), ("w_up", wub), ("w_down", wdb)))
        ]

    def rest_weights():
        slot = full % 2
        return [
            pltpu.make_async_copy(v[src].at[full * TILE :], dst.at[slot, 0:rest], v["wsem"].at[slot, q])
            for q, (src, dst) in enumerate((("w_gate", wgb), ("w_up", wub), ("w_down", wdb)))
        ]

    taps = taps_in[...].astype(f32)
    row_ids = lax.broadcasted_iota(jnp.int32, (SPAN, 1), 0)
    tap = [taps[k : k + 1, :] for k in range(3)]

    def span_facts(m, q):
        mine = order[m, place.s * spans + q]
        position = mine * SPAN + row_ids
        near = position >= 0
        far = position >= 0
        begin = jnp.int32(0)
        for n in range(docs):
            near = jnp.logical_and(near, position != begin)
            far = jnp.logical_and(far, position != begin + 1)
            begin = begin + lengths[m, n]
        return mine, near, jnp.logical_and(near, far)

    def terms(m, q, near, far, mine):
        here = bx[pl.ds(m * local + q * SPAN, SPAN), :].astype(f32)
        older = jnp.zeros((1, chan), f32)
        newer = jnp.zeros((1, chan), f32)
        for k in range(spans):
            took = order[m, place.before * spans + k] == mine - 1
            tail = v["halo_in"][m, k].astype(f32)
            older = older + jnp.where(took, tail[14:15], 0.0)
            newer = newer + jnp.where(took, tail[15:16], 0.0)
        far_term = pltpu.roll(here, 2, 0)
        far_term = jnp.where(row_ids == 0, older, jnp.where(row_ids == 1, newer, far_term))
        near_term = jnp.where(row_ids == 0, newer, pltpu.roll(here, 1, 0))
        return jnp.where(far, far_term, 0.0), jnp.where(near, near_term, 0.0), here

    def halo(m):
        return send_to(
            v["halo_out"].at[m], v["halo_in"].at[m], v["hsem"].at[0, m], v["hsem"].at[1, m], place.next
        )

    def halo_back(m):
        return send_to(
            v["back_out"].at[m], v["back_in"].at[m], v["hsem"].at[2, m], v["hsem"].at[3, m], place.last
        )

    def mixer_half(m, x):
        base = m * local

        @pl.loop(0, local // BLOCK)
        def _(r):
            at = rows_at(base + r * BLOCK, BLOCK)
            _, unit = normal(x[at, :].astype(f32))
            n1[at, :] = (unit * mix_gain[...]).astype(bf16)

        at = pl.ds(base, local)
        if m == 0:
            projections[0].wait()
        bs[at, :] = dot_nn(n1[at, :], pb[...])
        if m == 0:
            projections[1].wait()
        xs[at, :] = dot_nn(n1[at, :], px[...])
        for q in range(spans):
            rows_q = pl.ds(base + q * SPAN, SPAN)
            product = (bs[rows_q, :] * xs[rows_q, :]).astype(bf16)
            bx[rows_q, :] = product
            v["halo_out"][m, q] = product[SPAN - 16 :, :]

    def mixer_rest(m):
        base = m * local
        at = pl.ds(base, local)
        if m == 0:
            projections[2].wait()
        cs[at, :] = dot_nn(n1[at, :], pc[...])
        halo(m).wait_recv()
        for q in range(spans):
            rows_q = pl.ds(base + q * SPAN, SPAN)
            mine, near, far = span_facts(m, q)
            far_term, near_term, here = terms(m, q, near, far, mine)
            conv = tap[0] * far_term + tap[1] * near_term + tap[2] * here
            ym[rows_q, :] = (cs[rows_q, :] * conv).astype(bf16)
        if m == 0:
            projections[3].wait()
        term0[at, :] = dot_nn(ym[at, :], po[...]).astype(bf16)
        branch.start(m)

    def middle(m, x):
        branch.ready(m)

        @pl.loop(0, half // BLOCK)
        def _(r):
            at = rows_at(m * local + place.h * half + r * BLOCK, BLOCK)
            value = x[at, :].astype(f32) + branch.total(m, r)
            r1h[rows_at(m * half + r * BLOCK, BLOCK), :] = value
            _, unit = normal(value)
            n2[at, :] = (unit * ffn_gain[...]).astype(bf16)

        branch.spread(m, n2).start()

    def masked(m):
        cot_load[m].wait()
        for q in range(spans):
            kept = mask[m : m + 1, q * SPAN : (q + 1) * SPAN].astype(f32)
            kept = jnp.transpose(jnp.broadcast_to(kept, (SPAN, SPAN)))
            rows_q = pl.ds(m * local + q * SPAN, SPAN)
            for c in range(width // SPAN):
                cols = pl.ds(c * SPAN, SPAN)
                g[rows_q, cols] = (g[rows_q, cols].astype(f32) * kept).astype(bf16)

    def mixer_forward(x):
        x_load = [loading(m, v["tokens"].at[m], x.at[m * local : (m + 1) * local]) for m in range(MICRO)]
        for copy in [x_load[0]] + projections[:2] + [x_load[1]] + projections[2:] + cot_load + weights(0, 0):
            copy.start()
        x_load[0].wait()
        mixer_half(0, x)
        pl.semaphore_wait(barrier, 5 + line - 1)
        halo(0).start()
        x_load[1].wait()
        mixer_rest(0)
        mixer_half(1, x)
        halo(1).start()
        branch.relay(0)
        mixer_rest(1)
        masked(0)
        branch.relay(1)
        masked(1)
        middle(0, x)
        middle(1, x)
        for m in range(MICRO):
            branch.spread(m, n2).wait()
            branch.settle(m)

    pl.run_scoped(mixer_forward, pltpu.VMEM((tokens, width), bf16))

    def feed_forward(oacc, dacc, gs, us, ds, hb, dgb, dub):
        oacc[...] = jnp.zeros_like(oacc)
        dacc[...] = jnp.zeros_like(dacc)

        @pl.loop(0, n_ffn)
        def _(j):
            slot = lax.rem(j, 2)

            @pl.when(j < full)
            def _():
                for copy in weights(jnp.minimum(j, full - 1), slot):
                    copy.wait()

            if rest:

                @pl.when(j == full)
                def _():
                    for copy in rest_weights():
                        copy.wait()

            @pl.when(j + 1 < full)
            def _():
                for copy in weights(jnp.minimum(j + 1, full - 1), 1 - slot):
                    copy.start()

            if rest:

                @pl.when(j + 1 == full)
                def _():
                    for buffer in (wgb, wub, wdb):
                        buffer[full % 2, rest:, :] = jnp.zeros((TILE - rest, width), bf16)
                    for copy in rest_weights():
                        copy.start()

            gs[...] = dot_nt(n2[...], wgb[slot])
            us[...] = dot_nt(n2[...], wub[slot])
            ds[...] = dot_nt(g[...], wdb[slot])

            @pl.loop(0, tokens // 64)
            def _(r):
                at = rows_at(r * 64, 64)
                gate, up, back = gs[at, :], us[at, :], ds[at, :]
                sigma = jax.nn.sigmoid(gate)
                silu = gate * sigma
                hb[at, :] = (silu * up).astype(bf16)
                dgb[at, :] = (back * up * sigma * (1.0 + gate * (1.0 - sigma))).astype(bf16)
                dub[at, :] = (back * silu).astype(bf16)

            rs.produce(3 * j, [(0, dot_tn(g[...], hb[...]))])
            rs.produce(3 * j + 1, [(0, dot_tn(n2[...], dgb[...]))])
            rs.produce(3 * j + 2, [(0, dot_tn(n2[...], dub[...]))])
            oacc[...] += dot_nn(hb[...], wdb[slot])
            dacc[...] += dot_nn(dgb[...], wgb[slot])
            dacc[...] += dot_nn(dub[...], wub[slot])

        rs.flush(3 * n_ffn - 1)
        for m in range(MICRO):
            at = pl.ds(m * local, local)
            term1[at, :] = dacc[at, :].astype(bf16)
            second.start(m)
        for m in range(MICRO):
            at = pl.ds(m * local, local)
            term0[at, :] = oacc[at, :].astype(bf16)
            feed.start(m)

    pl.run_scoped(
        feed_forward,
        pltpu.VMEM((tokens, width), f32),
        pltpu.VMEM((tokens, width), f32),
        pltpu.VMEM((tokens, TILE), f32),
        pltpu.VMEM((tokens, TILE), f32),
        pltpu.VMEM((tokens, TILE), f32),
        pltpu.VMEM((tokens, TILE), bf16),
        pltpu.VMEM((tokens, TILE), bf16),
        pltpu.VMEM((tokens, TILE), bf16),
    )

    def backward(dr1, xh, dym, dbx, gain_one, gain_two, tap_rows):
        x_load = [
            loading(m, v["tokens"].at[m, rows_at(place.h * half, half)], xh.at[m * half : (m + 1) * half])
            for m in range(MICRO)
        ]
        for copy in x_load:
            copy.start()
        for m in range(MICRO):
            second.relay(m)
        for m in range(MICRO):
            feed.relay(m)
        gain_one[...] = jnp.zeros_like(gain_one)
        gain_two[...] = jnp.zeros_like(gain_two)
        rs.pump(0, 4)

        for m in range(MICRO):
            second.ready(m)

            @pl.loop(0, half // BLOCK)
            def _(r):
                at = rows_at(m * local + place.h * half + r * BLOCK, BLOCK)
                here = rows_at(m * half + r * BLOCK, BLOCK)
                grad = second.total(m, r)
                scale, unit = normal(r1h[here, :])
                gain_two[...] += fold(grad * unit)
                weighted = grad * ffn_gain[...]
                inner = jnp.mean(weighted * unit, axis=-1, keepdims=True)
                value = g[at, :].astype(f32) + scale * (weighted - unit * inner)
                dr1[here, :] = value
                n2[at, :] = value.astype(bf16)

            second.spread(m, n2).start()

        rs.pump(4, 8)
        for m in range(MICRO):
            feed.ready(m)

            @pl.loop(0, half // BLOCK)
            def _(r):
                here = rows_at(m * half + r * BLOCK, BLOCK)
                at = rows_at(r * BLOCK, BLOCK)
                across2[m, at, :] = (r1h[here, :] + feed.total(m, r)).astype(bf16)

            for copy in feed.publish(m, across2, v["block_out"]):
                copy.start()

        for m in range(MICRO):
            second.spread(m, n2).wait()
            second.settle(m)
        dym[...] = dot_nt(n2[...], po[...])
        tap_sums = [jnp.zeros((8, chan), f32) for _ in range(3)]
        for m in range(MICRO):
            for q in range(spans):
                rows_q = pl.ds(m * local + q * SPAN, SPAN)
                mine, near, far = span_facts(m, q)
                far_term, near_term, here = terms(m, q, near, far, mine)
                grad = dym[rows_q, :]
                cat[rows_q, chan : 2 * chan] = (
                    grad * (tap[0] * far_term + tap[1] * near_term + tap[2] * here)
                ).astype(bf16)
                grad = grad * cs[rows_q, :]
                for k, other in enumerate((far_term, near_term, here)):
                    tap_sums[k] = tap_sums[k] + fold(grad * other)
                old = jnp.where(far, tap[0] * grad, 0.0)
                mid = jnp.where(near, tap[1] * grad, 0.0)
                dbx[rows_q, :] = (
                    tap[2] * grad
                    + jnp.where(row_ids < SPAN - 1, pltpu.roll(mid, SPAN - 1, 0), 0.0)
                    + jnp.where(row_ids < SPAN - 2, pltpu.roll(old, SPAN - 2, 0), 0.0)
                )
                top_ids = row_ids[:8]
                v["back_out"][m, q] = jnp.where(top_ids < 2, old[:8], 0.0) + jnp.where(
                    top_ids == 1, mid[0:1], 0.0
                )
            halo_back(m).start()
        for k in range(3):
            tap_rows[k] = tap_sums[k]
        for m in range(MICRO):
            halo_back(m).wait_recv()
            for q in range(spans):
                rows_q = pl.ds(m * local + q * SPAN, SPAN)
                mine = order[m, place.s * spans + q]
                from_next = jnp.zeros((8, chan), f32)
                for k in range(spans):
                    took = order[m, place.after * spans + k] == mine + 1
                    from_next = from_next + jnp.where(took, v["back_in"][m, k], 0.0)
                value = dbx[rows_q, :]
                value = (
                    value
                    + jnp.where(row_ids == SPAN - 2, from_next[0:1], 0.0)
                    + jnp.where(row_ids == SPAN - 1, from_next[1:2], 0.0)
                )
                cat[rows_q, 0:chan] = (value * xs[rows_q, :]).astype(bf16)
                cat[rows_q, 2 * chan :] = (value * bs[rows_q, :]).astype(bf16)
        k0 = 3 * n_ffn
        wide = 3 * chan
        whole = wide // TILE
        for k in range(whole):
            rs.produce(k0 + k, [(0, dot_tn(n1[...], cat[:, k * TILE : (k + 1) * TILE]))])
        left = wide - whole * TILE
        rs.produce(
            k0 + whole,
            [
                (0, dot_tn(n1[...], cat[:, whole * TILE :])),
                (left, dot_tn(n2[...], ym[:, 0 : TILE - left])),
            ],
        )
        rs.produce(k0 + whole + 1, [(0, dot_tn(n2[...], ym[:, TILE - left :]))])
        rs.flush(k0 + whole + 1)

        for m in range(MICRO):
            feed.settle(m)
            at = pl.ds(m * local, local)
            term0[at, :] = (
                dot_nt(cat[at, 0:chan], pb[...])
                + dot_nt(cat[at, chan : 2 * chan], pc[...])
                + dot_nt(cat[at, 2 * chan :], px[...])
            ).astype(bf16)
            first.start(m)
        for m in range(MICRO):
            first.relay(m)
        rs.pump(8, 14)
        for m in range(MICRO):
            x_load[m].wait()
            first.ready(m)

            @pl.loop(0, half // BLOCK)
            def _(r):
                here = rows_at(m * half + r * BLOCK, BLOCK)
                at = rows_at(r * BLOCK, BLOCK)
                grad = first.total(m, r)
                scale, unit = normal(xh[here, :].astype(f32))
                gain_one[...] += fold(grad * unit)
                weighted = grad * mix_gain[...]
                inner = jnp.mean(weighted * unit, axis=-1, keepdims=True)
                across0[m, at, :] = (dr1[here, :] + scale * (weighted - unit * inner)).astype(bf16)

            for copy in first.publish(m, across0, v["d_tokens"]):
                copy.start()

        small, gather = v["small"], v["gather"]
        ssem = v["ssem"]
        small[0] = jnp.zeros((8, width), f32)
        small[0, 0:1, :] = jnp.sum(gain_one[...], axis=0, keepdims=True)
        small[0, 1:2, :] = jnp.sum(gain_two[...], axis=0, keepdims=True)
        for k in range(3):
            small[0, 2:3, k * chan : (k + 1) * chan] = jnp.sum(tap_rows[k], axis=0, keepdims=True)
        core = send_to(small.at[0], gather.at[0], ssem.at[0], ssem.at[1], place.core)
        core.start()
        core.wait_recv()
        small[1] = small[0] + jnp.where(lax.broadcasted_iota(jnp.int32, (8, 1), 0) < 2, gather[0], 0.0)
        pair = send_to(small.at[1], gather.at[1], ssem.at[2], ssem.at[3], place.pair)
        pair.start()
        pair.wait_recv()
        small[2] = small[1] + gather[1]

        def along(c, slot):
            return send_to(
                small.at[2], gather.at[2 + slot], ssem.at[4 + c], ssem.at[4 + line + slot], (c * 2 + place.b, place.t)
            )

        @pl.loop(0, line)
        def _(c):
            @pl.when(c != place.a)
            def _():
                along(c, place.a).start()

        gather[2 + place.a] = small[2]

        rs.pump(14, rs.n + line - 1)

        @pl.loop(0, line)
        def _(c):
            @pl.when(c != place.a)
            def _():
                along(c, c).wait_recv()
                along(c, place.a).wait_send()

        total = gather[2]
        for c in range(1, line):
            total = total + gather[2 + c]
        v["small_out"][...] = total
        core.wait_send()
        pair.wait_send()
        for m in range(MICRO):
            halo(m).wait_send()
            halo_back(m).wait_send()
            first.settle(m)
            for each, staged, out in ((feed, across2, v["block_out"]), (first, across0, v["d_tokens"])):
                for copy in each.publish(m, staged, out):
                    copy.wait()
        rs.finish()

    pl.run_scoped(
        backward,
        pltpu.VMEM((tokens // 2, width), f32),
        pltpu.VMEM((tokens // 2, width), bf16),
        pltpu.VMEM((tokens, chan), f32),
        pltpu.VMEM((tokens, chan), f32),
        pltpu.VMEM((8, width), f32),
        pltpu.VMEM((8, width), f32),
        pltpu.VMEM((3, 8, chan), f32),
    )


def body(
    seq_count,
    tokens,
    mix_gain,
    proj_b,
    proj_c,
    proj_x,
    conv_taps,
    proj_out,
    ffn_gain,
    w_gate,
    w_up,
    w_down,
    cotangent,
    seq_lengths,
    span_order,
    keep_mask,
):
    local, width = tokens.shape[1:]
    total = MICRO * local
    half = local // 2
    chan = proj_b.shape[1]
    units = w_gate.shape[1]
    n_ffn = pl.cdiv(units, TILE)
    line = seq_count // 2
    rows = width // seq_count
    n_tiles = 3 * n_ffn + 6
    spans = local // SPAN
    dma = pltpu.SemaphoreType.DMA
    vmem = pl.BlockSpec(memory_space=pltpu.VMEM)
    smem = pl.BlockSpec(memory_space=pltpu.SMEM)
    hbm = pl.BlockSpec(memory_space=pl.ANY)
    shape = jax.ShapeDtypeStruct
    inputs = [
        ("lengths", seq_lengths, smem),
        ("order", span_order, smem),
        ("mask", keep_mask, vmem),
        ("mix_gain", mix_gain.reshape(1, width), vmem),
        ("ffn_gain", ffn_gain.reshape(1, width), vmem),
        ("taps", conv_taps, vmem),
        ("tokens", tokens, hbm),
        ("cotangent", cotangent, hbm),
        ("proj_b", proj_b, hbm),
        ("proj_c", proj_c, hbm),
        ("proj_x", proj_x, hbm),
        ("proj_out", proj_out, hbm),
        ("w_gate", w_gate.T, hbm),
        ("w_up", w_up.T, hbm),
        ("w_down", w_down, hbm),
    ]
    piece = shape((n_tiles, line, rows, TILE), bf16)
    outputs = [
        ("block_out", shape(tokens.shape, bf16), hbm),
        ("d_tokens", shape(tokens.shape, bf16), hbm),
        ("grads", shape((4, rows, n_ffn * TILE), f32), hbm),
        ("small_out", shape((8, width), f32), vmem),
        ("sbuf", piece, hbm),
        ("obuf", piece, hbm),
        ("ybuf", piece, hbm),
    ]
    scratch = [
        ("n1", pltpu.VMEM((total, width), bf16)),
        ("n2", pltpu.VMEM((total, width), bf16)),
        ("g", pltpu.VMEM((total, width), bf16)),
        ("term0", pltpu.VMEM((total, width), bf16)),
        ("term1", pltpu.VMEM((total, width), bf16)),
        ("r1h", pltpu.VMEM((total // 2, width), f32)),
        ("inbox0", pltpu.VMEM((MICRO, half, width), bf16)),
        ("inbox1", pltpu.VMEM((MICRO, half, width), bf16)),
        ("across0", pltpu.VMEM((MICRO, half, width), bf16)),
        ("across1", pltpu.VMEM((MICRO, half, width), bf16)),
        ("across2", pltpu.VMEM((MICRO, half, width), bf16)),
        ("pb", pltpu.VMEM((width, chan), bf16)),
        ("pc", pltpu.VMEM((width, chan), bf16)),
        ("px", pltpu.VMEM((width, chan), bf16)),
        ("po", pltpu.VMEM((chan, width), bf16)),
        ("bs", pltpu.VMEM((total, chan), f32)),
        ("cs", pltpu.VMEM((total, chan), f32)),
        ("xs", pltpu.VMEM((total, chan), f32)),
        ("bx", pltpu.VMEM((total, chan), bf16)),
        ("ym", pltpu.VMEM((total, chan), bf16)),
        ("cat", pltpu.VMEM((total, 3 * chan), bf16)),
        ("wgb", pltpu.VMEM((2, TILE, width), bf16)),
        ("wub", pltpu.VMEM((2, TILE, width), bf16)),
        ("wdb", pltpu.VMEM((2, TILE, width), bf16)),
        ("halo_out", pltpu.VMEM((MICRO, spans, 16, chan), bf16)),
        ("halo_in", pltpu.VMEM((MICRO, spans, 16, chan), bf16)),
        ("back_out", pltpu.VMEM((MICRO, spans, 8, chan), f32)),
        ("back_in", pltpu.VMEM((MICRO, spans, 8, chan), f32)),
        ("small", pltpu.VMEM((3, 8, width), f32)),
        ("gather", pltpu.VMEM((2 + line, 8, width), f32)),
        ("load", dma((8,))),
        ("wsem", dma((2, 3))),
        ("sums", dma((4, MICRO, 7))),
        ("hsem", dma((4, MICRO))),
        ("ssem", dma((4 + 2 * line,))),
    ]
    scratch += list(zip(Scatter.NAMES, Scatter.scratch(n_tiles, line, rows)))
    names = [n for n, _, _ in inputs] + [n for n, _, _ in outputs] + [n for n, _ in scratch]
    results = pl.pallas_call(
        functools.partial(kernel, line, rows, n_ffn, names),
        out_shape=tuple(s for _, s, _ in outputs),
        in_specs=[s for _, _, s in inputs],
        out_specs=tuple(s for _, _, s in outputs),
        scratch_shapes=[s for _, s in scratch],
        compiler_params=pltpu.CompilerParams(
            collective_id=0, has_side_effects=True, vmem_limit_bytes=62 * 2**20 - 2**19
        ),
    )(*[a for _, a, _ in inputs])
    block_out, d_tokens, grads, small = results[:4]
    return (
        block_out,
        d_tokens,
        small[0],
        grads[3, :, 0:chan],
        grads[3, :, chan : 2 * chan],
        grads[3, :, 2 * chan : 3 * chan],
        small[2, : 3 * chan].reshape(3, chan),
        grads[3, :, 3 * chan : 4 * chan].T,
        small[1],
        grads[1, :, :units],
        grads[2, :, :units],
        grads[0, :, :units].T,
    )


def solution(mesh):
    placed = (
        P(None, "seq", None),
        P(),
        P(None, "tp"),
        P(None, "tp"),
        P(None, "tp"),
        P(None, "tp"),
        P("tp", None),
        P(),
        P(None, "tp"),
        P(None, "tp"),
        P("tp", None),
        P(None, "seq", None),
        P(),
        P(),
        P(None, "seq"),
    )
    return jax.shard_map(
        functools.partial(body, mesh.shape["seq"]),
        mesh=mesh,
        in_specs=placed,
        out_specs=(
            P(None, "seq", None),
            P(None, "seq", None),
            P(),
            P("seq", "tp"),
            P("seq", "tp"),
            P("seq", "tp"),
            P(None, "tp"),
            P("tp", "seq"),
            P(),
            P("seq", "tp"),
            P("seq", "tp"),
            P("tp", "seq"),
        ),
        check_vma=False,
    )
```

```python
import functools
import jax
import jax.numpy as jnp
from jax import lax
from jax.experimental import pallas as pl
from jax.experimental.pallas import tpu as pltpu
from jax.sharding import PartitionSpec as P

SPAN = 128
MICRO = 2
EPSILON = 1e-05
MESH = pl.DeviceIdType.MESH
TILE = 256
BLOCK = 32
ROWS = 384
f32 = jnp.float32
bf16 = jnp.bfloat16


def dot_nn(a, b):
    return jnp.dot(a, b, preferred_element_type=f32)


def dot_nt(a, b):
    return lax.dot_general(a, b, (((1,), (1,)), ((), ())), preferred_element_type=f32)


def dot_tn(a, b):
    return lax.dot_general(a, b, (((0,), (0,)), ((), ())), preferred_element_type=f32)


def send_to(src, dst, send_sem, recv_sem, device):
    return pltpu.make_async_remote_copy(
        src_ref=src,
        dst_ref=dst,
        send_sem=send_sem,
        recv_sem=recv_sem,
        device_id=device,
        device_id_type=MESH,
    )


def rows_at(start, size):
    return pl.ds(pl.multiple_of(start, 16), size)


class Place:
    def __init__(self, line):
        self.line = line
        self.s = lax.axis_index("seq")
        self.t = lax.axis_index("tp")
        self.a = lax.div(self.s, 2)
        self.b = lax.rem(self.s, 2)
        self.h = lax.rem(self.t, 2)
        count = 2 * line
        self.pair = (self.a * 2 + 1 - self.b, self.t)
        self.up = (lax.rem(self.a + 1, line) * 2 + self.b, self.t)
        self.down = (lax.rem(self.a + line - 1, line) * 2 + self.b, self.t)
        self.after = lax.rem(self.s + 1, count)
        self.before = lax.rem(self.s + count - 1, count)
        self.next = (self.after, self.t)
        self.last = (self.before, self.t)
        self.core = (self.s, self.t + 1 - 2 * self.h)
        self.across = (self.s, lax.rem(self.t + 2, 4))


class Scatter:
    NAMES = (
        "stage", "zin", "fetch", "yfetch", "acc", "final", "swap_out", "swap_in", "swap_sum",
        "stage_sem", "ysend_sem", "yrecv_sem", "zsend_sem", "zin_sem", "fetch_sem", "yfetch_sem", "final_sem",
        "swap_sem", "sum_sem",
    )
    GROUP = 6

    def __init__(self, place, n_tiles, ffn_tiles, rows, wbuf, ybuf, out, scratch):
        self.place, self.a, self.b, self.line = place, place.a, place.b, place.line
        self.n, self.ffn_tiles, self.rows = n_tiles, ffn_tiles, rows
        self.wbuf, self.ybuf, self.out = wbuf, ybuf, out
        for name, ref in zip(self.NAMES, scratch):
            setattr(self, name, ref)
        self.slots = self.zin.shape[0]
        self.items = self.count(n_tiles)
        self.steps = self.items + self.line - 1
        self.swaps = self.swap_sum.shape[0]

    @classmethod
    def count(cls, n_tiles):
        left = n_tiles % cls.GROUP
        assert left != 1
        return n_tiles // cls.GROUP * (cls.GROUP + 1) + (left + 1 if left else 0)

    @classmethod
    def scratch(cls, n_tiles, line, rows):
        slots = line + 1
        swaps = (n_tiles + cls.GROUP - 2) // cls.GROUP
        dma = pltpu.SemaphoreType.DMA
        return [
            pltpu.VMEM((2, 2, line, rows, TILE), bf16),
            pltpu.VMEM((slots, line + 1, rows, TILE), bf16),
            pltpu.VMEM((2, line, rows, TILE), bf16),
            pltpu.VMEM((2, line, rows, TILE), bf16),
            pltpu.VMEM((rows, TILE), f32),
            pltpu.VMEM((2, rows, TILE), f32),
            pltpu.VMEM((swaps, rows, TILE), bf16),
            pltpu.VMEM((swaps, rows, TILE), bf16),
            pltpu.VMEM((swaps, rows, TILE), f32),
            dma((2, 2)),
            dma((n_tiles,)),
            dma((n_tiles,)),
            dma((2, line)),
            dma((slots, line + 1)),
            dma((2, line)),
            dma((2, line)),
            dma((2,)),
            dma((2, swaps)),
            dma((swaps,)),
        ]


    def local(self, k):
        slot = lax.rem(k, 2)
        return (
            pltpu.make_async_copy(self.stage.at[slot, 1 - self.b], self.wbuf.at[k, 0], self.stage_sem.at[slot, 0]),
            pltpu.make_async_copy(self.stage.at[slot, self.b], self.wbuf.at[k, 1], self.stage_sem.at[slot, 1]),
        )

    def halved(self, k):
        return lax.rem(k, self.GROUP) != 1

    def halve(self, k):
        return send_to(
            self.wbuf.at[k, 0], self.ybuf.at[k], self.ysend_sem.at[k], self.yrecv_sem.at[k], self.place.pair
        )

    def flush(self, k):
        for copy in self.local(k):
            copy.wait()

        @pl.when(self.halved(k))
        def _():
            self.halve(k).start()

    def produce(self, k, parts):
        @pl.when(jnp.logical_and(k != 0, k != self.ffn_tiles))
        def _():
            self.flush(k - 1)

        slot = lax.rem(k, 2)
        for offset, left, right in parts:
            width = right().shape[1]
            for start in range(0, left.shape[1], ROWS):
                value = dot_tn(left[:, start : start + ROWS], right())
                for n in range(ROWS // self.rows):
                    c, half = divmod(start // self.rows + n, 2)
                    self.stage[slot, half, c, :, offset : offset + width] = value[
                        n * self.rows : (n + 1) * self.rows
                    ].astype(bf16)
        for copy in self.local(k):
            copy.start()


    def item_of(self, i, c):
        a, far = self.a, self.line - 1 - self.a
        return i - jnp.where(c > a, a, jnp.where(c < a, far, jnp.maximum(a, far)))

    def inside(self, q):
        return jnp.logical_and(q >= 0, q < self.items)

    def item(self, q):
        q = jnp.clip(q, 0, self.items - 1)
        group = lax.div(q, self.GROUP + 1)
        e = lax.rem(q, self.GROUP + 1)
        tile = self.GROUP * group + jnp.where(e < 2, 1, jnp.where(e == 2, 0, e - 1))
        return group, tile, jnp.minimum(e, 2)

    def block(self, n):
        return jnp.where(n < self.a, n, self.line - 1 - (n - self.a))

    def fetching(self, i, c):
        slot = lax.rem(i, 2)
        _, tile, kind = self.item(self.item_of(i, c))
        side = jnp.where(kind == 0, 0, 1)
        return pltpu.make_async_copy(
            self.wbuf.at[tile, side, c], self.fetch.at[slot, c], self.fetch_sem.at[slot, c]
        )

    def yfetching(self, i, c):
        slot = lax.rem(i, 2)
        _, tile, _ = self.item(self.item_of(i, c))
        return pltpu.make_async_copy(self.ybuf.at[tile, c], self.yfetch.at[slot, c], self.yfetch_sem.at[slot, c])

    def onward(self, i, c, upward):
        slot = lax.rem(i, 2)
        at = lax.rem(jnp.clip(self.item_of(i, c), 0, self.items - 1), self.slots)
        where = c + 1 if upward else c
        return send_to(
            self.fetch.at[slot, c],
            self.zin.at[at, where],
            self.zsend_sem.at[slot, c],
            self.zin_sem.at[at, where],
            self.place.up if upward else self.place.down,
        )

    def drain(self, i):
        @pl.loop(0, self.line)
        def _(c):
            @pl.when(jnp.logical_and(self.inside(self.item_of(i, c)), c != self.a))
            def _():
                self.onward(i, c, False).wait_send()

    def storing(self, q):
        slot = lax.rem(q, 2)
        _, tile, _ = self.item(q)
        return pltpu.make_async_copy(self.final.at[slot], self.place_of(tile), self.final_sem.at[slot])

    def place_of(self, tile):
        is_ffn = tile < self.ffn_tiles
        kind = jnp.where(is_ffn, lax.rem(tile, 3), 3)
        column = jnp.where(is_ffn, lax.div(tile, 3), tile - self.ffn_tiles)
        return self.out.at[kind, :, pl.ds(pl.multiple_of(column * TILE, TILE), TILE)]

    def swapping(self, group):
        return send_to(
            self.swap_out.at[group], self.swap_in.at[group], self.swap_sem.at[0, group], self.swap_sem.at[1, group],
            self.place.pair,
        )

    def begin(self, i):
        @pl.when(i >= 2)
        def _():
            self.drain(i - 2)

        q = i - jnp.minimum(self.a, self.line - 1 - self.a)
        _, tile, kind = self.item(q)

        @pl.when(jnp.logical_and(self.inside(q), kind == 2))
        def _():
            self.halve(tile).wait_recv()

        @pl.loop(0, self.line)
        def _(n):
            c = self.block(n)
            q = self.item_of(i, c)
            _, _, kind = self.item(q)

            @pl.when(self.inside(q))
            def _():
                self.fetching(i, c).start()

            @pl.when(jnp.logical_and(self.inside(q), kind == 2))
            def _():
                self.yfetching(i, c).start()

    def complete(self, i):
        line, a, acc = self.line, self.a, self.acc
        slot = lax.rem(i, 2)

        @pl.loop(0, line)
        def _(n):
            c = self.block(n)
            q = self.item_of(i, c)

            @pl.when(self.inside(q))
            def _():
                group, _, kind = self.item(q)
                at = lax.rem(q, self.slots)

                def arrival(where, device):
                    send_to(
                        self.fetch.at[slot, c],
                        self.zin.at[at, where],
                        self.zsend_sem.at[slot, c],
                        self.zin_sem.at[at, where],
                        device,
                    ).wait_recv()
                    acc[...] += self.zin[at, where].astype(f32)

                self.fetching(i, c).wait()
                acc[...] = self.fetch[slot, c].astype(f32)

                @pl.when(kind == 2)
                def _():
                    self.yfetching(i, c).wait()
                    acc[...] += self.yfetch[slot, c].astype(f32)

                @pl.when(jnp.logical_and(c >= a, a > 0))
                def _():
                    arrival(c + 1, self.place.down)

                @pl.when(jnp.logical_and(c <= a, a < line - 1))
                def _():
                    arrival(c, self.place.up)

                @pl.when(c != a)
                def _():
                    self.fetch[slot, c] = acc[...].astype(bf16)

                    @pl.when(c > a)
                    def _():
                        self.onward(i, c, True).start()

                    @pl.when(c < a)
                    def _():
                        self.onward(i, c, False).start()

                @pl.when(c == a)
                def _():
                    _, _, older = self.item(q - 2)

                    @pl.when(jnp.logical_and(q >= 2, older == 2))
                    def _():
                        self.storing(q - 2).wait()

                    @pl.when(kind == 0)
                    def _():
                        self.swap_out[group] = acc[...].astype(bf16)
                        self.swapping(group).start()

                    @pl.when(kind == 1)
                    def _():
                        self.swap_sum[group] = acc[...]

                    @pl.when(kind == 2)
                    def _():
                        self.final[lax.rem(q, 2)] = acc[...]
                        self.storing(q).start()

    def pump(self, low, high):
        @pl.loop(low, high)
        def _(i):
            self.begin(i)
            self.complete(i)

    def finish(self):
        def summed(group):
            return pltpu.make_async_copy(
                self.swap_sum.at[group], self.place_of(group * self.GROUP + 1), self.sum_sem.at[group]
            )

        @pl.loop(0, self.swaps)
        def _(group):
            self.swapping(group).wait_recv()
            self.swap_sum[group] += self.swap_in[group].astype(f32)
            summed(group).start()

        self.drain(self.steps - 2)
        self.drain(self.steps - 1)
        for q in (self.items - 2, self.items - 1):
            assert q % (self.GROUP + 1) >= 2
            self.storing(q).wait()

        @pl.loop(0, self.swaps)
        def _(group):
            self.swapping(group).wait_send()
            summed(group).wait()

        @pl.loop(0, self.n)
        def _(k):
            @pl.when(self.halved(k))
            def _():
                self.halve(k).wait_send()


class Sum:
    def __init__(self, place, which, term, inbox, across, sems):
        self.place, self.which, self.term, self.inbox, self.across, self.sems = place, which, term, inbox, across, sems
        self.half = inbox.shape[1]

    def own(self, m):
        return rows_at((2 * m + self.place.h) * self.half, self.half)

    def other(self, m):
        return rows_at((2 * m + 1 - self.place.h) * self.half, self.half)

    def first(self, m):
        return send_to(
            self.term.at[self.other(m)], self.inbox.at[m], self.sems.at[self.which, m, 0], self.sems.at[self.which, m, 1],
            self.place.core,
        )

    def second(self, m):
        return send_to(
            self.term.at[self.own(m)], self.across.at[m], self.sems.at[self.which, m, 2], self.sems.at[self.which, m, 3],
            self.place.across,
        )

    def start(self, m):
        self.first(m).start()

    def relay(self, m):
        self.first(m).wait_recv()
        base = (2 * m + self.place.h) * self.half

        @pl.loop(0, self.half // BLOCK)
        def _(r):
            at = rows_at(base + r * BLOCK, BLOCK)
            took = self.inbox[m, rows_at(r * BLOCK, BLOCK), :].astype(f32)
            self.term[at, :] = (self.term[at, :].astype(f32) + took).astype(bf16)

        self.second(m).start()

    def ready(self, m):
        self.second(m).wait_recv()

    def total(self, m, r):
        at = rows_at((2 * m + self.place.h) * self.half + r * BLOCK, BLOCK)
        return self.term[at, :].astype(f32) + self.across[m, rows_at(r * BLOCK, BLOCK), :].astype(f32)

    def settle(self, m):
        self.first(m).wait_send()
        self.second(m).wait_send()

    def spread(self, m, buffer):
        at = self.own(m)
        return send_to(
            buffer.at[at], buffer.at[at], self.sems.at[self.which, m, 4], self.sems.at[self.which, m, 5], self.place.core
        )

    def publish(self, m, staged, out):
        target = out.at[rows_at((2 * m + self.place.h) * self.half, self.half)]
        return (
            pltpu.make_async_copy(staged.at[m], target, self.sems.at[self.which, m, 6]),
            send_to(
                staged.at[m], target, self.sems.at[self.which, m, 4], self.sems.at[self.which, m, 5],
                self.place.core,
            ),
        )


def gain_row(gain):
    return gain[...].reshape(1, gain.shape[0])


def normal(values):
    scale = lax.rsqrt(jnp.mean(values * values, axis=-1, keepdims=True) + EPSILON)
    return scale, values * scale


def fold(values):
    return jnp.sum(values.reshape(values.shape[0] // 8, 8, values.shape[1]), axis=0)


def kernel(line, rows, n_ffn, names, *refs):
    v = dict(zip(names, refs))
    (lengths, order, mask, mix_gain, ffn_gain, taps_in) = (
        v[n] for n in ("lengths", "order", "mask", "mix_gain", "ffn_gain", "taps")
    )
    place = Place(line)
    n1, n2, g, term0, term1, r1h = (v[n] for n in ("n1", "n2", "g", "term0", "term1", "r1h"))
    inbox0, inbox1, across0, across1, across2 = (v[n] for n in ("inbox0", "inbox1", "across0", "across1", "across2"))
    pb, pc, px, po = (v[n] for n in ("pb", "pc", "px", "po"))
    bs, cs, xs, bx, ym, cat = (v[n] for n in ("bs", "cs", "xs", "bx", "ym", "cat"))
    sums, load = v["sums"], v["load"]
    tokens, width = n1.shape
    local = tokens // MICRO
    spans = local // SPAN
    pieces = MICRO * spans
    half = SPAN // 2
    chan = bs.shape[1]
    units = v["w_down"].shape[0]
    full = units // TILE
    rest = units - full * TILE
    docs = lengths.shape[1]
    rs = Scatter(
        place, 3 * n_ffn + 6, 3 * n_ffn, rows, v["wbuf"], v["ybuf"], v["grads"],
        [v[n] for n in Scatter.NAMES],
    )
    branch = Sum(place, 0, term0, inbox0, across0, sums)
    second = Sum(place, 1, term1, inbox1, across1, sums)
    feed = Sum(place, 2, term0, inbox0, across2, sums)
    first = Sum(place, 3, term0, inbox1, across0, sums)

    barrier = pltpu.get_barrier_semaphore()
    for device in (place.pair, place.next, place.last, place.core, place.across):
        pl.semaphore_signal(barrier, inc=1, device_id=device, device_id_type=MESH)

    @pl.loop(0, line)
    def _(c):
        @pl.when(c != place.a)
        def _():
            pl.semaphore_signal(barrier, inc=1, device_id=(c * 2 + place.b, place.t), device_id_type=MESH)

    def loading(which, src, dst):
        return pltpu.make_async_copy(src, dst, load.at[which])

    projections = [
        loading(2, v["proj_b"], pb),
        loading(3, v["proj_x"], px),
        loading(4, v["proj_c"], pc),
        loading(5, v["proj_out"], po),
    ]
    cot_load = [loading(6 + m, v["cotangent"].at[m], g.at[m * local : (m + 1) * local]) for m in range(MICRO)]
    wgu, wdb = v["wgu"], v["wdb"]

    def weights(j, slot):
        at = pl.ds(pl.multiple_of(j * TILE, TILE), TILE)
        return [
            pltpu.make_async_copy(v[src].at[at], dst, v["wsem"].at[slot, q])
            for q, (src, dst) in enumerate(
                (("w_gate", wgu.at[slot, 0:TILE]), ("w_up", wgu.at[slot, TILE:]), ("w_down", wdb.at[slot]))
            )
        ]

    def rest_weights():
        slot = full % 2
        return [
            pltpu.make_async_copy(v[src].at[full * TILE :], dst, v["wsem"].at[slot, q])
            for q, (src, dst) in enumerate(
                (
                    ("w_gate", wgu.at[slot, 0:rest]),
                    ("w_up", wgu.at[slot, TILE : TILE + rest]),
                    ("w_down", wdb.at[slot, 0:rest]),
                )
            )
        ]

    taps = taps_in[...].astype(f32)
    row_ids = lax.broadcasted_iota(jnp.int32, (SPAN, 1), 0)
    tap = [taps[k : k + 1, :] for k in range(3)]

    def span_facts(m, q):
        mine = order[m, place.s * spans + q]
        position = mine * SPAN + row_ids
        near = position >= 0
        far = position >= 0
        begin = jnp.int32(0)
        for n in range(docs):
            near = jnp.logical_and(near, position != begin)
            far = jnp.logical_and(far, position != begin + 1)
            begin = begin + lengths[m, n]
        return mine, near, jnp.logical_and(near, far)

    def terms(m, q, near, far, mine):
        here = bx[pl.ds(m * local + q * SPAN, SPAN), :].astype(f32)
        older = jnp.zeros((1, chan), f32)
        newer = jnp.zeros((1, chan), f32)
        for k in range(spans):
            took = order[m, place.before * spans + k] == mine - 1
            tail = v["halo_in"][m, k].astype(f32)
            older = older + jnp.where(took, tail[14:15], 0.0)
            newer = newer + jnp.where(took, tail[15:16], 0.0)
        far_term = pltpu.roll(here, 2, 0)
        far_term = jnp.where(row_ids == 0, older, jnp.where(row_ids == 1, newer, far_term))
        near_term = jnp.where(row_ids == 0, newer, pltpu.roll(here, 1, 0))
        return jnp.where(far, far_term, 0.0), jnp.where(near, near_term, 0.0), here

    def halo(m):
        return send_to(
            v["halo_out"].at[m], v["halo_in"].at[m], v["hsem"].at[0, m], v["hsem"].at[1, m], place.next
        )

    def halo_back(m):
        return send_to(
            v["back_out"].at[m], v["back_in"].at[m], v["hsem"].at[2, m], v["hsem"].at[3, m], place.last
        )

    def mixer_half(m, x):
        base = m * local

        @pl.loop(0, local // BLOCK)
        def _(r):
            at = rows_at(base + r * BLOCK, BLOCK)
            _, unit = normal(x[at, :].astype(f32))
            n1[at, :] = (unit * gain_row(mix_gain)).astype(bf16)

        at = pl.ds(base, local)
        if m == 0:
            projections[0].wait()
        bs[at, :] = dot_nn(n1[at, :], pb[...])
        if m == 0:
            projections[1].wait()
        xs[at, :] = dot_nn(n1[at, :], px[...])
        for q in range(spans):
            rows_q = pl.ds(base + q * SPAN, SPAN)
            product = (bs[rows_q, :] * xs[rows_q, :]).astype(bf16)
            bx[rows_q, :] = product
            v["halo_out"][m, q] = product[SPAN - 16 :, :]

    def mixer_rest(m):
        base = m * local
        at = pl.ds(base, local)
        if m == 0:
            projections[2].wait()
        cs[at, :] = dot_nn(n1[at, :], pc[...])
        halo(m).wait_recv()
        for q in range(spans):
            rows_q = pl.ds(base + q * SPAN, SPAN)
            mine, near, far = span_facts(m, q)
            far_term, near_term, here = terms(m, q, near, far, mine)
            conv = tap[0] * far_term + tap[1] * near_term + tap[2] * here
            ym[rows_q, :] = (cs[rows_q, :] * conv).astype(bf16)
            if m == 0 and q == 0:
                projections[3].wait()
            term0[rows_q, :] = dot_nn(ym[rows_q, :], po[...]).astype(bf16)
            piece = m * spans + q
            branch.start(piece)
            if piece > 0:
                branch.relay(piece - 1)

    def middle(p, x):
        branch.ready(p)

        @pl.loop(0, half // BLOCK)
        def _(r):
            at = rows_at((2 * p + place.h) * half + r * BLOCK, BLOCK)
            value = x[at, :].astype(f32) + branch.total(p, r)
            r1h[rows_at(p * half + r * BLOCK, BLOCK), :] = value
            _, unit = normal(value)
            n2[at, :] = (unit * gain_row(ffn_gain)).astype(bf16)

        branch.spread(p, n2).start()

    def masked(m):
        cot_load[m].wait()
        for q in range(spans):
            kept = mask[m : m + 1, q * SPAN : (q + 1) * SPAN].astype(f32)
            kept = jnp.transpose(jnp.broadcast_to(kept, (SPAN, SPAN)))
            rows_q = pl.ds(m * local + q * SPAN, SPAN)
            for c in range(width // SPAN):
                cols = pl.ds(c * SPAN, SPAN)
                g[rows_q, cols] = (g[rows_q, cols].astype(f32) * kept).astype(bf16)

    def mixer_forward(x):
        x_load = [loading(m, v["tokens"].at[m], x.at[m * local : (m + 1) * local]) for m in range(MICRO)]
        for copy in [x_load[0]] + projections[:2] + [x_load[1]] + projections[2:] + cot_load + weights(0, 0):
            copy.start()
        x_load[0].wait()
        mixer_half(0, x)
        pl.semaphore_wait(barrier, 5 + line - 1)
        halo(0).start()
        x_load[1].wait()
        mixer_rest(0)
        mixer_half(1, x)
        halo(1).start()
        mixer_rest(1)
        masked(0)
        branch.relay(pieces - 1)
        masked(1)
        for p in range(pieces):
            middle(p, x)
        for p in range(pieces):
            branch.spread(p, n2).wait()
            branch.settle(p)

    pl.run_scoped(mixer_forward, pltpu.VMEM((tokens, width), bf16))

    def steps_by(j):
        return jnp.where(j < 0, 0, 2 * j - jnp.where(j >= 3, 1, 0) - jnp.where(j >= 4, 1, 0))

    def feed_forward(oacc, dacc, hb, dgu):
        oacc[...] = jnp.zeros_like(oacc)
        dacc[...] = jnp.zeros_like(dacc)

        @pl.loop(0, n_ffn)
        def _(j):
            slot = lax.rem(j, 2)

            @pl.when(j < full)
            def _():
                for copy in weights(jnp.minimum(j, full - 1), slot):
                    copy.wait()

            if rest:

                @pl.when(j == full)
                def _():
                    for copy in rest_weights():
                        copy.wait()

            @pl.when(j + 1 < full)
            def _():
                for copy in weights(jnp.minimum(j + 1, full - 1), 1 - slot):
                    copy.start()

            if rest:

                @pl.when(j + 1 == full)
                def _():
                    blank = jnp.zeros((TILE - rest, width), bf16)
                    wgu[full % 2, rest:TILE, :] = blank
                    wgu[full % 2, TILE + rest :, :] = blank
                    wdb[full % 2, rest:, :] = blank
                    for copy in rest_weights():
                        copy.start()

            step = steps_by(j - 1)
            one = steps_by(j) > step
            two = steps_by(j) > step + 1

            @pl.when(one)
            def _():
                rs.begin(step)

            for m in range(MICRO):
                at = slice(m * local, (m + 1) * local)
                both = dot_nt(n2[at, :], wgu[slot])
                back = dot_nt(g[at, :], wdb[slot])
                gate, up = both[:, :TILE], both[:, TILE:]
                sigma = jax.nn.sigmoid(gate)
                silu = gate * sigma
                hb[at, :] = (silu * up).astype(bf16)
                dgu[at, :TILE] = (back * up * sigma * (1.0 + gate * (1.0 - sigma))).astype(bf16)
                dgu[at, TILE:] = (back * silu).astype(bf16)

            @pl.when(one)
            def _():
                rs.complete(step)

            @pl.when(two)
            def _():
                rs.begin(step + 1)

            rs.produce(3 * j, [(0, g, lambda: hb[...])])
            oacc[...] += dot_nn(hb[...], wdb[slot])

            @pl.when(two)
            def _():
                rs.complete(step + 1)

            rs.produce(3 * j + 1, [(0, n2, lambda: dgu[:, :TILE])])
            dacc[...] += dot_nn(dgu[...], wgu[slot])
            rs.produce(3 * j + 2, [(0, n2, lambda: dgu[:, TILE:])])

        rs.flush(3 * n_ffn - 1)
        for p in range(pieces):
            at = pl.ds(p * SPAN, SPAN)
            term1[at, :] = dacc[at, :].astype(bf16)
            second.start(p)
            if p > 1:
                second.relay(p - 2)
        for p in range(pieces):
            at = pl.ds(p * SPAN, SPAN)
            term0[at, :] = oacc[at, :].astype(bf16)
            feed.start(p)
            if p < 2:
                second.relay(pieces - 2 + p)

    pl.run_scoped(
        feed_forward,
        pltpu.VMEM((tokens, width), f32),
        pltpu.VMEM((tokens, width), f32),
        pltpu.VMEM((tokens, TILE), bf16),
        pltpu.VMEM((tokens, 2 * TILE), bf16),
    )
    taken = [2 * (n_ffn - 1) - 2]

    def pump(count):
        rs.pump(taken[0], taken[0] + count)
        taken[0] += count

    def backward(dr1, xh, dym, dbx, gain_one, gain_two, tap_rows):
        x_load = [
            loading(
                8 + p,
                v["tokens"].at[p // spans, rows_at(p % spans * SPAN + place.h * half, half)],
                xh.at[p * half : (p + 1) * half],
            )
            for p in range(pieces)
        ]
        for copy in x_load:
            copy.start()
        gain_one[...] = jnp.zeros_like(gain_one)
        gain_two[...] = jnp.zeros_like(gain_two)
        pump(3)
        for p in range(pieces):
            feed.relay(p)
        pump(1)

        for p in range(pieces):
            second.ready(p)

            @pl.loop(0, half // BLOCK)
            def _(r):
                at = rows_at((2 * p + place.h) * half + r * BLOCK, BLOCK)
                here = rows_at(p * half + r * BLOCK, BLOCK)
                grad = second.total(p, r)
                scale, unit = normal(r1h[here, :])
                gain_two[...] += fold(grad * unit)
                weighted = grad * gain_row(ffn_gain)
                inner = jnp.mean(weighted * unit, axis=-1, keepdims=True)
                value = g[at, :].astype(f32) + scale * (weighted - unit * inner)
                dr1[here, :] = value
                n2[at, :] = value.astype(bf16)

            second.spread(p, n2).start()
            if p % 3 == 2:
                pump(2)

        for p in range(pieces):
            second.spread(p, n2).wait()
            second.settle(p)
        dym[...] = dot_nt(n2[...], po[...])
        tap_sums = [jnp.zeros((8, chan), f32) for _ in range(3)]
        for m in range(MICRO):
            for q in range(spans):
                rows_q = pl.ds(m * local + q * SPAN, SPAN)
                mine, near, far = span_facts(m, q)
                far_term, near_term, here = terms(m, q, near, far, mine)
                grad = dym[rows_q, :]
                cat[rows_q, chan : 2 * chan] = (
                    grad * (tap[0] * far_term + tap[1] * near_term + tap[2] * here)
                ).astype(bf16)
                grad = grad * cs[rows_q, :]
                for k, other in enumerate((far_term, near_term, here)):
                    tap_sums[k] = tap_sums[k] + fold(grad * other)
                old = jnp.where(far, tap[0] * grad, 0.0)
                mid = jnp.where(near, tap[1] * grad, 0.0)
                dbx[rows_q, :] = (
                    tap[2] * grad
                    + jnp.where(row_ids < SPAN - 1, pltpu.roll(mid, SPAN - 1, 0), 0.0)
                    + jnp.where(row_ids < SPAN - 2, pltpu.roll(old, SPAN - 2, 0), 0.0)
                )
                top_ids = row_ids[:8]
                v["back_out"][m, q] = jnp.where(top_ids < 2, old[:8], 0.0) + jnp.where(
                    top_ids == 1, mid[0:1], 0.0
                )
            halo_back(m).start()
            pump(1)
        for k in range(3):
            tap_rows[k] = tap_sums[k]
        for m in range(MICRO):
            halo_back(m).wait_recv()
            for q in range(spans):
                rows_q = pl.ds(m * local + q * SPAN, SPAN)
                mine = order[m, place.s * spans + q]
                from_next = jnp.zeros((8, chan), f32)
                for k in range(spans):
                    took = order[m, place.after * spans + k] == mine + 1
                    from_next = from_next + jnp.where(took, v["back_in"][m, k], 0.0)
                value = dbx[rows_q, :]
                value = (
                    value
                    + jnp.where(row_ids == SPAN - 2, from_next[0:1], 0.0)
                    + jnp.where(row_ids == SPAN - 1, from_next[1:2], 0.0)
                )
                cat[rows_q, 0:chan] = (value * xs[rows_q, :]).astype(bf16)
                cat[rows_q, 2 * chan :] = (value * bs[rows_q, :]).astype(bf16)
        k0 = 3 * n_ffn
        wide = 3 * chan
        whole = wide // TILE
        for k in range(whole):
            rs.produce(k0 + k, [(0, n1, lambda k=k: cat[:, k * TILE : (k + 1) * TILE])])
            if k == 1:
                pump(1)
        left = wide - whole * TILE
        rs.produce(
            k0 + whole,
            [
                (0, n1, lambda: cat[:, whole * TILE :]),
                (left, n2, lambda: ym[:, 0 : TILE - left]),
            ],
        )
        rs.produce(k0 + whole + 1, [(0, n2, lambda: ym[:, TILE - left :])])
        rs.flush(k0 + whole + 1)
        pump(2)

        for p in range(pieces):
            feed.ready(p)

            @pl.loop(0, half // BLOCK)
            def _(r):
                here = rows_at(p * half + r * BLOCK, BLOCK)
                at = rows_at(r * BLOCK, BLOCK)
                across2[p, at, :] = (r1h[here, :] + feed.total(p, r)).astype(bf16)

            for copy in feed.publish(p, across2, v["block_out"]):
                copy.start()
            feed.settle(p)
        pump(1)
        for m in range(MICRO):
            at = pl.ds(m * local, local)
            term0[at, :] = (
                dot_nt(cat[at, 0:chan], pb[...])
                + dot_nt(cat[at, chan : 2 * chan], pc[...])
                + dot_nt(cat[at, 2 * chan :], px[...])
            ).astype(bf16)
            for p in range(m * spans, (m + 1) * spans):
                first.start(p)
            pump(1)
        for p in range(pieces):
            first.relay(p)
        pump(2)
        for p in range(pieces):
            x_load[p].wait()
            first.ready(p)

            @pl.loop(0, half // BLOCK)
            def _(r):
                here = rows_at(p * half + r * BLOCK, BLOCK)
                at = rows_at(r * BLOCK, BLOCK)
                grad = first.total(p, r)
                scale, unit = normal(xh[here, :].astype(f32))
                gain_one[...] += fold(grad * unit)
                weighted = grad * gain_row(mix_gain)
                inner = jnp.mean(weighted * unit, axis=-1, keepdims=True)
                across0[p, at, :] = (dr1[here, :] + scale * (weighted - unit * inner)).astype(bf16)

            for copy in first.publish(p, across0, v["d_tokens"]):
                copy.start()
            if p % 3 == 2:
                pump(1)

        small, gather = v["small"], v["gather"]
        ssem = v["ssem"]
        side = width // 2
        small[0] = jnp.zeros((8, side), f32)
        for n, gain in enumerate((gain_one, gain_two)):
            row = jnp.sum(gain[...], axis=0, keepdims=True)
            small[0, 2 * n : 2 * n + 1, :] = row[:, :side]
            small[0, 2 * n + 1 : 2 * n + 2, :] = row[:, side:]
        for k in range(3):
            at = k % 2 * chan
            small[0, 4 + k // 2 : 5 + k // 2, at : at + chan] = jnp.sum(tap_rows[k], axis=0, keepdims=True)
        core = send_to(small.at[0], gather.at[0], ssem.at[0], ssem.at[1], place.core)
        core.start()
        core.wait_recv()
        small[1] = small[0] + jnp.where(lax.broadcasted_iota(jnp.int32, (8, 1), 0) < 4, gather[0], 0.0)
        pair = send_to(small.at[1], gather.at[1], ssem.at[2], ssem.at[3], place.pair)
        pair.start()
        pair.wait_recv()
        small[2] = small[1] + gather[1]

        def along(c, slot):
            return send_to(
                small.at[2], gather.at[2 + slot], ssem.at[4 + c], ssem.at[4 + line + slot], (c * 2 + place.b, place.t)
            )

        @pl.loop(0, line)
        def _(c):
            @pl.when(c != place.a)
            def _():
                along(c, place.a).start()

        gather[2 + place.a] = small[2]

        rs.pump(taken[0], rs.steps)

        @pl.loop(0, line)
        def _(c):
            @pl.when(c != place.a)
            def _():
                along(c, c).wait_recv()
                along(c, place.a).wait_send()

        total = gather[2]
        for c in range(1, line):
            total = total + gather[2 + c]
        v["small_out"][...] = total
        core.wait_send()
        pair.wait_send()
        for m in range(MICRO):
            halo(m).wait_send()
            halo_back(m).wait_send()
        for m in range(pieces):
            first.settle(m)
            for each, staged, out in ((feed, across2, v["block_out"]), (first, across0, v["d_tokens"])):
                for copy in each.publish(m, staged, out):
                    copy.wait()
        rs.finish()

    pl.run_scoped(
        backward,
        pltpu.VMEM((tokens // 2, width), f32),
        pltpu.VMEM((tokens // 2, width), bf16),
        pltpu.VMEM((tokens, chan), f32),
        pltpu.VMEM((tokens, chan), f32),
        pltpu.VMEM((8, width), f32),
        pltpu.VMEM((8, width), f32),
        pltpu.VMEM((3, 8, chan), f32),
    )


def body(
    seq_count,
    tokens,
    mix_gain,
    proj_b,
    proj_c,
    proj_x,
    conv_taps,
    proj_out,
    ffn_gain,
    w_gate,
    w_up,
    w_down,
    cotangent,
    seq_lengths,
    span_order,
    keep_mask,
):
    local, width = tokens.shape[1:]
    total = MICRO * local
    half = SPAN // 2
    chan = proj_b.shape[1]
    units = w_gate.shape[1]
    n_ffn = pl.cdiv(units, TILE)
    line = seq_count // 2
    rows = width // seq_count
    n_tiles = 3 * n_ffn + 6
    spans = local // SPAN
    pieces = MICRO * spans
    dma = pltpu.SemaphoreType.DMA
    vmem = pl.BlockSpec(memory_space=pltpu.VMEM)
    smem = pl.BlockSpec(memory_space=pltpu.SMEM)
    hbm = pl.BlockSpec(memory_space=pl.ANY)
    shape = jax.ShapeDtypeStruct
    inputs = [
        ("lengths", seq_lengths, smem),
        ("order", span_order, smem),
        ("mask", keep_mask, vmem),
        ("mix_gain", mix_gain, vmem),
        ("ffn_gain", ffn_gain, vmem),
        ("taps", conv_taps, vmem),
        ("tokens", tokens, hbm),
        ("cotangent", cotangent, hbm),
        ("proj_b", proj_b, hbm),
        ("proj_c", proj_c, hbm),
        ("proj_x", proj_x, hbm),
        ("proj_out", proj_out, hbm),
        ("w_gate", w_gate.T, hbm),
        ("w_up", w_up.T, hbm),
        ("w_down", w_down, hbm),
    ]
    outputs = [
        ("block_out", shape((total, width), bf16), hbm),
        ("d_tokens", shape((total, width), bf16), hbm),
        ("grads", shape((4, rows, n_ffn * TILE), f32), hbm),
        ("small_out", shape((8, width // 2), f32), vmem),
        ("wbuf", shape((n_tiles, 2, line, rows, TILE), bf16), hbm),
        ("ybuf", shape((n_tiles, line, rows, TILE), bf16), hbm),
    ]
    scratch = [
        ("n1", pltpu.VMEM((total, width), bf16)),
        ("n2", pltpu.VMEM((total, width), bf16)),
        ("g", pltpu.VMEM((total, width), bf16)),
        ("term0", pltpu.VMEM((total, width), bf16)),
        ("term1", pltpu.VMEM((total, width), bf16)),
        ("r1h", pltpu.VMEM((total // 2, width), f32)),
        ("inbox0", pltpu.VMEM((pieces, half, width), bf16)),
        ("inbox1", pltpu.VMEM((pieces, half, width), bf16)),
        ("across0", pltpu.VMEM((pieces, half, width), bf16)),
        ("across1", pltpu.VMEM((pieces, half, width), bf16)),
        ("across2", pltpu.VMEM((pieces, half, width), bf16)),
        ("pb", pltpu.VMEM((width, chan), bf16)),
        ("pc", pltpu.VMEM((width, chan), bf16)),
        ("px", pltpu.VMEM((width, chan), bf16)),
        ("po", pltpu.VMEM((chan, width), bf16)),
        ("bs", pltpu.VMEM((total, chan), f32)),
        ("cs", pltpu.VMEM((total, chan), f32)),
        ("xs", pltpu.VMEM((total, chan), f32)),
        ("bx", pltpu.VMEM((total, chan), bf16)),
        ("ym", pltpu.VMEM((total, chan), bf16)),
        ("cat", pltpu.VMEM((total, 3 * chan), bf16)),
        ("wgu", pltpu.VMEM((2, 2 * TILE, width), bf16)),
        ("wdb", pltpu.VMEM((2, TILE, width), bf16)),
        ("halo_out", pltpu.VMEM((MICRO, spans, 16, chan), bf16)),
        ("halo_in", pltpu.VMEM((MICRO, spans, 16, chan), bf16)),
        ("back_out", pltpu.VMEM((MICRO, spans, 8, chan), f32)),
        ("back_in", pltpu.VMEM((MICRO, spans, 8, chan), f32)),
        ("small", pltpu.VMEM((3, 8, width // 2), f32)),
        ("gather", pltpu.VMEM((2 + line, 8, width // 2), f32)),
        ("load", dma((8 + pieces,))),
        ("wsem", dma((2, 3))),
        ("sums", dma((4, pieces, 7))),
        ("hsem", dma((4, MICRO))),
        ("ssem", dma((4 + 2 * line,))),
    ]
    scratch += list(zip(Scatter.NAMES, Scatter.scratch(n_tiles, line, rows)))
    names = [n for n, _, _ in inputs] + [n for n, _, _ in outputs] + [n for n, _ in scratch]
    results = pl.pallas_call(
        functools.partial(kernel, line, rows, n_ffn, names),
        out_shape=tuple(s for _, s, _ in outputs),
        in_specs=[s for _, _, s in inputs],
        out_specs=tuple(s for _, _, s in outputs),
        scratch_shapes=[s for _, s in scratch],
        compiler_params=pltpu.CompilerParams(
            collective_id=0, has_side_effects=True, vmem_limit_bytes=62 * 2**20 - 2**19
        ),
    )(*[a for _, a, _ in inputs])
    block_out, d_tokens, grads, small = results[:4]
    return (
        block_out.reshape(tokens.shape),
        d_tokens.reshape(tokens.shape),
        small[0:2].reshape(width),
        grads[3, :, 0:chan],
        grads[3, :, chan : 2 * chan],
        grads[3, :, 2 * chan : 3 * chan],
        small[4:6].reshape(4, chan)[:3],
        grads[3, :, 3 * chan : 4 * chan].T,
        small[2:4].reshape(width),
        grads[1, :, :units],
        grads[2, :, :units],
        grads[0, :, :units].T,
    )


def solution(mesh):
    placed = (
        P(None, "seq", None),
        P(),
        P(None, "tp"),
        P(None, "tp"),
        P(None, "tp"),
        P(None, "tp"),
        P("tp", None),
        P(),
        P(None, "tp"),
        P(None, "tp"),
        P("tp", None),
        P(None, "seq", None),
        P(),
        P(),
        P(None, "seq"),
    )
    return jax.shard_map(
        functools.partial(body, mesh.shape["seq"]),
        mesh=mesh,
        in_specs=placed,
        out_specs=(
            P(None, "seq", None),
            P(None, "seq", None),
            P(),
            P("seq", "tp"),
            P("seq", "tp"),
            P("seq", "tp"),
            P(None, "tp"),
            P("tp", "seq"),
            P(),
            P("seq", "tp"),
            P("seq", "tp"),
            P("tp", "seq"),
        ),
        check_vma=False,
    )
```

```python
import functools
import jax
import jax.numpy as jnp
from jax import lax
from jax.experimental import pallas as pl
from jax.experimental.pallas import tpu as pltpu
from jax.sharding import PartitionSpec as P

SPAN = 128
MICRO = 2
EPSILON = 1e-05
MESH = pl.DeviceIdType.MESH
TILE = 256
BLOCK = 32
ROWS = 384
f32 = jnp.float32
bf16 = jnp.bfloat16


def dot_nn(a, b):
    return jnp.dot(a, b, preferred_element_type=f32)


def dot_nt(a, b):
    return lax.dot_general(a, b, (((1,), (1,)), ((), ())), preferred_element_type=f32)


def dot_tn(a, b):
    return lax.dot_general(a, b, (((0,), (0,)), ((), ())), preferred_element_type=f32)


def send_to(src, dst, send_sem, recv_sem, device):
    return pltpu.make_async_remote_copy(
        src_ref=src,
        dst_ref=dst,
        send_sem=send_sem,
        recv_sem=recv_sem,
        device_id=device,
        device_id_type=MESH,
    )


def rows_at(start, size):
    return pl.ds(pl.multiple_of(start, 16), size)


class Place:
    def __init__(self, line):
        self.line = line
        self.s = lax.axis_index("seq")
        self.t = lax.axis_index("tp")
        self.a = lax.div(self.s, 2)
        self.b = lax.rem(self.s, 2)
        self.h = lax.rem(self.t, 2)
        count = 2 * line
        self.pair = (self.a * 2 + 1 - self.b, self.t)
        self.up = (lax.rem(self.a + 1, line) * 2 + self.b, self.t)
        self.down = (lax.rem(self.a + line - 1, line) * 2 + self.b, self.t)
        self.after = lax.rem(self.s + 1, count)
        self.before = lax.rem(self.s + count - 1, count)
        self.next = (self.after, self.t)
        self.last = (self.before, self.t)
        self.core = (self.s, self.t + 1 - 2 * self.h)
        self.across = (self.s, lax.rem(self.t + 2, 4))


class Scatter:
    NAMES = (
        "stage", "zin", "fetch", "yfetch", "acc", "final", "swap_out", "swap_in", "swap_sum",
        "stage_sem", "ysend_sem", "yrecv_sem", "zsend_sem", "zin_sem", "fetch_sem", "yfetch_sem", "final_sem",
        "swap_sem", "sum_sem",
    )
    EARLY = 4
    AHEAD = 7

    def __init__(self, place, n_tiles, ffn_tiles, rows, wbuf, ybuf, out, scratch):
        self.place, self.a, self.b, self.line = place, place.a, place.b, place.line
        self.n, self.ffn_tiles, self.rows = n_tiles, ffn_tiles, rows
        self.wbuf, self.ybuf, self.out = wbuf, ybuf, out
        for name, ref in zip(self.NAMES, scratch):
            setattr(self, name, ref)
        self.slots = self.zin.shape[0]
        self.items = n_tiles + self.EARLY
        self.hop = self.hop_of(self.line)
        self.held = self.fetch.shape[0]
        self.steps = self.items + self.hop * (self.line - 1)
        self.swaps = self.swap_sum.shape[0]

    @staticmethod
    def hop_of(line):
        return 2 if line <= 4 else 1

    @classmethod
    def scratch(cls, n_tiles, line, rows):
        slots = cls.hop_of(line) * line + 1
        held = 2 * cls.hop_of(line)
        swaps = cls.EARLY
        dma = pltpu.SemaphoreType.DMA
        return [
            pltpu.VMEM((2, 2, line, rows, TILE), bf16),
            pltpu.VMEM((slots, line + 1, rows, TILE), bf16),
            pltpu.VMEM((held, line, rows, TILE), bf16),
            pltpu.VMEM((2, line, rows, TILE), bf16),
            pltpu.VMEM((rows, TILE), f32),
            pltpu.VMEM((2, rows, TILE), f32),
            pltpu.VMEM((swaps, rows, TILE), bf16),
            pltpu.VMEM((swaps, rows, TILE), bf16),
            pltpu.VMEM((swaps, rows, TILE), f32),
            dma((2, 2)),
            dma((n_tiles,)),
            dma((n_tiles,)),
            dma((held, line)),
            dma((slots, line + 1)),
            dma((held, line)),
            dma((2, line)),
            dma((2,)),
            dma((2, swaps)),
            dma((swaps,)),
        ]


    def local(self, k):
        slot = lax.rem(k, 2)
        return (
            pltpu.make_async_copy(self.stage.at[slot, 1 - self.b], self.wbuf.at[k, 0], self.stage_sem.at[slot, 0]),
            pltpu.make_async_copy(self.stage.at[slot, self.b], self.wbuf.at[k, 1], self.stage_sem.at[slot, 1]),
        )

    def halved(self, k):
        return jnp.logical_or(lax.rem(k, 3) == 0, k > self.early_tile(self.EARLY - 1))

    @staticmethod
    def early_tile(n):
        return n + 1 + n // 2 if isinstance(n, int) else n + 1 + lax.div(n, 2)

    def halve(self, k):
        return send_to(
            self.wbuf.at[k, 0], self.ybuf.at[k], self.ysend_sem.at[k], self.yrecv_sem.at[k], self.place.pair
        )

    def flush(self, k):
        for copy in self.local(k):
            copy.wait()

    def halved_tile(self, n):
        return jnp.where(n < 2, 3 * n, n + self.EARLY)

    def start_halving(self, n):
        self.halve(self.halved_tile(n)).start()

    def produce(self, k, parts):
        @pl.when(jnp.logical_and(k != 0, k != self.ffn_tiles))
        def _():
            self.flush(k - 1)

        slot = lax.rem(k, 2)
        for offset, left, right in parts:
            width = right().shape[1]
            for start in range(0, left.shape[1], ROWS):
                value = dot_tn(left[:, start : start + ROWS], right())
                for n in range(ROWS // self.rows):
                    c, half = divmod(start // self.rows + n, 2)
                    self.stage[slot, half, c, :, offset : offset + width] = value[
                        n * self.rows : (n + 1) * self.rows
                    ].astype(bf16)
        for copy in self.local(k):
            copy.start()


    def item_of(self, i, c):
        a, far = self.a, self.line - 1 - self.a
        return i - self.hop * jnp.where(c > a, a, jnp.where(c < a, far, jnp.maximum(a, far)))

    def inside(self, q):
        return jnp.logical_and(q >= 0, q < self.items)

    def item(self, q):
        q = jnp.clip(q, 0, self.items - 1)
        early = q < 2 * self.EARLY
        n = q - 2 * self.EARLY
        tile = self.halved_tile(n)
        return (
            jnp.where(early, self.early_tile(lax.div(q, 2)), tile),
            jnp.where(early, lax.rem(q, 2), 2),
        )

    def block(self, n):
        return jnp.where(n < self.a, n, self.line - 1 - (n - self.a))

    def fetching(self, i, c):
        slot = lax.rem(i, self.held)
        tile, kind = self.item(self.item_of(i, c))
        side = jnp.where(kind == 0, 0, 1)
        return pltpu.make_async_copy(
            self.wbuf.at[tile, side, c], self.fetch.at[slot, c], self.fetch_sem.at[slot, c]
        )

    def yfetching(self, i, c):
        slot = lax.rem(i, 2)
        tile, _ = self.item(self.item_of(i, c))
        return pltpu.make_async_copy(self.ybuf.at[tile, c], self.yfetch.at[slot, c], self.yfetch_sem.at[slot, c])

    def onward(self, i, c, upward):
        slot = lax.rem(i, self.held)
        at = lax.rem(jnp.clip(self.item_of(i, c), 0, self.items - 1), self.slots)
        where = c + 1 if upward else c
        return send_to(
            self.fetch.at[slot, c],
            self.zin.at[at, where],
            self.zsend_sem.at[slot, c],
            self.zin_sem.at[at, where],
            self.place.up if upward else self.place.down,
        )

    def drain(self, i):
        @pl.loop(0, self.line)
        def _(c):
            @pl.when(jnp.logical_and(self.inside(self.item_of(i, c)), c != self.a))
            def _():
                self.onward(i, c, False).wait_send()

    def storing(self, q):
        slot = lax.rem(q, 2)
        tile, _ = self.item(q)
        return pltpu.make_async_copy(self.final.at[slot], self.place_of(tile), self.final_sem.at[slot])

    def place_of(self, tile):
        is_ffn = tile < self.ffn_tiles
        kind = jnp.where(is_ffn, lax.rem(tile, 3), 3)
        column = jnp.where(is_ffn, lax.div(tile, 3), tile - self.ffn_tiles)
        return self.out.at[kind, :, pl.ds(pl.multiple_of(column * TILE, TILE), TILE)]

    def swapping(self, group):
        return send_to(
            self.swap_out.at[group], self.swap_in.at[group], self.swap_sem.at[0, group], self.swap_sem.at[1, group],
            self.place.pair,
        )

    def begin(self, i):
        @pl.when(i >= self.held)
        def _():
            self.drain(i - self.held)

        ahead = lax.div(3 * i, 4)
        fresh = jnp.logical_and(ahead > lax.div(3 * i - 3, 4), i >= self.AHEAD)

        @pl.when(jnp.logical_and(fresh, ahead + 2 < self.n - self.EARLY))
        def _():
            self.start_halving(ahead + 2)

        q = i - self.hop * jnp.minimum(self.a, self.line - 1 - self.a)
        tile, kind = self.item(q)

        @pl.when(jnp.logical_and(self.inside(q), kind == 2))
        def _():
            self.halve(tile).wait_recv()

        @pl.loop(0, self.line)
        def _(n):
            c = self.block(n)
            q = self.item_of(i, c)
            _, kind = self.item(q)

            @pl.when(self.inside(q))
            def _():
                self.fetching(i, c).start()

            @pl.when(jnp.logical_and(self.inside(q), kind == 2))
            def _():
                self.yfetching(i, c).start()

    def complete(self, i):
        line, a, acc = self.line, self.a, self.acc
        slot = lax.rem(i, self.held)
        yslot = lax.rem(i, 2)

        @pl.loop(0, line)
        def _(n):
            c = self.block(n)
            q = self.item_of(i, c)

            @pl.when(self.inside(q))
            def _():
                _, kind = self.item(q)
                group = jnp.minimum(lax.div(q, 2), self.EARLY - 1)
                at = lax.rem(q, self.slots)

                def arrival(where, device):
                    send_to(
                        self.fetch.at[slot, c],
                        self.zin.at[at, where],
                        self.zsend_sem.at[slot, c],
                        self.zin_sem.at[at, where],
                        device,
                    ).wait_recv()
                    acc[...] += self.zin[at, where].astype(f32)

                self.fetching(i, c).wait()
                acc[...] = self.fetch[slot, c].astype(f32)

                @pl.when(kind == 2)
                def _():
                    self.yfetching(i, c).wait()
                    acc[...] += self.yfetch[yslot, c].astype(f32)

                @pl.when(jnp.logical_and(c >= a, a > 0))
                def _():
                    arrival(c + 1, self.place.down)

                @pl.when(jnp.logical_and(c <= a, a < line - 1))
                def _():
                    arrival(c, self.place.up)

                @pl.when(c != a)
                def _():
                    self.fetch[slot, c] = acc[...].astype(bf16)

                    @pl.when(c > a)
                    def _():
                        self.onward(i, c, True).start()

                    @pl.when(c < a)
                    def _():
                        self.onward(i, c, False).start()

                @pl.when(c == a)
                def _():
                    _, older = self.item(q - 2)

                    @pl.when(jnp.logical_and(q >= 2, older == 2))
                    def _():
                        self.storing(q - 2).wait()

                    @pl.when(kind == 0)
                    def _():
                        self.swap_out[group] = acc[...].astype(bf16)
                        self.swapping(group).start()

                    @pl.when(kind == 1)
                    def _():
                        self.swap_sum[group] = acc[...]

                    @pl.when(kind == 2)
                    def _():
                        self.final[lax.rem(q, 2)] = acc[...]
                        self.storing(q).start()

    def pump(self, low, high):
        @pl.loop(low, high)
        def _(i):
            self.begin(i)
            self.complete(i)

    def finish(self):
        def summed(group):
            return pltpu.make_async_copy(
                self.swap_sum.at[group], self.place_of(self.early_tile(group)), self.sum_sem.at[group]
            )

        @pl.loop(0, self.swaps)
        def _(group):
            self.swapping(group).wait_recv()
            self.swap_sum[group] += self.swap_in[group].astype(f32)
            summed(group).start()

        for n in range(self.held):
            self.drain(self.steps - 1 - n)
        for q in (self.items - 2, self.items - 1):
            assert q >= 2 * self.EARLY
            self.storing(q).wait()

        @pl.loop(0, self.swaps)
        def _(group):
            self.swapping(group).wait_send()
            summed(group).wait()

        @pl.loop(0, self.n)
        def _(k):
            @pl.when(self.halved(k))
            def _():
                self.halve(k).wait_send()


class Sum:
    def __init__(self, place, which, term, inbox, across, sems):
        self.place, self.which, self.term, self.inbox, self.across, self.sems = place, which, term, inbox, across, sems
        self.half = inbox.shape[1]

    def own(self, m):
        return rows_at((2 * m + self.place.h) * self.half, self.half)

    def other(self, m):
        return rows_at((2 * m + 1 - self.place.h) * self.half, self.half)

    def first(self, m):
        return send_to(
            self.term.at[self.other(m)], self.inbox.at[m], self.sems.at[self.which, m, 0], self.sems.at[self.which, m, 1],
            self.place.core,
        )

    def second(self, m):
        return send_to(
            self.term.at[self.own(m)], self.across.at[m], self.sems.at[self.which, m, 2], self.sems.at[self.which, m, 3],
            self.place.across,
        )

    def start(self, m):
        self.first(m).start()

    def relay(self, m):
        self.first(m).wait_recv()
        base = (2 * m + self.place.h) * self.half

        @pl.loop(0, self.half // BLOCK)
        def _(r):
            at = rows_at(base + r * BLOCK, BLOCK)
            took = self.inbox[m, rows_at(r * BLOCK, BLOCK), :].astype(f32)
            self.term[at, :] = (self.term[at, :].astype(f32) + took).astype(bf16)

        self.second(m).start()

    def ready(self, m):
        self.second(m).wait_recv()

    def total(self, m, r):
        at = rows_at((2 * m + self.place.h) * self.half + r * BLOCK, BLOCK)
        return self.term[at, :].astype(f32) + self.across[m, rows_at(r * BLOCK, BLOCK), :].astype(f32)

    def settle(self, m):
        self.first(m).wait_send()
        self.second(m).wait_send()

    def spread(self, m, buffer):
        at = self.own(m)
        return send_to(
            buffer.at[at], buffer.at[at], self.sems.at[self.which, m, 4], self.sems.at[self.which, m, 5], self.place.core
        )

    def publish(self, m, staged, out):
        target = out.at[rows_at((2 * m + self.place.h) * self.half, self.half)]
        return (
            pltpu.make_async_copy(staged.at[m], target, self.sems.at[self.which, m, 6]),
            send_to(
                staged.at[m], target, self.sems.at[self.which, m, 4], self.sems.at[self.which, m, 5],
                self.place.core,
            ),
        )


def gain_row(gain):
    return gain[...].reshape(1, gain.shape[0])


def normal(values):
    scale = lax.rsqrt(jnp.mean(values * values, axis=-1, keepdims=True) + EPSILON)
    return scale, values * scale


def fold(values):
    return jnp.sum(values.reshape(values.shape[0] // 8, 8, values.shape[1]), axis=0)


def kernel(line, rows, n_ffn, names, *refs):
    v = dict(zip(names, refs))
    (lengths, order, mask, mix_gain, ffn_gain, taps_in) = (
        v[n] for n in ("lengths", "order", "mask", "mix_gain", "ffn_gain", "taps")
    )
    place = Place(line)
    n1, n2, g, term0, term1, r1h = (v[n] for n in ("n1", "n2", "g", "term0", "term1", "r1h"))
    inbox0, inbox1, across0, across1, across2 = (v[n] for n in ("inbox0", "inbox1", "across0", "across1", "across2"))
    pb, pc, px, po = (v[n] for n in ("pb", "pc", "px", "po"))
    bs, cs, xs, bx, ym, cat = (v[n] for n in ("bs", "cs", "xs", "bx", "ym", "cat"))
    sums, load = v["sums"], v["load"]
    tokens, width = n1.shape
    local = tokens // MICRO
    spans = local // SPAN
    pieces = MICRO * spans
    half = SPAN // 2
    chan = bs.shape[1]
    units = v["w_down"].shape[0]
    full = units // TILE
    rest = units - full * TILE
    docs = lengths.shape[1]
    rs = Scatter(
        place, 3 * n_ffn + 6, 3 * n_ffn, rows, v["wbuf"], v["ybuf"], v["grads"],
        [v[n] for n in Scatter.NAMES],
    )
    branch = Sum(place, 0, term0, inbox0, across0, sums)
    second = Sum(place, 1, term1, inbox1, across1, sums)
    feed = Sum(place, 2, term0, inbox0, across2, sums)
    first = Sum(place, 3, term0, inbox1, across0, sums)

    barrier = pltpu.get_barrier_semaphore()
    for device in (place.pair, place.next, place.last, place.core, place.across):
        pl.semaphore_signal(barrier, inc=1, device_id=device, device_id_type=MESH)

    @pl.loop(0, line)
    def _(c):
        @pl.when(c != place.a)
        def _():
            pl.semaphore_signal(barrier, inc=1, device_id=(c * 2 + place.b, place.t), device_id_type=MESH)

    def loading(which, src, dst):
        return pltpu.make_async_copy(src, dst, load.at[which])

    projections = [
        loading(2, v["proj_b"], pb),
        loading(3, v["proj_x"], px),
        loading(4, v["proj_c"], pc),
        loading(5, v["proj_out"], po),
    ]
    cot_load = [loading(6 + m, v["cotangent"].at[m], g.at[m * local : (m + 1) * local]) for m in range(MICRO)]
    wgu, wdb = v["wgu"], v["wdb"]

    def weights(j, slot):
        at = pl.ds(pl.multiple_of(j * TILE, TILE), TILE)
        return [
            pltpu.make_async_copy(v[src].at[at], dst, v["wsem"].at[slot, q])
            for q, (src, dst) in enumerate(
                (("w_gate", wgu.at[slot, 0:TILE]), ("w_up", wgu.at[slot, TILE:]), ("w_down", wdb.at[slot]))
            )
        ]

    def rest_weights():
        slot = full % 2
        return [
            pltpu.make_async_copy(v[src].at[full * TILE :], dst, v["wsem"].at[slot, q])
            for q, (src, dst) in enumerate(
                (
                    ("w_gate", wgu.at[slot, 0:rest]),
                    ("w_up", wgu.at[slot, TILE : TILE + rest]),
                    ("w_down", wdb.at[slot, 0:rest]),
                )
            )
        ]

    taps = taps_in[...].astype(f32)
    row_ids = lax.broadcasted_iota(jnp.int32, (SPAN, 1), 0)
    tap = [taps[k : k + 1, :] for k in range(3)]

    def span_facts(m, q):
        mine = order[m, place.s * spans + q]
        position = mine * SPAN + row_ids
        near = position >= 0
        far = position >= 0
        begin = jnp.int32(0)
        for n in range(docs):
            near = jnp.logical_and(near, position != begin)
            far = jnp.logical_and(far, position != begin + 1)
            begin = begin + lengths[m, n]
        return mine, near, jnp.logical_and(near, far)

    def terms(m, q, near, far, mine):
        here = bx[pl.ds(m * local + q * SPAN, SPAN), :].astype(f32)
        older = jnp.zeros((1, chan), f32)
        newer = jnp.zeros((1, chan), f32)
        for k in range(spans):
            took = order[m, place.before * spans + k] == mine - 1
            tail = v["halo_in"][m, k].astype(f32)
            older = older + jnp.where(took, tail[14:15], 0.0)
            newer = newer + jnp.where(took, tail[15:16], 0.0)
        far_term = pltpu.roll(here, 2, 0)
        far_term = jnp.where(row_ids == 0, older, jnp.where(row_ids == 1, newer, far_term))
        near_term = jnp.where(row_ids == 0, newer, pltpu.roll(here, 1, 0))
        return jnp.where(far, far_term, 0.0), jnp.where(near, near_term, 0.0), here

    def halo(m):
        return send_to(
            v["halo_out"].at[m], v["halo_in"].at[m], v["hsem"].at[0, m], v["hsem"].at[1, m], place.next
        )

    def halo_back(m):
        return send_to(
            v["back_out"].at[m], v["back_in"].at[m], v["hsem"].at[2, m], v["hsem"].at[3, m], place.last
        )

    def mixer_half(m, x):
        base = m * local

        @pl.loop(0, local // BLOCK)
        def _(r):
            at = rows_at(base + r * BLOCK, BLOCK)
            _, unit = normal(x[at, :].astype(f32))
            n1[at, :] = (unit * gain_row(mix_gain)).astype(bf16)

        at = pl.ds(base, local)
        if m == 0:
            projections[0].wait()
        bs[at, :] = dot_nn(n1[at, :], pb[...])
        if m == 0:
            projections[1].wait()
        xs[at, :] = dot_nn(n1[at, :], px[...])
        for q in range(spans):
            rows_q = pl.ds(base + q * SPAN, SPAN)
            product = (bs[rows_q, :] * xs[rows_q, :]).astype(bf16)
            bx[rows_q, :] = product
            v["halo_out"][m, q] = product[SPAN - 16 :, :]

    def mixer_rest(m):
        base = m * local
        at = pl.ds(base, local)
        if m == 0:
            projections[2].wait()
        cs[at, :] = dot_nn(n1[at, :], pc[...])
        halo(m).wait_recv()
        for q in range(spans):
            rows_q = pl.ds(base + q * SPAN, SPAN)
            mine, near, far = span_facts(m, q)
            far_term, near_term, here = terms(m, q, near, far, mine)
            conv = tap[0] * far_term + tap[1] * near_term + tap[2] * here
            ym[rows_q, :] = (cs[rows_q, :] * conv).astype(bf16)
            if m == 0 and q == 0:
                projections[3].wait()
            term0[rows_q, :] = dot_nn(ym[rows_q, :], po[...]).astype(bf16)
            piece = m * spans + q
            branch.start(piece)
            if piece > 0:
                branch.relay(piece - 1)

    def middle(p, x):
        branch.ready(p)

        @pl.loop(0, half // BLOCK)
        def _(r):
            at = rows_at((2 * p + place.h) * half + r * BLOCK, BLOCK)
            value = x[at, :].astype(f32) + branch.total(p, r)
            r1h[rows_at(p * half + r * BLOCK, BLOCK), :] = value
            _, unit = normal(value)
            n2[at, :] = (unit * gain_row(ffn_gain)).astype(bf16)

        branch.spread(p, n2).start()

    def masked(m):
        cot_load[m].wait()
        for q in range(spans):
            kept = mask[m : m + 1, q * SPAN : (q + 1) * SPAN].astype(f32)
            kept = jnp.transpose(jnp.broadcast_to(kept, (SPAN, SPAN)))
            rows_q = pl.ds(m * local + q * SPAN, SPAN)
            for c in range(width // SPAN):
                cols = pl.ds(c * SPAN, SPAN)
                g[rows_q, cols] = (g[rows_q, cols].astype(f32) * kept).astype(bf16)

    def mixer_forward(x):
        x_load = [loading(m, v["tokens"].at[m], x.at[m * local : (m + 1) * local]) for m in range(MICRO)]
        for copy in [x_load[0]] + projections[:2] + [x_load[1]] + projections[2:] + cot_load + weights(0, 0):
            copy.start()
        x_load[0].wait()
        mixer_half(0, x)
        pl.semaphore_wait(barrier, 5 + line - 1)
        halo(0).start()
        x_load[1].wait()
        mixer_rest(0)
        mixer_half(1, x)
        halo(1).start()
        mixer_rest(1)
        masked(0)
        branch.relay(pieces - 1)
        masked(1)
        for p in range(pieces):
            middle(p, x)
        for p in range(pieces):
            branch.spread(p, n2).wait()
            branch.settle(p)

    pl.run_scoped(mixer_forward, pltpu.VMEM((tokens, width), bf16))

    early = n_ffn - 1

    def feed_forward(oacc, dacc, hb, dgu):
        oacc[...] = jnp.zeros_like(oacc)
        dacc[...] = jnp.zeros_like(dacc)

        @pl.loop(0, n_ffn)
        def _(j):
            slot = lax.rem(j, 2)

            @pl.when(j < full)
            def _():
                for copy in weights(jnp.minimum(j, full - 1), slot):
                    copy.wait()

            if rest:

                @pl.when(j == full)
                def _():
                    for copy in rest_weights():
                        copy.wait()

            @pl.when(j + 1 < full)
            def _():
                for copy in weights(jnp.minimum(j + 1, full - 1), 1 - slot):
                    copy.start()

            if rest:

                @pl.when(j + 1 == full)
                def _():
                    blank = jnp.zeros((TILE - rest, width), bf16)
                    wgu[full % 2, rest:TILE, :] = blank
                    wgu[full % 2, TILE + rest :, :] = blank
                    wdb[full % 2, rest:, :] = blank
                    for copy in rest_weights():
                        copy.start()

            step = jnp.maximum(j - 1, 0)
            one = jnp.logical_and(j >= 1, j <= early)

            @pl.when(one)
            def _():
                rs.begin(step)

            for m in range(MICRO):
                at = slice(m * local, (m + 1) * local)
                both = dot_nt(n2[at, :], wgu[slot])
                back = dot_nt(g[at, :], wdb[slot])
                gate, up = both[:, :TILE], both[:, TILE:]
                sigma = jax.nn.sigmoid(gate)
                silu = gate * sigma
                hb[at, :] = (silu * up).astype(bf16)
                dgu[at, :TILE] = (back * up * sigma * (1.0 + gate * (1.0 - sigma))).astype(bf16)
                dgu[at, TILE:] = (back * silu).astype(bf16)

            @pl.when(one)
            def _():
                rs.complete(step)

            rs.produce(3 * j, [(0, g, lambda: hb[...])])
            oacc[...] += dot_nn(hb[...], wdb[slot])

            rs.produce(3 * j + 1, [(0, n2, lambda: dgu[:, :TILE])])
            rs.start_halving(j)
            dacc[...] += dot_nn(dgu[...], wgu[slot])
            rs.produce(3 * j + 2, [(0, n2, lambda: dgu[:, TILE:])])

        rs.flush(3 * n_ffn - 1)
        for p in range(pieces):
            at = pl.ds(p * SPAN, SPAN)
            term1[at, :] = dacc[at, :].astype(bf16)
            second.start(p)
            if p > 1:
                second.relay(p - 2)
        for p in range(pieces):
            at = pl.ds(p * SPAN, SPAN)
            term0[at, :] = oacc[at, :].astype(bf16)
            feed.start(p)
            if p < 2:
                second.relay(pieces - 2 + p)

    pl.run_scoped(
        feed_forward,
        pltpu.VMEM((tokens, width), f32),
        pltpu.VMEM((tokens, width), f32),
        pltpu.VMEM((tokens, TILE), bf16),
        pltpu.VMEM((tokens, 2 * TILE), bf16),
    )
    taken = [early]

    def pump(count):
        rs.pump(taken[0], taken[0] + count)
        taken[0] += count

    def backward(dr1, xh, dym, dbx, gain_one, gain_two, tap_rows):
        x_load = [
            loading(
                8 + p,
                v["tokens"].at[p // spans, rows_at(p % spans * SPAN + place.h * half, half)],
                xh.at[p * half : (p + 1) * half],
            )
            for p in range(pieces)
        ]
        for copy in x_load:
            copy.start()
        gain_one[...] = jnp.zeros_like(gain_one)
        gain_two[...] = jnp.zeros_like(gain_two)
        pump(2)
        for p in range(pieces):
            feed.relay(p)
        pump(1)

        for p in range(pieces):
            second.ready(p)

            @pl.loop(0, half // BLOCK)
            def _(r):
                at = rows_at((2 * p + place.h) * half + r * BLOCK, BLOCK)
                here = rows_at(p * half + r * BLOCK, BLOCK)
                grad = second.total(p, r)
                scale, unit = normal(r1h[here, :])
                gain_two[...] += fold(grad * unit)
                weighted = grad * gain_row(ffn_gain)
                inner = jnp.mean(weighted * unit, axis=-1, keepdims=True)
                value = g[at, :].astype(f32) + scale * (weighted - unit * inner)
                dr1[here, :] = value
                n2[at, :] = value.astype(bf16)

            second.spread(p, n2).start()
            if p == 2:
                pump(2)

        for p in range(pieces):
            second.spread(p, n2).wait()
            second.settle(p)
        dym[...] = dot_nt(n2[...], po[...])
        tap_sums = [jnp.zeros((8, chan), f32) for _ in range(3)]
        for m in range(MICRO):
            for q in range(spans):
                rows_q = pl.ds(m * local + q * SPAN, SPAN)
                mine, near, far = span_facts(m, q)
                far_term, near_term, here = terms(m, q, near, far, mine)
                grad = dym[rows_q, :]
                cat[rows_q, chan : 2 * chan] = (
                    grad * (tap[0] * far_term + tap[1] * near_term + tap[2] * here)
                ).astype(bf16)
                grad = grad * cs[rows_q, :]
                for k, other in enumerate((far_term, near_term, here)):
                    tap_sums[k] = tap_sums[k] + fold(grad * other)
                old = jnp.where(far, tap[0] * grad, 0.0)
                mid = jnp.where(near, tap[1] * grad, 0.0)
                dbx[rows_q, :] = (
                    tap[2] * grad
                    + jnp.where(row_ids < SPAN - 1, pltpu.roll(mid, SPAN - 1, 0), 0.0)
                    + jnp.where(row_ids < SPAN - 2, pltpu.roll(old, SPAN - 2, 0), 0.0)
                )
                top_ids = row_ids[:8]
                v["back_out"][m, q] = jnp.where(top_ids < 2, old[:8], 0.0) + jnp.where(
                    top_ids == 1, mid[0:1], 0.0
                )
            halo_back(m).start()
        pump(2)
        for k in range(3):
            tap_rows[k] = tap_sums[k]
        for m in range(MICRO):
            halo_back(m).wait_recv()
            for q in range(spans):
                rows_q = pl.ds(m * local + q * SPAN, SPAN)
                mine = order[m, place.s * spans + q]
                from_next = jnp.zeros((8, chan), f32)
                for k in range(spans):
                    took = order[m, place.after * spans + k] == mine + 1
                    from_next = from_next + jnp.where(took, v["back_in"][m, k], 0.0)
                value = dbx[rows_q, :]
                value = (
                    value
                    + jnp.where(row_ids == SPAN - 2, from_next[0:1], 0.0)
                    + jnp.where(row_ids == SPAN - 1, from_next[1:2], 0.0)
                )
                cat[rows_q, 0:chan] = (value * xs[rows_q, :]).astype(bf16)
                cat[rows_q, 2 * chan :] = (value * bs[rows_q, :]).astype(bf16)
        k0 = 3 * n_ffn
        wide = 3 * chan
        whole = wide // TILE
        for k in range(whole):
            rs.produce(k0 + k, [(0, n1, lambda k=k: cat[:, k * TILE : (k + 1) * TILE])])
            if k % 2 == 1:
                pump(1)
        left = wide - whole * TILE
        rs.produce(
            k0 + whole,
            [
                (0, n1, lambda: cat[:, whole * TILE :]),
                (left, n2, lambda: ym[:, 0 : TILE - left]),
            ],
        )
        rs.produce(k0 + whole + 1, [(0, n2, lambda: ym[:, TILE - left :])])
        rs.flush(k0 + whole + 1)
        assert taken[0] < rs.AHEAD + 13
        pump(1)

        for p in range(pieces):
            feed.ready(p)

            @pl.loop(0, half // BLOCK)
            def _(r):
                here = rows_at(p * half + r * BLOCK, BLOCK)
                at = rows_at(r * BLOCK, BLOCK)
                across2[p, at, :] = (r1h[here, :] + feed.total(p, r)).astype(bf16)

            for copy in feed.publish(p, across2, v["block_out"]):
                copy.start()
            feed.settle(p)
        pump(1)
        for m in range(MICRO):
            at = pl.ds(m * local, local)
            term0[at, :] = (
                dot_nt(cat[at, 0:chan], pb[...])
                + dot_nt(cat[at, chan : 2 * chan], pc[...])
                + dot_nt(cat[at, 2 * chan :], px[...])
            ).astype(bf16)
            for p in range(m * spans, (m + 1) * spans):
                first.start(p)
        for p in range(pieces):
            first.relay(p)
        pump(2)
        for p in range(pieces):
            x_load[p].wait()
            first.ready(p)

            @pl.loop(0, half // BLOCK)
            def _(r):
                here = rows_at(p * half + r * BLOCK, BLOCK)
                at = rows_at(r * BLOCK, BLOCK)
                grad = first.total(p, r)
                scale, unit = normal(xh[here, :].astype(f32))
                gain_one[...] += fold(grad * unit)
                weighted = grad * gain_row(mix_gain)
                inner = jnp.mean(weighted * unit, axis=-1, keepdims=True)
                across0[p, at, :] = (dr1[here, :] + scale * (weighted - unit * inner)).astype(bf16)

            for copy in first.publish(p, across0, v["d_tokens"]):
                copy.start()
            if p % 2 == 1:
                pump(1)

        small, gather = v["small"], v["gather"]
        ssem = v["ssem"]
        side = width // 2
        small[0] = jnp.zeros((8, side), f32)
        for n, gain in enumerate((gain_one, gain_two)):
            row = jnp.sum(gain[...], axis=0, keepdims=True)
            small[0, 2 * n : 2 * n + 1, :] = row[:, :side]
            small[0, 2 * n + 1 : 2 * n + 2, :] = row[:, side:]
        for k in range(3):
            at = k % 2 * chan
            small[0, 4 + k // 2 : 5 + k // 2, at : at + chan] = jnp.sum(tap_rows[k], axis=0, keepdims=True)
        core = send_to(small.at[0], gather.at[0], ssem.at[0], ssem.at[1], place.core)
        core.start()
        pump(1)
        core.wait_recv()
        small[1] = small[0] + jnp.where(lax.broadcasted_iota(jnp.int32, (8, 1), 0) < 4, gather[0], 0.0)
        pair = send_to(small.at[1], gather.at[1], ssem.at[2], ssem.at[3], place.pair)
        pair.start()
        pump(3)
        pair.wait_recv()
        small[2] = small[1] + gather[1]

        def along(c, slot):
            return send_to(
                small.at[2], gather.at[2 + slot], ssem.at[4 + c], ssem.at[4 + line + slot], (c * 2 + place.b, place.t)
            )

        @pl.loop(0, line)
        def _(c):
            @pl.when(c != place.a)
            def _():
                along(c, place.a).start()

        gather[2 + place.a] = small[2]

        rs.pump(taken[0], rs.steps)

        @pl.loop(0, line)
        def _(c):
            @pl.when(c != place.a)
            def _():
                along(c, c).wait_recv()
                along(c, place.a).wait_send()

        total = gather[2]
        for c in range(1, line):
            total = total + gather[2 + c]
        v["small_out"][...] = total
        core.wait_send()
        pair.wait_send()
        for m in range(MICRO):
            halo(m).wait_send()
            halo_back(m).wait_send()
        for m in range(pieces):
            first.settle(m)
            for each, staged, out in ((feed, across2, v["block_out"]), (first, across0, v["d_tokens"])):
                for copy in each.publish(m, staged, out):
                    copy.wait()
        rs.finish()

    pl.run_scoped(
        backward,
        pltpu.VMEM((tokens // 2, width), f32),
        pltpu.VMEM((tokens // 2, width), bf16),
        pltpu.VMEM((tokens, chan), f32),
        pltpu.VMEM((tokens, chan), f32),
        pltpu.VMEM((8, width), f32),
        pltpu.VMEM((8, width), f32),
        pltpu.VMEM((3, 8, chan), f32),
    )


def body(
    seq_count,
    tokens,
    mix_gain,
    proj_b,
    proj_c,
    proj_x,
    conv_taps,
    proj_out,
    ffn_gain,
    w_gate,
    w_up,
    w_down,
    cotangent,
    seq_lengths,
    span_order,
    keep_mask,
):
    local, width = tokens.shape[1:]
    total = MICRO * local
    half = SPAN // 2
    chan = proj_b.shape[1]
    units = w_gate.shape[1]
    n_ffn = pl.cdiv(units, TILE)
    line = seq_count // 2
    rows = width // seq_count
    n_tiles = 3 * n_ffn + 6
    spans = local // SPAN
    pieces = MICRO * spans
    dma = pltpu.SemaphoreType.DMA
    vmem = pl.BlockSpec(memory_space=pltpu.VMEM)
    smem = pl.BlockSpec(memory_space=pltpu.SMEM)
    hbm = pl.BlockSpec(memory_space=pl.ANY)
    shape = jax.ShapeDtypeStruct
    inputs = [
        ("lengths", seq_lengths, smem),
        ("order", span_order, smem),
        ("mask", keep_mask, vmem),
        ("mix_gain", mix_gain, vmem),
        ("ffn_gain", ffn_gain, vmem),
        ("taps", conv_taps, vmem),
        ("tokens", tokens, hbm),
        ("cotangent", cotangent, hbm),
        ("proj_b", proj_b, hbm),
        ("proj_c", proj_c, hbm),
        ("proj_x", proj_x, hbm),
        ("proj_out", proj_out, hbm),
        ("w_gate", w_gate.T, hbm),
        ("w_up", w_up.T, hbm),
        ("w_down", w_down, hbm),
    ]
    outputs = [
        ("block_out", shape((total, width), bf16), hbm),
        ("d_tokens", shape((total, width), bf16), hbm),
        ("grads", shape((4, rows, n_ffn * TILE), f32), hbm),
        ("small_out", shape((8, width // 2), f32), vmem),
        ("wbuf", shape((n_tiles, 2, line, rows, TILE), bf16), hbm),
        ("ybuf", shape((n_tiles, line, rows, TILE), bf16), hbm),
    ]
    scratch = [
        ("n1", pltpu.VMEM((total, width), bf16)),
        ("n2", pltpu.VMEM((total, width), bf16)),
        ("g", pltpu.VMEM((total, width), bf16)),
        ("term0", pltpu.VMEM((total, width), bf16)),
        ("term1", pltpu.VMEM((total, width), bf16)),
        ("r1h", pltpu.VMEM((total // 2, width), f32)),
        ("inbox0", pltpu.VMEM((pieces, half, width), bf16)),
        ("inbox1", pltpu.VMEM((pieces, half, width), bf16)),
        ("across0", pltpu.VMEM((pieces, half, width), bf16)),
        ("across1", pltpu.VMEM((pieces, half, width), bf16)),
        ("across2", pltpu.VMEM((pieces, half, width), bf16)),
        ("pb", pltpu.VMEM((width, chan), bf16)),
        ("pc", pltpu.VMEM((width, chan), bf16)),
        ("px", pltpu.VMEM((width, chan), bf16)),
        ("po", pltpu.VMEM((chan, width), bf16)),
        ("bs", pltpu.VMEM((total, chan), f32)),
        ("cs", pltpu.VMEM((total, chan), f32)),
        ("xs", pltpu.VMEM((total, chan), f32)),
        ("bx", pltpu.VMEM((total, chan), bf16)),
        ("ym", pltpu.VMEM((total, chan), bf16)),
        ("cat", pltpu.VMEM((total, 3 * chan), bf16)),
        ("wgu", pltpu.VMEM((2, 2 * TILE, width), bf16)),
        ("wdb", pltpu.VMEM((2, TILE, width), bf16)),
        ("halo_out", pltpu.VMEM((MICRO, spans, 16, chan), bf16)),
        ("halo_in", pltpu.VMEM((MICRO, spans, 16, chan), bf16)),
        ("back_out", pltpu.VMEM((MICRO, spans, 8, chan), f32)),
        ("back_in", pltpu.VMEM((MICRO, spans, 8, chan), f32)),
        ("small", pltpu.VMEM((3, 8, width // 2), f32)),
        ("gather", pltpu.VMEM((2 + line, 8, width // 2), f32)),
        ("load", dma((8 + pieces,))),
        ("wsem", dma((2, 3))),
        ("sums", dma((4, pieces, 7))),
        ("hsem", dma((4, MICRO))),
        ("ssem", dma((4 + 2 * line,))),
    ]
    scratch += list(zip(Scatter.NAMES, Scatter.scratch(n_tiles, line, rows)))
    names = [n for n, _, _ in inputs] + [n for n, _, _ in outputs] + [n for n, _ in scratch]
    results = pl.pallas_call(
        functools.partial(kernel, line, rows, n_ffn, names),
        out_shape=tuple(s for _, s, _ in outputs),
        in_specs=[s for _, _, s in inputs],
        out_specs=tuple(s for _, _, s in outputs),
        scratch_shapes=[s for _, s in scratch],
        compiler_params=pltpu.CompilerParams(
            collective_id=0, has_side_effects=True, vmem_limit_bytes=62 * 2**20 - 2**19
        ),
    )(*[a for _, a, _ in inputs])
    done = finish_call(results[:4], total, width, chan, units, rows)
    return (
        done[0].reshape(tokens.shape),
        done[1].reshape(tokens.shape),
        done[2],
        done[3],
        done[4],
        done[5],
        done[6],
        done[7].T,
        done[8],
        done[9],
        done[10],
        done[11].T,
    )


def finish_kernel(
    block_in, tokens_in, grads, small, block_out, d_tokens, d_mixgain, d_b, d_c, d_x, d_taps, d_out, d_ffngain, d_gate, d_up, d_down
):
    chan, units = d_b.shape[1], d_gate.shape[1]
    side = small.shape[1]
    block_out[...] = block_in[...]
    d_tokens[...] = tokens_in[...]
    for n, out in enumerate((d_b, d_c, d_x, d_out)):
        out[...] = grads[3, :, n * chan : (n + 1) * chan]
    for n, out in enumerate((d_down, d_gate, d_up)):
        out[...] = grads[n, :, :units]

    @pl.when(pl.program_id(0) == 0)
    def _():
        for n, out in enumerate((d_mixgain, d_ffngain)):
            out[0:side] = small[2 * n : 2 * n + 1, :].reshape(side)
            out[side:] = small[2 * n + 1 : 2 * n + 2, :].reshape(side)
        for k in range(3):
            at = k % 2 * chan
            d_taps[k : k + 1, :] = small[4 + k // 2 : 5 + k // 2, at : at + chan]


def finish_call(arrays, tokens, width, chan, units, rows):
    cuts = 6
    shape = jax.ShapeDtypeStruct

    def by_rows(count, columns):
        return pl.BlockSpec((count // cuts, columns), lambda i: (i, 0))

    def whole(*sizes):
        return pl.BlockSpec(sizes, lambda i: (0,) * len(sizes))

    return pl.pallas_call(
        finish_kernel,
        grid=(cuts,),
        in_specs=[
            by_rows(tokens, width),
            by_rows(tokens, width),
            pl.BlockSpec((4, rows // cuts, arrays[2].shape[2]), lambda i: (0, i, 0)),
            whole(*arrays[3].shape),
        ],
        out_shape=(
            shape((tokens, width), bf16),
            shape((tokens, width), bf16),
            shape((width,), f32),
            shape((rows, chan), f32),
            shape((rows, chan), f32),
            shape((rows, chan), f32),
            shape((3, chan), f32),
            shape((rows, chan), f32),
            shape((width,), f32),
            shape((rows, units), f32),
            shape((rows, units), f32),
            shape((rows, units), f32),
        ),
        out_specs=(
            by_rows(tokens, width),
            by_rows(tokens, width),
            whole(width),
            by_rows(rows, chan),
            by_rows(rows, chan),
            by_rows(rows, chan),
            whole(3, chan),
            by_rows(rows, chan),
            whole(width),
            by_rows(rows, units),
            by_rows(rows, units),
            by_rows(rows, units),
        ),
    )(*arrays)


def solution(mesh):
    placed = (
        P(None, "seq", None),
        P(),
        P(None, "tp"),
        P(None, "tp"),
        P(None, "tp"),
        P(None, "tp"),
        P("tp", None),
        P(),
        P(None, "tp"),
        P(None, "tp"),
        P("tp", None),
        P(None, "seq", None),
        P(),
        P(),
        P(None, "seq"),
    )
    return jax.shard_map(
        functools.partial(body, mesh.shape["seq"]),
        mesh=mesh,
        in_specs=placed,
        out_specs=(
            P(None, "seq", None),
            P(None, "seq", None),
            P(),
            P("seq", "tp"),
            P("seq", "tp"),
            P("seq", "tp"),
            P(None, "tp"),
            P("tp", "seq"),
            P(),
            P("seq", "tp"),
            P("seq", "tp"),
            P("tp", "seq"),
        ),
        check_vma=False,
    )
```

```python
import functools
import jax
import jax.numpy as jnp
from jax import lax
from jax.experimental import pallas as pl
from jax.experimental.pallas import tpu as pltpu
from jax.sharding import PartitionSpec as P

SPAN = 128
MICRO = 2
EPSILON = 1e-05
MESH = pl.DeviceIdType.MESH
TILE = 256
BLOCK = 32
ROWS = 384
f32 = jnp.float32
bf16 = jnp.bfloat16


def dot_nn(a, b):
    return jnp.dot(a, b, preferred_element_type=f32)


def dot_nt(a, b):
    return lax.dot_general(a, b, (((1,), (1,)), ((), ())), preferred_element_type=f32)


def dot_tn(a, b):
    return lax.dot_general(a, b, (((0,), (0,)), ((), ())), preferred_element_type=f32)


def send_to(src, dst, send_sem, recv_sem, device):
    return pltpu.make_async_remote_copy(
        src_ref=src,
        dst_ref=dst,
        send_sem=send_sem,
        recv_sem=recv_sem,
        device_id=device,
        device_id_type=MESH,
    )


def rows_at(start, size):
    return pl.ds(pl.multiple_of(start, 16), size)


class Place:
    def __init__(self, line):
        self.line = line
        self.s = lax.axis_index("seq")
        self.t = lax.axis_index("tp")
        self.a = lax.div(self.s, 2)
        self.b = lax.rem(self.s, 2)
        self.h = lax.rem(self.t, 2)
        count = 2 * line
        self.pair = (self.a * 2 + 1 - self.b, self.t)
        self.up = (lax.rem(self.a + 1, line) * 2 + self.b, self.t)
        self.down = (lax.rem(self.a + line - 1, line) * 2 + self.b, self.t)
        self.after = lax.rem(self.s + 1, count)
        self.before = lax.rem(self.s + count - 1, count)
        self.next = (self.after, self.t)
        self.last = (self.before, self.t)
        self.core = (self.s, self.t + 1 - 2 * self.h)
        self.across = (self.s, lax.rem(self.t + 2, 4))


class Scatter:
    NAMES = (
        "stage", "zin", "fetch", "yfetch", "acc", "final", "swap_out", "swap_in", "swap_sum",
        "stage_sem", "ysend_sem", "yrecv_sem", "zsend_sem", "zin_sem", "fetch_sem", "yfetch_sem", "final_sem",
        "swap_sem", "sum_sem",
    )
    EARLY = 4
    AHEAD = 7

    def __init__(self, place, n_tiles, ffn_tiles, rows, wbuf, ybuf, out, scratch):
        self.place, self.a, self.b, self.line = place, place.a, place.b, place.line
        self.n, self.ffn_tiles, self.rows = n_tiles, ffn_tiles, rows
        self.wbuf, self.ybuf, self.out = wbuf, ybuf, out
        for name, ref in zip(self.NAMES, scratch):
            setattr(self, name, ref)
        self.slots = self.zin.shape[0]
        self.items = n_tiles + self.EARLY
        self.hop = self.hop_of(self.line)
        self.held = self.fetch.shape[0]
        self.steps = self.items + self.hop * (self.line - 1)
        self.swaps = self.swap_sum.shape[0]

    @staticmethod
    def hop_of(line):
        return 2 if line <= 4 else 1

    @classmethod
    def scratch(cls, n_tiles, line, rows):
        slots = cls.hop_of(line) * line + 1
        held = 2 * cls.hop_of(line)
        swaps = cls.EARLY
        dma = pltpu.SemaphoreType.DMA
        return [
            pltpu.VMEM((2, 2, line, rows, TILE), bf16),
            pltpu.VMEM((slots, line + 1, rows, TILE), bf16),
            pltpu.VMEM((held, line, rows, TILE), bf16),
            pltpu.VMEM((2, line, rows, TILE), bf16),
            pltpu.VMEM((rows, TILE), f32),
            pltpu.VMEM((2, rows, TILE), f32),
            pltpu.VMEM((swaps, rows, TILE), bf16),
            pltpu.VMEM((swaps, rows, TILE), bf16),
            pltpu.VMEM((swaps, rows, TILE), f32),
            dma((2, 2)),
            dma((n_tiles,)),
            dma((n_tiles,)),
            dma((held, line)),
            dma((slots, line + 1)),
            dma((held, line)),
            dma((2, line)),
            dma((2,)),
            dma((2, swaps)),
            dma((swaps,)),
        ]


    def local(self, k):
        slot = lax.rem(k, 2)
        return (
            pltpu.make_async_copy(self.stage.at[slot, 1 - self.b], self.wbuf.at[k, 0], self.stage_sem.at[slot, 0]),
            pltpu.make_async_copy(self.stage.at[slot, self.b], self.wbuf.at[k, 1], self.stage_sem.at[slot, 1]),
        )

    def halved(self, k):
        return jnp.logical_or(lax.rem(k, 3) == 0, k > self.early_tile(self.EARLY - 1))

    @staticmethod
    def early_tile(n):
        return n + 1 + n // 2 if isinstance(n, int) else n + 1 + lax.div(n, 2)

    def halve(self, k):
        return send_to(
            self.wbuf.at[k, 0], self.ybuf.at[k], self.ysend_sem.at[k], self.yrecv_sem.at[k], self.place.pair
        )

    def flush(self, k):
        for copy in self.local(k):
            copy.wait()

    def halved_tile(self, n):
        return jnp.where(n <= self.EARLY // 2, 3 * n, n + self.EARLY)

    def start_halving(self, n):
        self.halve(self.halved_tile(n)).start()

    def produce(self, k, parts, flushed=False):
        if not flushed:

            @pl.when(jnp.logical_and(k != 0, k != self.ffn_tiles))
            def _():
                self.flush(k - 1)

        slot = lax.rem(k, 2)
        for offset, left, right in parts:
            width = right().shape[1]
            for start in range(0, left.shape[1], ROWS):
                value = dot_tn(left[:, start : start + ROWS], right())
                for n in range(ROWS // self.rows):
                    c, half = divmod(start // self.rows + n, 2)
                    self.stage[slot, half, c, :, offset : offset + width] = value[
                        n * self.rows : (n + 1) * self.rows
                    ].astype(bf16)
        for copy in self.local(k):
            copy.start()


    def item_of(self, i, c):
        a, far = self.a, self.line - 1 - self.a
        return i - self.hop * jnp.where(c > a, a, jnp.where(c < a, far, jnp.maximum(a, far)))

    def inside(self, q):
        return jnp.logical_and(q >= 0, q < self.items)

    def item(self, q):
        q = jnp.clip(q, 0, self.items - 1)
        early = q < 2 * self.EARLY
        n = q - 2 * self.EARLY
        tile = self.halved_tile(n)
        return (
            jnp.where(early, self.early_tile(lax.div(q, 2)), tile),
            jnp.where(early, lax.rem(q, 2), 2),
        )

    def block(self, n):
        return jnp.where(n < self.a, n, self.line - 1 - (n - self.a))

    def fetching(self, i, c):
        slot = lax.rem(i, self.held)
        tile, kind = self.item(self.item_of(i, c))
        side = jnp.where(kind == 0, 0, 1)
        return pltpu.make_async_copy(
            self.wbuf.at[tile, side, c], self.fetch.at[slot, c], self.fetch_sem.at[slot, c]
        )

    def yfetching(self, i, c):
        slot = lax.rem(i, 2)
        tile, _ = self.item(self.item_of(i, c))
        return pltpu.make_async_copy(self.ybuf.at[tile, c], self.yfetch.at[slot, c], self.yfetch_sem.at[slot, c])

    def onward(self, i, c, upward):
        slot = lax.rem(i, self.held)
        at = lax.rem(jnp.clip(self.item_of(i, c), 0, self.items - 1), self.slots)
        where = c + 1 if upward else c
        return send_to(
            self.fetch.at[slot, c],
            self.zin.at[at, where],
            self.zsend_sem.at[slot, c],
            self.zin_sem.at[at, where],
            self.place.up if upward else self.place.down,
        )

    def drain(self, i):
        @pl.loop(0, self.line)
        def _(c):
            @pl.when(jnp.logical_and(self.inside(self.item_of(i, c)), c != self.a))
            def _():
                self.onward(i, c, False).wait_send()

    def storing(self, q):
        slot = lax.rem(q, 2)
        tile, _ = self.item(q)
        return pltpu.make_async_copy(self.final.at[slot], self.place_of(tile), self.final_sem.at[slot])

    def place_of(self, tile):
        is_ffn = tile < self.ffn_tiles
        kind = jnp.where(is_ffn, lax.rem(tile, 3), 3)
        column = jnp.where(is_ffn, lax.div(tile, 3), tile - self.ffn_tiles)
        return self.out.at[kind, :, pl.ds(pl.multiple_of(column * TILE, TILE), TILE)]

    def swapping(self, group):
        return send_to(
            self.swap_out.at[group], self.swap_in.at[group], self.swap_sem.at[0, group], self.swap_sem.at[1, group],
            self.place.pair,
        )

    def begin(self, i):
        @pl.when(i >= self.held)
        def _():
            self.drain(i - self.held)

        ahead = lax.div(3 * i, 4)
        fresh = jnp.logical_and(ahead > lax.div(3 * i - 3, 4), i >= self.AHEAD)

        @pl.when(jnp.logical_and(fresh, ahead + 2 < self.n - self.EARLY))
        def _():
            self.start_halving(ahead + 2)

        q = i - self.hop * jnp.minimum(self.a, self.line - 1 - self.a)
        tile, kind = self.item(q)

        @pl.when(jnp.logical_and(self.inside(q), kind == 2))
        def _():
            self.halve(tile).wait_recv()

        @pl.loop(0, self.line)
        def _(n):
            c = self.block(n)
            q = self.item_of(i, c)
            _, kind = self.item(q)

            @pl.when(self.inside(q))
            def _():
                self.fetching(i, c).start()

            @pl.when(jnp.logical_and(self.inside(q), kind == 2))
            def _():
                self.yfetching(i, c).start()

    def complete(self, i):
        line, a, acc = self.line, self.a, self.acc
        slot = lax.rem(i, self.held)
        yslot = lax.rem(i, 2)

        @pl.loop(0, line)
        def _(n):
            c = self.block(n)
            q = self.item_of(i, c)

            @pl.when(self.inside(q))
            def _():
                _, kind = self.item(q)
                group = jnp.minimum(lax.div(q, 2), self.EARLY - 1)
                at = lax.rem(q, self.slots)

                def arrival(where, device):
                    send_to(
                        self.fetch.at[slot, c],
                        self.zin.at[at, where],
                        self.zsend_sem.at[slot, c],
                        self.zin_sem.at[at, where],
                        device,
                    ).wait_recv()
                    acc[...] += self.zin[at, where].astype(f32)

                self.fetching(i, c).wait()
                acc[...] = self.fetch[slot, c].astype(f32)

                @pl.when(kind == 2)
                def _():
                    self.yfetching(i, c).wait()
                    acc[...] += self.yfetch[yslot, c].astype(f32)

                @pl.when(jnp.logical_and(c >= a, a > 0))
                def _():
                    arrival(c + 1, self.place.down)

                @pl.when(jnp.logical_and(c <= a, a < line - 1))
                def _():
                    arrival(c, self.place.up)

                @pl.when(c != a)
                def _():
                    self.fetch[slot, c] = acc[...].astype(bf16)

                    @pl.when(c > a)
                    def _():
                        self.onward(i, c, True).start()

                    @pl.when(c < a)
                    def _():
                        self.onward(i, c, False).start()

                @pl.when(c == a)
                def _():
                    _, older = self.item(q - 2)

                    @pl.when(jnp.logical_and(q >= 2, older == 2))
                    def _():
                        self.storing(q - 2).wait()

                    @pl.when(kind == 0)
                    def _():
                        self.swap_out[group] = acc[...].astype(bf16)
                        self.swapping(group).start()

                    @pl.when(kind == 1)
                    def _():
                        self.swap_sum[group] = acc[...]

                    @pl.when(kind == 2)
                    def _():
                        self.final[lax.rem(q, 2)] = acc[...]
                        self.storing(q).start()

    def pump(self, low, high):
        @pl.loop(low, high)
        def _(i):
            self.begin(i)
            self.complete(i)

    def finish(self):
        def summed(group):
            return pltpu.make_async_copy(
                self.swap_sum.at[group], self.place_of(self.early_tile(group)), self.sum_sem.at[group]
            )

        @pl.loop(0, self.swaps)
        def _(group):
            self.swapping(group).wait_recv()
            self.swap_sum[group] += self.swap_in[group].astype(f32)
            summed(group).start()

        for n in range(self.held):
            self.drain(self.steps - 1 - n)
        for q in (self.items - 2, self.items - 1):
            assert q >= 2 * self.EARLY
            self.storing(q).wait()

        @pl.loop(0, self.swaps)
        def _(group):
            self.swapping(group).wait_send()
            summed(group).wait()

        @pl.loop(0, self.n)
        def _(k):
            @pl.when(self.halved(k))
            def _():
                self.halve(k).wait_send()


class Sum:
    def __init__(self, place, which, term, inbox, across, sems):
        self.place, self.which, self.term, self.inbox, self.across, self.sems = place, which, term, inbox, across, sems
        self.half = inbox.shape[1]

    def own(self, m):
        return rows_at((2 * m + self.place.h) * self.half, self.half)

    def other(self, m):
        return rows_at((2 * m + 1 - self.place.h) * self.half, self.half)

    def first(self, m):
        return send_to(
            self.term.at[self.other(m)], self.inbox.at[m], self.sems.at[self.which, m, 0], self.sems.at[self.which, m, 1],
            self.place.core,
        )

    def second(self, m):
        return send_to(
            self.term.at[self.own(m)], self.across.at[m], self.sems.at[self.which, m, 2], self.sems.at[self.which, m, 3],
            self.place.across,
        )

    def start(self, m):
        self.first(m).start()

    def relay(self, m):
        self.first(m).wait_recv()
        base = (2 * m + self.place.h) * self.half

        @pl.loop(0, self.half // BLOCK)
        def _(r):
            at = rows_at(base + r * BLOCK, BLOCK)
            took = self.inbox[m, rows_at(r * BLOCK, BLOCK), :].astype(f32)
            self.term[at, :] = (self.term[at, :].astype(f32) + took).astype(bf16)

        self.second(m).start()

    def ready(self, m):
        self.second(m).wait_recv()

    def total(self, m, r):
        at = rows_at((2 * m + self.place.h) * self.half + r * BLOCK, BLOCK)
        return self.term[at, :].astype(f32) + self.across[m, rows_at(r * BLOCK, BLOCK), :].astype(f32)

    def settle(self, m):
        self.first(m).wait_send()
        self.second(m).wait_send()

    def spread(self, m, buffer):
        at = self.own(m)
        return send_to(
            buffer.at[at], buffer.at[at], self.sems.at[self.which, m, 4], self.sems.at[self.which, m, 5], self.place.core
        )

    def publish(self, m, staged, out):
        target = out.at[rows_at((2 * m + self.place.h) * self.half, self.half)]
        return (
            pltpu.make_async_copy(staged.at[m], target, self.sems.at[self.which, m, 6]),
            send_to(
                staged.at[m], target, self.sems.at[self.which, m, 4], self.sems.at[self.which, m, 5],
                self.place.core,
            ),
        )


def gain_row(gain):
    return gain[...].reshape(1, gain.shape[0])


def normal(values):
    scale = lax.rsqrt(jnp.mean(values * values, axis=-1, keepdims=True) + EPSILON)
    return scale, values * scale


def fold(values):
    return jnp.sum(values.reshape(values.shape[0] // 8, 8, values.shape[1]), axis=0)


def kernel(line, rows, n_ffn, names, *refs):
    v = dict(zip(names, refs))
    (lengths, order, mask, mix_gain, ffn_gain, taps_in) = (
        v[n] for n in ("lengths", "order", "mask", "mix_gain", "ffn_gain", "taps")
    )
    place = Place(line)
    n1, n2, g, term0, term1, r1h = (v[n] for n in ("n1", "n2", "g", "term0", "term1", "r1h"))
    inbox0, inbox1, across0, across1, across2 = (v[n] for n in ("inbox0", "inbox1", "across0", "across1", "across2"))
    pb, pc, px, po = (v[n] for n in ("pb", "pc", "px", "po"))
    bs, cs, xs, bx, ym, cat = (v[n] for n in ("bs", "cs", "xs", "bx", "ym", "cat"))
    hb, dgu = v["hb"], v["dgu"]
    sums, load = v["sums"], v["load"]
    tokens, width = n1.shape
    local = tokens // MICRO
    spans = local // SPAN
    pieces = MICRO * spans
    half = SPAN // 2
    chan = bs.shape[1]
    units = v["w_down"].shape[0]
    full = units // TILE
    rest = units - full * TILE
    docs = lengths.shape[1]
    rs = Scatter(
        place, 3 * n_ffn + 6, 3 * n_ffn, rows, v["wbuf"], v["ybuf"], v["grads"],
        [v[n] for n in Scatter.NAMES],
    )
    branch = Sum(place, 0, term0, inbox0, across0, sums)
    second = Sum(place, 1, term1, inbox1, across1, sums)
    feed = Sum(place, 2, term0, inbox0, across2, sums)
    first = Sum(place, 3, term0, inbox1, across0, sums)

    barrier = pltpu.get_barrier_semaphore()
    for device in (place.pair, place.next, place.last, place.core, place.across):
        pl.semaphore_signal(barrier, inc=1, device_id=device, device_id_type=MESH)

    @pl.loop(0, line)
    def _(c):
        @pl.when(c != place.a)
        def _():
            pl.semaphore_signal(barrier, inc=1, device_id=(c * 2 + place.b, place.t), device_id_type=MESH)

    def loading(which, src, dst):
        return pltpu.make_async_copy(src, dst, load.at[which])

    projections = [
        loading(2, v["proj_b"], pb),
        loading(3, v["proj_x"], px),
        loading(4, v["proj_c"], pc),
        loading(5, v["proj_out"], po),
    ]
    cot_load = [loading(6 + m, v["cotangent"].at[m], g.at[m * local : (m + 1) * local]) for m in range(MICRO)]
    wgu, wdb = v["wgu"], v["wdb"]

    def weights(j, slot):
        at = pl.ds(pl.multiple_of(j * TILE, TILE), TILE)
        return [
            pltpu.make_async_copy(v[src].at[at], dst, v["wsem"].at[slot, q])
            for q, (src, dst) in enumerate(
                (("w_gate", wgu.at[slot, 0:TILE]), ("w_up", wgu.at[slot, TILE:]), ("w_down", wdb.at[slot]))
            )
        ]

    def rest_weights():
        slot = full % 2
        return [
            pltpu.make_async_copy(v[src].at[full * TILE :], dst, v["wsem"].at[slot, q])
            for q, (src, dst) in enumerate(
                (
                    ("w_gate", wgu.at[slot, 0:rest]),
                    ("w_up", wgu.at[slot, TILE : TILE + rest]),
                    ("w_down", wdb.at[slot, 0:rest]),
                )
            )
        ]

    taps = taps_in[...].astype(f32)
    row_ids = lax.broadcasted_iota(jnp.int32, (SPAN, 1), 0)
    tap = [taps[k : k + 1, :] for k in range(3)]

    def span_facts(m, q):
        mine = order[m, place.s * spans + q]
        position = mine * SPAN + row_ids
        near = position >= 0
        far = position >= 0
        begin = jnp.int32(0)
        for n in range(docs):
            near = jnp.logical_and(near, position != begin)
            far = jnp.logical_and(far, position != begin + 1)
            begin = begin + lengths[m, n]
        return mine, near, jnp.logical_and(near, far)

    def terms(m, q, near, far, mine):
        here = bx[pl.ds(m * local + q * SPAN, SPAN), :].astype(f32)
        older = jnp.zeros((1, chan), f32)
        newer = jnp.zeros((1, chan), f32)
        for k in range(spans):
            took = order[m, place.before * spans + k] == mine - 1
            tail = v["halo_in"][m, k].astype(f32)
            older = older + jnp.where(took, tail[14:15], 0.0)
            newer = newer + jnp.where(took, tail[15:16], 0.0)
        far_term = pltpu.roll(here, 2, 0)
        far_term = jnp.where(row_ids == 0, older, jnp.where(row_ids == 1, newer, far_term))
        near_term = jnp.where(row_ids == 0, newer, pltpu.roll(here, 1, 0))
        return jnp.where(far, far_term, 0.0), jnp.where(near, near_term, 0.0), here

    def halo(m):
        return send_to(
            v["halo_out"].at[m], v["halo_in"].at[m], v["hsem"].at[0, m], v["hsem"].at[1, m], place.next
        )

    def halo_back(m):
        return send_to(
            v["back_out"].at[m], v["back_in"].at[m], v["hsem"].at[2, m], v["hsem"].at[3, m], place.last
        )

    def mixer_half(m, x):
        base = m * local

        @pl.loop(0, local // BLOCK)
        def _(r):
            at = rows_at(base + r * BLOCK, BLOCK)
            _, unit = normal(x[at, :].astype(f32))
            n1[at, :] = (unit * gain_row(mix_gain)).astype(bf16)

        at = pl.ds(base, local)
        bs[at, :] = dot_nn(n1[at, :], pb[...])
        xs[at, :] = dot_nn(n1[at, :], px[...])
        for q in range(spans):
            rows_q = pl.ds(base + q * SPAN, SPAN)
            product = (bs[rows_q, :] * xs[rows_q, :]).astype(bf16)
            bx[rows_q, :] = product
            if m:
                v["halo_out"][m, q] = product[SPAN - 16 :, :]

    def mixer_rest(m):
        base = m * local
        at = pl.ds(base, local)
        if m == 0:
            projections[2].wait()
        cs[at, :] = dot_nn(n1[at, :], pc[...])
        halo(m).wait_recv()
        for q in range(spans):
            rows_q = pl.ds(base + q * SPAN, SPAN)
            mine, near, far = span_facts(m, q)
            far_term, near_term, here = terms(m, q, near, far, mine)
            conv = tap[0] * far_term + tap[1] * near_term + tap[2] * here
            ym[rows_q, :] = (cs[rows_q, :] * conv).astype(bf16)
            if m == 0 and q == 0:
                projections[3].wait()
            term0[rows_q, :] = dot_nn(ym[rows_q, :], po[...]).astype(bf16)
            piece = m * spans + q
            branch.start(piece)
            if piece > 0:
                branch.relay(piece - 1)

    def middle(p, x):
        branch.ready(p)

        @pl.loop(0, half // BLOCK)
        def _(r):
            at = rows_at((2 * p + place.h) * half + r * BLOCK, BLOCK)
            value = x[at, :].astype(f32) + branch.total(p, r)
            r1h[rows_at(p * half + r * BLOCK, BLOCK), :] = value
            _, unit = normal(value)
            n2[at, :] = (unit * gain_row(ffn_gain)).astype(bf16)

        branch.spread(p, n2).start()

    def masked(m):
        cot_load[m].wait()
        for q in range(spans):
            kept = mask[m : m + 1, q * SPAN : (q + 1) * SPAN].astype(f32)
            kept = jnp.transpose(jnp.broadcast_to(kept, (SPAN, SPAN)))
            rows_q = pl.ds(m * local + q * SPAN, SPAN)
            for c in range(width // SPAN):
                cols = pl.ds(c * SPAN, SPAN)
                g[rows_q, cols] = (g[rows_q, cols].astype(f32) * kept).astype(bf16)

    def front(slot, m):
        at = slice(m * local, (m + 1) * local)
        both = dot_nt(n2[at, :], wgu[slot])
        back = dot_nt(g[at, :], wdb[slot])
        gate, up = both[:, :TILE], both[:, TILE:]
        sigma = jax.nn.sigmoid(gate)
        silu = gate * sigma
        hb[at, :] = (silu * up).astype(bf16)
        dgu[at, :TILE] = (back * up * sigma * (1.0 + gate * (1.0 - sigma))).astype(bf16)
        dgu[at, TILE:] = (back * silu).astype(bf16)

    def mixer_forward(x, tails):
        x_load = [loading(m, v["tokens"].at[m], x.at[m * local : (m + 1) * local]) for m in range(MICRO)]
        for copy in [x_load[0]] + projections[:2] + [x_load[1]] + projections[2:] + cot_load + weights(0, 0):
            copy.start()
        x_load[0].wait()
        for q in range(spans):
            _, unit = normal(x[(q + 1) * SPAN - 16 : (q + 1) * SPAN, :].astype(f32))
            tails[q * 16 : (q + 1) * 16, :] = (unit * gain_row(mix_gain)).astype(bf16)
        projections[0].wait()
        projections[1].wait()
        ends = (dot_nn(tails[...], pb[...]) * dot_nn(tails[...], px[...])).astype(bf16)
        for q in range(spans):
            v["halo_out"][0, q] = ends[q * 16 : (q + 1) * 16]
        pl.semaphore_wait(barrier, 5 + line - 1)
        halo(0).start()
        mixer_half(0, x)
        x_load[1].wait()
        mixer_rest(0)
        mixer_half(1, x)
        halo(1).start()
        mixer_rest(1)
        masked(0)
        branch.relay(pieces - 1)
        masked(1)
        for m in range(MICRO):
            for p in range(m * spans, (m + 1) * spans):
                middle(p, x)
            for p in range(m * spans, (m + 1) * spans):
                branch.spread(p, n2).wait()
                branch.settle(p)
            if m == 0:
                for copy in weights(0, 0):
                    copy.wait()
                front(0, 0)

    pl.run_scoped(mixer_forward, pltpu.VMEM((tokens, width), bf16), pltpu.VMEM((16 * spans, width), bf16))

    def feed_forward(oacc, dacc):
        oacc[...] = jnp.zeros_like(oacc)
        dacc[...] = jnp.zeros_like(dacc)

        @pl.loop(0, n_ffn)
        def _(j):
            slot = lax.rem(j, 2)

            @pl.when(jnp.logical_and(j > 0, j < full))
            def _():
                for copy in weights(jnp.minimum(j, full - 1), slot):
                    copy.wait()

            if rest:

                @pl.when(j == full)
                def _():
                    for copy in rest_weights():
                        copy.wait()

            @pl.when(j + 1 < full)
            def _():
                for copy in weights(jnp.minimum(j + 1, full - 1), 1 - slot):
                    copy.start()

            if rest:

                @pl.when(j + 1 == full)
                def _():
                    blank = jnp.zeros((TILE - rest, width), bf16)
                    wgu[full % 2, rest:TILE, :] = blank
                    wgu[full % 2, TILE + rest :, :] = blank
                    wdb[full % 2, rest:, :] = blank
                    for copy in rest_weights():
                        copy.start()

            @pl.when(j > 0)
            def _():
                front(slot, 0)
                front(slot, 1)

            @pl.when(j == 0)
            def _():
                front(0, 1)

            rs.produce(3 * j, [(0, g, lambda: hb[...])])
            oacc[...] += dot_nn(hb[...], wdb[slot])
            rs.flush(3 * j)
            rs.start_halving(j)
            rs.produce(3 * j + 1, [(0, n2, lambda: dgu[:, :TILE])], flushed=True)
            rs.produce(3 * j + 2, [(0, n2, lambda: dgu[:, TILE:])])
            rs.begin(j)
            dacc[...] += dot_nn(dgu[...], wgu[slot])
            rs.complete(j)

        rs.flush(3 * n_ffn - 1)
        for p in range(pieces):
            at = pl.ds(p * SPAN, SPAN)
            term1[at, :] = dacc[at, :].astype(bf16)
            second.start(p)
            if p > 1:
                second.relay(p - 2)
        for p in range(pieces):
            at = pl.ds(p * SPAN, SPAN)
            term0[at, :] = oacc[at, :].astype(bf16)
            feed.start(p)
            if p < 2:
                second.relay(pieces - 2 + p)

    pl.run_scoped(
        feed_forward,
        pltpu.VMEM((tokens, width), f32),
        pltpu.VMEM((tokens, width), f32),
    )
    taken = [n_ffn]

    def pump(count):
        rs.pump(taken[0], taken[0] + count)
        taken[0] += count

    def backward(dr1, xh, dym, dbx, gain_one, gain_two, tap_rows):
        x_load = [
            loading(
                8 + p,
                v["tokens"].at[p // spans, rows_at(p % spans * SPAN + place.h * half, half)],
                xh.at[p * half : (p + 1) * half],
            )
            for p in range(pieces)
        ]
        for copy in x_load:
            copy.start()
        gain_one[...] = jnp.zeros_like(gain_one)
        gain_two[...] = jnp.zeros_like(gain_two)
        pump(2)
        for p in range(pieces):
            feed.relay(p)
        pump(1)

        for p in range(pieces):
            second.ready(p)

            @pl.loop(0, half // BLOCK)
            def _(r):
                at = rows_at((2 * p + place.h) * half + r * BLOCK, BLOCK)
                here = rows_at(p * half + r * BLOCK, BLOCK)
                grad = second.total(p, r)
                scale, unit = normal(r1h[here, :])
                gain_two[...] += fold(grad * unit)
                weighted = grad * gain_row(ffn_gain)
                inner = jnp.mean(weighted * unit, axis=-1, keepdims=True)
                value = g[at, :].astype(f32) + scale * (weighted - unit * inner)
                dr1[here, :] = value
                n2[at, :] = value.astype(bf16)

            second.spread(p, n2).start()
            if p == 2:
                pump(2)

        for p in range(pieces):
            second.spread(p, n2).wait()
            second.settle(p)
        dym[...] = dot_nt(n2[...], po[...])
        tap_sums = [jnp.zeros((8, chan), f32) for _ in range(3)]
        for m in range(MICRO):
            for q in range(spans):
                rows_q = pl.ds(m * local + q * SPAN, SPAN)
                mine, near, far = span_facts(m, q)
                far_term, near_term, here = terms(m, q, near, far, mine)
                grad = dym[rows_q, :]
                cat[rows_q, chan : 2 * chan] = (
                    grad * (tap[0] * far_term + tap[1] * near_term + tap[2] * here)
                ).astype(bf16)
                grad = grad * cs[rows_q, :]
                for k, other in enumerate((far_term, near_term, here)):
                    tap_sums[k] = tap_sums[k] + fold(grad * other)
                old = jnp.where(far, tap[0] * grad, 0.0)
                mid = jnp.where(near, tap[1] * grad, 0.0)
                dbx[rows_q, :] = (
                    tap[2] * grad
                    + jnp.where(row_ids < SPAN - 1, pltpu.roll(mid, SPAN - 1, 0), 0.0)
                    + jnp.where(row_ids < SPAN - 2, pltpu.roll(old, SPAN - 2, 0), 0.0)
                )
                top_ids = row_ids[:8]
                v["back_out"][m, q] = jnp.where(top_ids < 2, old[:8], 0.0) + jnp.where(
                    top_ids == 1, mid[0:1], 0.0
                )
            halo_back(m).start()
        pump(2)
        for k in range(3):
            tap_rows[k] = tap_sums[k]
        for m in range(MICRO):
            halo_back(m).wait_recv()
            for q in range(spans):
                rows_q = pl.ds(m * local + q * SPAN, SPAN)
                mine = order[m, place.s * spans + q]
                from_next = jnp.zeros((8, chan), f32)
                for k in range(spans):
                    took = order[m, place.after * spans + k] == mine + 1
                    from_next = from_next + jnp.where(took, v["back_in"][m, k], 0.0)
                value = dbx[rows_q, :]
                value = (
                    value
                    + jnp.where(row_ids == SPAN - 2, from_next[0:1], 0.0)
                    + jnp.where(row_ids == SPAN - 1, from_next[1:2], 0.0)
                )
                cat[rows_q, 0:chan] = (value * xs[rows_q, :]).astype(bf16)
                cat[rows_q, 2 * chan :] = (value * bs[rows_q, :]).astype(bf16)
        k0 = 3 * n_ffn
        wide = 3 * chan
        whole = wide // TILE
        for k in range(whole):
            rs.produce(k0 + k, [(0, n1, lambda k=k: cat[:, k * TILE : (k + 1) * TILE])])
            if k % 2 == 1:
                pump(1)
        left = wide - whole * TILE
        rs.produce(
            k0 + whole,
            [
                (0, n1, lambda: cat[:, whole * TILE :]),
                (left, n2, lambda: ym[:, 0 : TILE - left]),
            ],
        )
        rs.produce(k0 + whole + 1, [(0, n2, lambda: ym[:, TILE - left :])])
        rs.flush(k0 + whole + 1)
        assert taken[0] < rs.AHEAD + 13
        pump(1)

        for p in range(pieces):
            feed.ready(p)

            @pl.loop(0, half // BLOCK)
            def _(r):
                here = rows_at(p * half + r * BLOCK, BLOCK)
                at = rows_at(r * BLOCK, BLOCK)
                across2[p, at, :] = (r1h[here, :] + feed.total(p, r)).astype(bf16)

            for copy in feed.publish(p, across2, v["block_out"]):
                copy.start()
            feed.settle(p)
        pump(1)
        for m in range(MICRO):
            at = pl.ds(m * local, local)
            term0[at, :] = (
                dot_nt(cat[at, 0:chan], pb[...])
                + dot_nt(cat[at, chan : 2 * chan], pc[...])
                + dot_nt(cat[at, 2 * chan :], px[...])
            ).astype(bf16)
            for p in range(m * spans, (m + 1) * spans):
                first.start(p)
        for p in range(pieces):
            first.relay(p)
        pump(2)
        for p in range(pieces):
            x_load[p].wait()
            first.ready(p)

            @pl.loop(0, half // BLOCK)
            def _(r):
                here = rows_at(p * half + r * BLOCK, BLOCK)
                at = rows_at(r * BLOCK, BLOCK)
                grad = first.total(p, r)
                scale, unit = normal(xh[here, :].astype(f32))
                gain_one[...] += fold(grad * unit)
                weighted = grad * gain_row(mix_gain)
                inner = jnp.mean(weighted * unit, axis=-1, keepdims=True)
                across0[p, at, :] = (dr1[here, :] + scale * (weighted - unit * inner)).astype(bf16)

            for copy in first.publish(p, across0, v["d_tokens"]):
                copy.start()
            if p % 2 == 1:
                pump(1)

        small, gather = v["small"], v["gather"]
        ssem = v["ssem"]
        side = width // 2
        small[0] = jnp.zeros((8, side), f32)
        for n, gain in enumerate((gain_one, gain_two)):
            row = jnp.sum(gain[...], axis=0, keepdims=True)
            small[0, 2 * n : 2 * n + 1, :] = row[:, :side]
            small[0, 2 * n + 1 : 2 * n + 2, :] = row[:, side:]
        for k in range(3):
            at = k % 2 * chan
            small[0, 4 + k // 2 : 5 + k // 2, at : at + chan] = jnp.sum(tap_rows[k], axis=0, keepdims=True)
        core = send_to(small.at[0], gather.at[0], ssem.at[0], ssem.at[1], place.core)
        core.start()
        pump(1)
        core.wait_recv()
        small[1] = small[0] + jnp.where(lax.broadcasted_iota(jnp.int32, (8, 1), 0) < 4, gather[0], 0.0)
        pair = send_to(small.at[1], gather.at[1], ssem.at[2], ssem.at[3], place.pair)
        pair.start()
        pump(3)
        pair.wait_recv()
        small[2] = small[1] + gather[1]

        def along(c, slot):
            return send_to(
                small.at[2], gather.at[2 + slot], ssem.at[4 + c], ssem.at[4 + line + slot], (c * 2 + place.b, place.t)
            )

        @pl.loop(0, line)
        def _(c):
            @pl.when(c != place.a)
            def _():
                along(c, place.a).start()

        gather[2 + place.a] = small[2]

        rs.pump(taken[0], rs.steps)

        @pl.loop(0, line)
        def _(c):
            @pl.when(c != place.a)
            def _():
                along(c, c).wait_recv()
                along(c, place.a).wait_send()

        total = gather[2]
        for c in range(1, line):
            total = total + gather[2 + c]
        v["small_out"][...] = total
        core.wait_send()
        pair.wait_send()
        for m in range(MICRO):
            halo(m).wait_send()
            halo_back(m).wait_send()
        for m in range(pieces):
            first.settle(m)
            for each, staged, out in ((feed, across2, v["block_out"]), (first, across0, v["d_tokens"])):
                for copy in each.publish(m, staged, out):
                    copy.wait()
        rs.finish()

    pl.run_scoped(
        backward,
        pltpu.VMEM((tokens // 2, width), f32),
        pltpu.VMEM((tokens // 2, width), bf16),
        pltpu.VMEM((tokens, chan), f32),
        pltpu.VMEM((tokens, chan), f32),
        pltpu.VMEM((8, width), f32),
        pltpu.VMEM((8, width), f32),
        pltpu.VMEM((3, 8, chan), f32),
    )


def body(
    seq_count,
    tokens,
    mix_gain,
    proj_b,
    proj_c,
    proj_x,
    conv_taps,
    proj_out,
    ffn_gain,
    w_gate,
    w_up,
    w_down,
    cotangent,
    seq_lengths,
    span_order,
    keep_mask,
):
    local, width = tokens.shape[1:]
    total = MICRO * local
    half = SPAN // 2
    chan = proj_b.shape[1]
    units = w_gate.shape[1]
    n_ffn = pl.cdiv(units, TILE)
    line = seq_count // 2
    rows = width // seq_count
    n_tiles = 3 * n_ffn + 6
    spans = local // SPAN
    pieces = MICRO * spans
    dma = pltpu.SemaphoreType.DMA
    vmem = pl.BlockSpec(memory_space=pltpu.VMEM)
    smem = pl.BlockSpec(memory_space=pltpu.SMEM)
    hbm = pl.BlockSpec(memory_space=pl.ANY)
    shape = jax.ShapeDtypeStruct
    inputs = [
        ("lengths", seq_lengths, smem),
        ("order", span_order, smem),
        ("mask", keep_mask, vmem),
        ("mix_gain", mix_gain, vmem),
        ("ffn_gain", ffn_gain, vmem),
        ("taps", conv_taps, vmem),
        ("tokens", tokens, hbm),
        ("cotangent", cotangent, hbm),
        ("proj_b", proj_b, hbm),
        ("proj_c", proj_c, hbm),
        ("proj_x", proj_x, hbm),
        ("proj_out", proj_out, hbm),
        ("w_gate", w_gate.T, hbm),
        ("w_up", w_up.T, hbm),
        ("w_down", w_down, hbm),
    ]
    outputs = [
        ("block_out", shape((total, width), bf16), hbm),
        ("d_tokens", shape((total, width), bf16), hbm),
        ("grads", shape((4, rows, n_ffn * TILE), f32), hbm),
        ("small_out", shape((8, width // 2), f32), vmem),
        ("wbuf", shape((n_tiles, 2, line, rows, TILE), bf16), hbm),
        ("ybuf", shape((n_tiles, line, rows, TILE), bf16), hbm),
    ]
    scratch = [
        ("n1", pltpu.VMEM((total, width), bf16)),
        ("n2", pltpu.VMEM((total, width), bf16)),
        ("g", pltpu.VMEM((total, width), bf16)),
        ("term0", pltpu.VMEM((total, width), bf16)),
        ("term1", pltpu.VMEM((total, width), bf16)),
        ("r1h", pltpu.VMEM((total // 2, width), f32)),
        ("inbox0", pltpu.VMEM((pieces, half, width), bf16)),
        ("inbox1", pltpu.VMEM((pieces, half, width), bf16)),
        ("across0", pltpu.VMEM((pieces, half, width), bf16)),
        ("across1", pltpu.VMEM((pieces, half, width), bf16)),
        ("across2", pltpu.VMEM((pieces, half, width), bf16)),
        ("pb", pltpu.VMEM((width, chan), bf16)),
        ("pc", pltpu.VMEM((width, chan), bf16)),
        ("px", pltpu.VMEM((width, chan), bf16)),
        ("po", pltpu.VMEM((chan, width), bf16)),
        ("bs", pltpu.VMEM((total, chan), f32)),
        ("cs", pltpu.VMEM((total, chan), f32)),
        ("xs", pltpu.VMEM((total, chan), f32)),
        ("bx", pltpu.VMEM((total, chan), bf16)),
        ("ym", pltpu.VMEM((total, chan), bf16)),
        ("cat", pltpu.VMEM((total, 3 * chan), bf16)),
        ("wgu", pltpu.VMEM((2, 2 * TILE, width), bf16)),
        ("wdb", pltpu.VMEM((2, TILE, width), bf16)),
        ("hb", pltpu.VMEM((total, TILE), bf16)),
        ("dgu", pltpu.VMEM((total, 2 * TILE), bf16)),
        ("halo_out", pltpu.VMEM((MICRO, spans, 16, chan), bf16)),
        ("halo_in", pltpu.VMEM((MICRO, spans, 16, chan), bf16)),
        ("back_out", pltpu.VMEM((MICRO, spans, 8, chan), f32)),
        ("back_in", pltpu.VMEM((MICRO, spans, 8, chan), f32)),
        ("small", pltpu.VMEM((3, 8, width // 2), f32)),
        ("gather", pltpu.VMEM((2 + line, 8, width // 2), f32)),
        ("load", dma((8 + pieces,))),
        ("wsem", dma((2, 3))),
        ("sums", dma((4, pieces, 7))),
        ("hsem", dma((4, MICRO))),
        ("ssem", dma((4 + 2 * line,))),
    ]
    scratch += list(zip(Scatter.NAMES, Scatter.scratch(n_tiles, line, rows)))
    names = [n for n, _, _ in inputs] + [n for n, _, _ in outputs] + [n for n, _ in scratch]
    results = pl.pallas_call(
        functools.partial(kernel, line, rows, n_ffn, names),
        out_shape=tuple(s for _, s, _ in outputs),
        in_specs=[s for _, _, s in inputs],
        out_specs=tuple(s for _, _, s in outputs),
        scratch_shapes=[s for _, s in scratch],
        compiler_params=pltpu.CompilerParams(
            collective_id=0, has_side_effects=True, vmem_limit_bytes=62 * 2**20 - 2**19
        ),
    )(*[a for _, a, _ in inputs])
    done = finish_call(results[:4], total, width, chan, units, rows)
    return (
        done[0].reshape(tokens.shape),
        done[1].reshape(tokens.shape),
        done[2],
        done[3],
        done[4],
        done[5],
        done[6],
        done[7].T,
        done[8],
        done[9],
        done[10],
        done[11].T,
    )


def finish_kernel(
    block_in, tokens_in, grads, small, block_out, d_tokens, d_mixgain, d_b, d_c, d_x, d_taps, d_out, d_ffngain, d_gate, d_up, d_down
):
    chan, units = d_b.shape[1], d_gate.shape[1]
    side = small.shape[1]
    block_out[...] = block_in[...]
    d_tokens[...] = tokens_in[...]
    for n, out in enumerate((d_b, d_c, d_x, d_out)):
        out[...] = grads[3, :, n * chan : (n + 1) * chan]
    for n, out in enumerate((d_down, d_gate, d_up)):
        out[...] = grads[n, :, :units]

    @pl.when(pl.program_id(0) == 0)
    def _():
        for n, out in enumerate((d_mixgain, d_ffngain)):
            out[0:side] = small[2 * n : 2 * n + 1, :].reshape(side)
            out[side:] = small[2 * n + 1 : 2 * n + 2, :].reshape(side)
        for k in range(3):
            at = k % 2 * chan
            d_taps[k : k + 1, :] = small[4 + k // 2 : 5 + k // 2, at : at + chan]


def finish_call(arrays, tokens, width, chan, units, rows):
    cuts = 3
    shape = jax.ShapeDtypeStruct

    def by_rows(count, columns):
        return pl.BlockSpec((count // cuts, columns), lambda i: (i, 0))

    def whole(*sizes):
        return pl.BlockSpec(sizes, lambda i: (0,) * len(sizes))

    return pl.pallas_call(
        finish_kernel,
        grid=(cuts,),
        in_specs=[
            by_rows(tokens, width),
            by_rows(tokens, width),
            pl.BlockSpec((4, rows // cuts, arrays[2].shape[2]), lambda i: (0, i, 0)),
            whole(*arrays[3].shape),
        ],
        out_shape=(
            shape((tokens, width), bf16),
            shape((tokens, width), bf16),
            shape((width,), f32),
            shape((rows, chan), f32),
            shape((rows, chan), f32),
            shape((rows, chan), f32),
            shape((3, chan), f32),
            shape((rows, chan), f32),
            shape((width,), f32),
            shape((rows, units), f32),
            shape((rows, units), f32),
            shape((rows, units), f32),
        ),
        out_specs=(
            by_rows(tokens, width),
            by_rows(tokens, width),
            whole(width),
            by_rows(rows, chan),
            by_rows(rows, chan),
            by_rows(rows, chan),
            whole(3, chan),
            by_rows(rows, chan),
            whole(width),
            by_rows(rows, units),
            by_rows(rows, units),
            by_rows(rows, units),
        ),
    )(*arrays)


def solution(mesh):
    placed = (
        P(None, "seq", None),
        P(),
        P(None, "tp"),
        P(None, "tp"),
        P(None, "tp"),
        P(None, "tp"),
        P("tp", None),
        P(),
        P(None, "tp"),
        P(None, "tp"),
        P("tp", None),
        P(None, "seq", None),
        P(),
        P(),
        P(None, "seq"),
    )
    return jax.shard_map(
        functools.partial(body, mesh.shape["seq"]),
        mesh=mesh,
        in_specs=placed,
        out_specs=(
            P(None, "seq", None),
            P(None, "seq", None),
            P(),
            P("seq", "tp"),
            P("seq", "tp"),
            P("seq", "tp"),
            P(None, "tp"),
            P("tp", "seq"),
            P(),
            P("seq", "tp"),
            P("seq", "tp"),
            P("tp", "seq"),
        ),
        check_vma=False,
    )
```

```python
import functools
import jax
import jax.numpy as jnp
from jax import lax
from jax.experimental import pallas as pl
from jax.experimental.pallas import tpu as pltpu
from jax.sharding import PartitionSpec as P

SPAN = 128
MICRO = 2
EPSILON = 1e-05
MESH = pl.DeviceIdType.MESH
TILE = 256
BLOCK = 32
ROWS = 384
f32 = jnp.float32
bf16 = jnp.bfloat16


def dot_nn(a, b):
    return jnp.dot(a, b, preferred_element_type=f32)


def dot_nt(a, b):
    return lax.dot_general(a, b, (((1,), (1,)), ((), ())), preferred_element_type=f32)


def dot_tn(a, b):
    return lax.dot_general(a, b, (((0,), (0,)), ((), ())), preferred_element_type=f32)


def send_to(src, dst, send_sem, recv_sem, device):
    return pltpu.make_async_remote_copy(
        src_ref=src,
        dst_ref=dst,
        send_sem=send_sem,
        recv_sem=recv_sem,
        device_id=device,
        device_id_type=MESH,
    )


def rows_at(start, size):
    return pl.ds(pl.multiple_of(start, 16), size)


class Place:
    def __init__(self, line):
        self.line = line
        self.s = lax.axis_index("seq")
        self.t = lax.axis_index("tp")
        self.a = lax.div(self.s, 2)
        self.b = lax.rem(self.s, 2)
        self.h = lax.rem(self.t, 2)
        count = 2 * line
        self.pair = (self.a * 2 + 1 - self.b, self.t)
        self.up = (lax.rem(self.a + 1, line) * 2 + self.b, self.t)
        self.down = (lax.rem(self.a + line - 1, line) * 2 + self.b, self.t)
        self.after = lax.rem(self.s + 1, count)
        self.before = lax.rem(self.s + count - 1, count)
        self.next = (self.after, self.t)
        self.last = (self.before, self.t)
        self.core = (self.s, self.t + 1 - 2 * self.h)
        self.across = (self.s, lax.rem(self.t + 2, 4))


class Scatter:
    NAMES = (
        "stage", "zin", "fetch", "yfetch", "acc", "final", "swap_out", "swap_in", "swap_sum",
        "stage_sem", "ysend_sem", "yrecv_sem", "zsend_sem", "zin_sem", "fetch_sem", "yfetch_sem", "final_sem",
        "swap_sem", "sum_sem",
    )
    EARLY = 4
    AHEAD = 7

    def __init__(self, place, n_tiles, ffn_tiles, rows, wbuf, ybuf, out, scratch):
        self.place, self.a, self.b, self.line = place, place.a, place.b, place.line
        self.n, self.ffn_tiles, self.rows = n_tiles, ffn_tiles, rows
        self.wbuf, self.ybuf, self.out = wbuf, ybuf, out
        for name, ref in zip(self.NAMES, scratch):
            setattr(self, name, ref)
        self.slots = self.zin.shape[0]
        self.items = n_tiles + self.EARLY
        self.hop = self.hop_of(self.line)
        self.held = self.fetch.shape[0]
        self.steps = self.items + self.hop * (self.line - 1)
        self.swaps = self.swap_sum.shape[0]

    @staticmethod
    def hop_of(line):
        return 2 if line <= 4 else 1

    @classmethod
    def scratch(cls, n_tiles, line, rows):
        slots = cls.hop_of(line) * line + 1
        held = 2 * cls.hop_of(line)
        swaps = cls.EARLY
        dma = pltpu.SemaphoreType.DMA
        return [
            pltpu.VMEM((2, 2, line, rows, TILE), bf16),
            pltpu.VMEM((slots, line + 1, rows, TILE), bf16),
            pltpu.VMEM((held, line, rows, TILE), bf16),
            pltpu.VMEM((2, line, rows, TILE), bf16),
            pltpu.VMEM((rows, TILE), f32),
            pltpu.VMEM((2, rows, TILE), f32),
            pltpu.VMEM((swaps, rows, TILE), bf16),
            pltpu.VMEM((swaps, rows, TILE), bf16),
            pltpu.VMEM((swaps, rows, TILE), f32),
            dma((2, 2)),
            dma((n_tiles,)),
            dma((n_tiles,)),
            dma((held, line)),
            dma((slots, line + 1)),
            dma((held, line)),
            dma((2, line)),
            dma((2,)),
            dma((2, swaps)),
            dma((swaps,)),
        ]


    def local(self, k):
        slot = lax.rem(k, 2)
        return (
            pltpu.make_async_copy(self.stage.at[slot, 1 - self.b], self.wbuf.at[k, 0], self.stage_sem.at[slot, 0]),
            pltpu.make_async_copy(self.stage.at[slot, self.b], self.wbuf.at[k, 1], self.stage_sem.at[slot, 1]),
        )

    def halved(self, k):
        return jnp.logical_or(lax.rem(k, 3) == 0, k > self.early_tile(self.EARLY - 1))

    @staticmethod
    def early_tile(n):
        return n + 1 + n // 2 if isinstance(n, int) else n + 1 + lax.div(n, 2)

    def halve(self, k):
        return send_to(
            self.wbuf.at[k, 0], self.ybuf.at[k], self.ysend_sem.at[k], self.yrecv_sem.at[k], self.place.pair
        )

    def flush(self, k):
        for copy in self.local(k):
            copy.wait()

    def halved_tile(self, n):
        return jnp.where(n <= self.EARLY // 2, 3 * n, n + self.EARLY)

    def start_halving(self, n):
        self.halve(self.halved_tile(n)).start()

    def produce(self, k, parts, flushed=False):
        if not flushed:

            @pl.when(jnp.logical_and(k != 0, k != self.ffn_tiles))
            def _():
                self.flush(k - 1)

        slot = lax.rem(k, 2)
        for offset, left, right in parts:
            width = right().shape[1]
            for start in range(0, left.shape[1], ROWS):
                value = dot_tn(left[:, start : start + ROWS], right())
                for n in range(ROWS // self.rows):
                    c, half = divmod(start // self.rows + n, 2)
                    self.stage[slot, half, c, :, offset : offset + width] = value[
                        n * self.rows : (n + 1) * self.rows
                    ].astype(bf16)
        for copy in self.local(k):
            copy.start()


    def item_of(self, i, c):
        a, far = self.a, self.line - 1 - self.a
        return i - self.hop * jnp.where(c > a, a, jnp.where(c < a, far, jnp.maximum(a, far)))

    def inside(self, q):
        return jnp.logical_and(q >= 0, q < self.items)

    def item(self, q):
        q = jnp.clip(q, 0, self.items - 1)
        early = q < 2 * self.EARLY
        n = q - 2 * self.EARLY
        tile = self.halved_tile(n)
        return (
            jnp.where(early, self.early_tile(lax.div(q, 2)), tile),
            jnp.where(early, lax.rem(q, 2), 2),
        )

    def block(self, n):
        return jnp.where(n < self.a, n, self.line - 1 - (n - self.a))

    def fetching(self, i, c):
        slot = lax.rem(i, self.held)
        tile, kind = self.item(self.item_of(i, c))
        side = jnp.where(kind == 0, 0, 1)
        return pltpu.make_async_copy(
            self.wbuf.at[tile, side, c], self.fetch.at[slot, c], self.fetch_sem.at[slot, c]
        )

    def yfetching(self, i, c):
        slot = lax.rem(i, 2)
        tile, _ = self.item(self.item_of(i, c))
        return pltpu.make_async_copy(self.ybuf.at[tile, c], self.yfetch.at[slot, c], self.yfetch_sem.at[slot, c])

    def onward(self, i, c, upward):
        slot = lax.rem(i, self.held)
        at = lax.rem(jnp.clip(self.item_of(i, c), 0, self.items - 1), self.slots)
        where = c + 1 if upward else c
        return send_to(
            self.fetch.at[slot, c],
            self.zin.at[at, where],
            self.zsend_sem.at[slot, c],
            self.zin_sem.at[at, where],
            self.place.up if upward else self.place.down,
        )

    def drain(self, i):
        @pl.loop(0, self.line)
        def _(c):
            @pl.when(jnp.logical_and(self.inside(self.item_of(i, c)), c != self.a))
            def _():
                self.onward(i, c, False).wait_send()

    def storing(self, q):
        slot = lax.rem(q, 2)
        tile, _ = self.item(q)
        return pltpu.make_async_copy(self.final.at[slot], self.place_of(tile), self.final_sem.at[slot])

    def place_of(self, tile):
        is_ffn = tile < self.ffn_tiles
        kind = jnp.where(is_ffn, lax.rem(tile, 3), 3)
        column = jnp.where(is_ffn, lax.div(tile, 3), tile - self.ffn_tiles)
        return self.out.at[kind, :, pl.ds(pl.multiple_of(column * TILE, TILE), TILE)]

    def swapping(self, group):
        return send_to(
            self.swap_out.at[group], self.swap_in.at[group], self.swap_sem.at[0, group], self.swap_sem.at[1, group],
            self.place.pair,
        )

    def begin(self, i):
        @pl.when(i >= self.held)
        def _():
            self.drain(i - self.held)

        ahead = lax.div(3 * i, 4)
        fresh = jnp.logical_and(ahead > lax.div(3 * i - 3, 4), i >= self.AHEAD)

        @pl.when(jnp.logical_and(fresh, ahead + 2 < self.n - self.EARLY))
        def _():
            self.start_halving(ahead + 2)

        q = i - self.hop * jnp.minimum(self.a, self.line - 1 - self.a)
        tile, kind = self.item(q)

        @pl.when(jnp.logical_and(self.inside(q), kind == 2))
        def _():
            self.halve(tile).wait_recv()

        @pl.loop(0, self.line)
        def _(n):
            c = self.block(n)
            q = self.item_of(i, c)
            _, kind = self.item(q)

            @pl.when(self.inside(q))
            def _():
                self.fetching(i, c).start()

            @pl.when(jnp.logical_and(self.inside(q), kind == 2))
            def _():
                self.yfetching(i, c).start()

    def complete(self, i):
        line, a, acc = self.line, self.a, self.acc
        slot = lax.rem(i, self.held)
        yslot = lax.rem(i, 2)

        @pl.loop(0, line)
        def _(n):
            c = self.block(n)
            q = self.item_of(i, c)

            @pl.when(self.inside(q))
            def _():
                _, kind = self.item(q)
                group = jnp.minimum(lax.div(q, 2), self.EARLY - 1)
                at = lax.rem(q, self.slots)

                def arrival(where, device):
                    send_to(
                        self.fetch.at[slot, c],
                        self.zin.at[at, where],
                        self.zsend_sem.at[slot, c],
                        self.zin_sem.at[at, where],
                        device,
                    ).wait_recv()
                    acc[...] += self.zin[at, where].astype(f32)

                self.fetching(i, c).wait()
                acc[...] = self.fetch[slot, c].astype(f32)

                @pl.when(kind == 2)
                def _():
                    self.yfetching(i, c).wait()
                    acc[...] += self.yfetch[yslot, c].astype(f32)

                @pl.when(jnp.logical_and(c >= a, a > 0))
                def _():
                    arrival(c + 1, self.place.down)

                @pl.when(jnp.logical_and(c <= a, a < line - 1))
                def _():
                    arrival(c, self.place.up)

                @pl.when(c != a)
                def _():
                    self.fetch[slot, c] = acc[...].astype(bf16)

                    @pl.when(c > a)
                    def _():
                        self.onward(i, c, True).start()

                    @pl.when(c < a)
                    def _():
                        self.onward(i, c, False).start()

                @pl.when(c == a)
                def _():
                    _, older = self.item(q - 2)

                    @pl.when(jnp.logical_and(q >= 2, older == 2))
                    def _():
                        self.storing(q - 2).wait()

                    @pl.when(kind == 0)
                    def _():
                        self.swap_out[group] = acc[...].astype(bf16)
                        self.swapping(group).start()

                    @pl.when(kind == 1)
                    def _():
                        self.swap_sum[group] = acc[...]

                    @pl.when(kind == 2)
                    def _():
                        self.final[lax.rem(q, 2)] = acc[...]
                        self.storing(q).start()

    def pump(self, low, high):
        @pl.loop(low, high)
        def _(i):
            self.begin(i)
            self.complete(i)

    def finish(self):
        def summed(group):
            return pltpu.make_async_copy(
                self.swap_sum.at[group], self.place_of(self.early_tile(group)), self.sum_sem.at[group]
            )

        @pl.loop(0, self.swaps)
        def _(group):
            self.swapping(group).wait_recv()
            self.swap_sum[group] += self.swap_in[group].astype(f32)
            summed(group).start()

        for n in range(self.held):
            self.drain(self.steps - 1 - n)
        for q in (self.items - 2, self.items - 1):
            assert q >= 2 * self.EARLY
            self.storing(q).wait()

        @pl.loop(0, self.swaps)
        def _(group):
            self.swapping(group).wait_send()
            summed(group).wait()

        @pl.loop(0, self.n)
        def _(k):
            @pl.when(self.halved(k))
            def _():
                self.halve(k).wait_send()


class Sum:
    def __init__(self, place, which, term, inbox, across, sems):
        self.place, self.which, self.term, self.inbox, self.across, self.sems = place, which, term, inbox, across, sems
        self.half = inbox.shape[1]

    def own(self, m):
        return rows_at((2 * m + self.place.h) * self.half, self.half)

    def other(self, m):
        return rows_at((2 * m + 1 - self.place.h) * self.half, self.half)

    def first(self, m):
        return send_to(
            self.term.at[self.other(m)], self.inbox.at[m], self.sems.at[self.which, m, 0], self.sems.at[self.which, m, 1],
            self.place.core,
        )

    def second(self, m):
        return send_to(
            self.term.at[self.own(m)], self.across.at[m], self.sems.at[self.which, m, 2], self.sems.at[self.which, m, 3],
            self.place.across,
        )

    def start(self, m):
        self.first(m).start()

    def relay(self, m):
        self.first(m).wait_recv()
        base = (2 * m + self.place.h) * self.half

        @pl.loop(0, self.half // BLOCK)
        def _(r):
            at = rows_at(base + r * BLOCK, BLOCK)
            took = self.inbox[m, rows_at(r * BLOCK, BLOCK), :].astype(f32)
            self.term[at, :] = (self.term[at, :].astype(f32) + took).astype(bf16)

        self.second(m).start()

    def ready(self, m):
        self.second(m).wait_recv()

    def total(self, m, r):
        at = rows_at((2 * m + self.place.h) * self.half + r * BLOCK, BLOCK)
        return self.term[at, :].astype(f32) + self.across[m, rows_at(r * BLOCK, BLOCK), :].astype(f32)

    def settle(self, m):
        self.first(m).wait_send()
        self.second(m).wait_send()

    def spread(self, m, buffer):
        at = self.own(m)
        return send_to(
            buffer.at[at], buffer.at[at], self.sems.at[self.which, m, 4], self.sems.at[self.which, m, 5], self.place.core
        )

    def publish(self, m, staged, out):
        target = out.at[rows_at((2 * m + self.place.h) * self.half, self.half)]
        return (
            pltpu.make_async_copy(staged.at[m], target, self.sems.at[self.which, m, 6]),
            send_to(
                staged.at[m], target, self.sems.at[self.which, m, 4], self.sems.at[self.which, m, 5],
                self.place.core,
            ),
        )


def gain_row(gain):
    return gain[...].reshape(1, gain.shape[0])


def normal(values):
    scale = lax.rsqrt(jnp.mean(values * values, axis=-1, keepdims=True) + EPSILON)
    return scale, values * scale


def fold(values):
    return jnp.sum(values.reshape(values.shape[0] // 8, 8, values.shape[1]), axis=0)


def kernel(line, rows, n_ffn, names, *refs):
    v = dict(zip(names, refs))
    (lengths, order, mask, mix_gain, ffn_gain, taps_in) = (
        v[n] for n in ("lengths", "order", "mask", "mix_gain", "ffn_gain", "taps")
    )
    place = Place(line)
    n1, n2, g, term0, term1, r1h = (v[n] for n in ("n1", "n2", "g", "term0", "term1", "r1h"))
    inbox0, inbox1, across0, across1, across2 = (v[n] for n in ("inbox0", "inbox1", "across0", "across1", "across2"))
    pb, pc, px, po = (v[n] for n in ("pb", "pc", "px", "po"))
    bs, cs, xs, bx, ym, cat = (v[n] for n in ("bs", "cs", "xs", "bx", "ym", "cat"))
    hb, dgu = v["hb"], v["dgu"]
    sums, load = v["sums"], v["load"]
    tokens, width = n1.shape
    local = tokens // MICRO
    spans = local // SPAN
    pieces = MICRO * spans
    half = SPAN // 2
    chan = bs.shape[1]
    units = v["w_down"].shape[0]
    full = units // TILE
    rest = units - full * TILE
    docs = lengths.shape[1]
    rs = Scatter(
        place, 3 * n_ffn + 6, 3 * n_ffn, rows, v["wbuf"], v["ybuf"], v["grads"],
        [v[n] for n in Scatter.NAMES],
    )
    branch = Sum(place, 0, term0, inbox0, across0, sums)
    second = Sum(place, 1, term1, inbox1, across1, sums)
    feed = Sum(place, 2, term0, inbox0, across2, sums)
    first = Sum(place, 3, term0, inbox1, across0, sums)

    barrier = pltpu.get_barrier_semaphore()
    for device in (place.pair, place.next, place.last, place.core, place.across):
        pl.semaphore_signal(barrier, inc=1, device_id=device, device_id_type=MESH)

    @pl.loop(0, line)
    def _(c):
        @pl.when(c != place.a)
        def _():
            pl.semaphore_signal(barrier, inc=1, device_id=(c * 2 + place.b, place.t), device_id_type=MESH)

    def loading(which, src, dst):
        return pltpu.make_async_copy(src, dst, load.at[which])

    projections = [
        loading(2, v["proj_b"], pb),
        loading(3, v["proj_x"], px),
        loading(4, v["proj_c"], pc),
        loading(5, v["proj_out"], po),
    ]
    cot_load = [loading(6 + m, v["cotangent"].at[m], g.at[m * local : (m + 1) * local]) for m in range(MICRO)]
    wgu, wdb = v["wgu"], v["wdb"]

    def weights(j, slot):
        at = pl.ds(pl.multiple_of(j * TILE, TILE), TILE)
        return [
            pltpu.make_async_copy(v[src].at[at], dst, v["wsem"].at[slot, q])
            for q, (src, dst) in enumerate(
                (("w_gate", wgu.at[slot, 0:TILE]), ("w_up", wgu.at[slot, TILE:]), ("w_down", wdb.at[slot]))
            )
        ]

    def rest_weights():
        slot = full % 2
        return [
            pltpu.make_async_copy(v[src].at[full * TILE :], dst, v["wsem"].at[slot, q])
            for q, (src, dst) in enumerate(
                (
                    ("w_gate", wgu.at[slot, 0:rest]),
                    ("w_up", wgu.at[slot, TILE : TILE + rest]),
                    ("w_down", wdb.at[slot, 0:rest]),
                )
            )
        ]

    taps = taps_in[...].astype(f32)
    row_ids = lax.broadcasted_iota(jnp.int32, (SPAN, 1), 0)
    tap = [taps[k : k + 1, :] for k in range(3)]

    def span_facts(m, q):
        mine = order[m, place.s * spans + q]
        position = mine * SPAN + row_ids
        near = position >= 0
        far = position >= 0
        begin = jnp.int32(0)
        for n in range(docs):
            near = jnp.logical_and(near, position != begin)
            far = jnp.logical_and(far, position != begin + 1)
            begin = begin + lengths[m, n]
        return mine, near, jnp.logical_and(near, far)

    def terms(m, q, near, far, mine):
        here = bx[pl.ds(m * local + q * SPAN, SPAN), :].astype(f32)
        older = jnp.zeros((1, chan), f32)
        newer = jnp.zeros((1, chan), f32)
        for k in range(spans):
            took = order[m, place.before * spans + k] == mine - 1
            tail = v["halo_in"][m, k].astype(f32)
            older = older + jnp.where(took, tail[14:15], 0.0)
            newer = newer + jnp.where(took, tail[15:16], 0.0)
        far_term = pltpu.roll(here, 2, 0)
        far_term = jnp.where(row_ids == 0, older, jnp.where(row_ids == 1, newer, far_term))
        near_term = jnp.where(row_ids == 0, newer, pltpu.roll(here, 1, 0))
        return jnp.where(far, far_term, 0.0), jnp.where(near, near_term, 0.0), here

    def halo(m):
        return send_to(
            v["halo_out"].at[m], v["halo_in"].at[m], v["hsem"].at[0, m], v["hsem"].at[1, m], place.next
        )

    def halo_back(m):
        return send_to(
            v["back_out"].at[m], v["back_in"].at[m], v["hsem"].at[2, m], v["hsem"].at[3, m], place.last
        )

    def mixer_half(m, x):
        base = m * local

        @pl.loop(0, local // BLOCK)
        def _(r):
            at = rows_at(base + r * BLOCK, BLOCK)
            _, unit = normal(x[at, :].astype(f32))
            n1[at, :] = (unit * gain_row(mix_gain)).astype(bf16)

        at = pl.ds(base, local)
        bs[at, :] = dot_nn(n1[at, :], pb[...])
        xs[at, :] = dot_nn(n1[at, :], px[...])
        for q in range(spans):
            rows_q = pl.ds(base + q * SPAN, SPAN)
            product = (bs[rows_q, :] * xs[rows_q, :]).astype(bf16)
            bx[rows_q, :] = product
            if m:
                v["halo_out"][m, q] = product[SPAN - 16 :, :]

    def mixer_rest(m):
        base = m * local
        at = pl.ds(base, local)
        if m == 0:
            projections[2].wait()
        cs[at, :] = dot_nn(n1[at, :], pc[...])
        halo(m).wait_recv()
        for q in range(spans):
            rows_q = pl.ds(base + q * SPAN, SPAN)
            mine, near, far = span_facts(m, q)
            far_term, near_term, here = terms(m, q, near, far, mine)
            conv = tap[0] * far_term + tap[1] * near_term + tap[2] * here
            ym[rows_q, :] = (cs[rows_q, :] * conv).astype(bf16)
            if m == 0 and q == 0:
                projections[3].wait()
            term0[rows_q, :] = dot_nn(ym[rows_q, :], po[...]).astype(bf16)
            piece = m * spans + q
            branch.start(piece)
            if piece > 0:
                branch.relay(piece - 1)

    def middle(p, x):
        branch.ready(p)

        @pl.loop(0, half // BLOCK)
        def _(r):
            at = rows_at((2 * p + place.h) * half + r * BLOCK, BLOCK)
            value = x[at, :].astype(f32) + branch.total(p, r)
            r1h[rows_at(p * half + r * BLOCK, BLOCK), :] = value
            _, unit = normal(value)
            n2[at, :] = (unit * gain_row(ffn_gain)).astype(bf16)

        branch.spread(p, n2).start()

    def masked(m):
        cot_load[m].wait()
        for q in range(spans):
            kept = mask[m : m + 1, q * SPAN : (q + 1) * SPAN].astype(f32)
            kept = jnp.transpose(jnp.broadcast_to(kept, (SPAN, SPAN)))
            rows_q = pl.ds(m * local + q * SPAN, SPAN)
            for c in range(width // SPAN):
                cols = pl.ds(c * SPAN, SPAN)
                g[rows_q, cols] = (g[rows_q, cols].astype(f32) * kept).astype(bf16)

    def front(slot, m):
        at = slice(m * local, (m + 1) * local)
        both = dot_nt(n2[at, :], wgu[slot])
        back = dot_nt(g[at, :], wdb[slot])
        gate, up = both[:, :TILE], both[:, TILE:]
        sigma = jax.nn.sigmoid(gate)
        silu = gate * sigma
        hb[at, :] = (silu * up).astype(bf16)
        dgu[at, :TILE] = (back * up * sigma * (1.0 + gate * (1.0 - sigma))).astype(bf16)
        dgu[at, TILE:] = (back * silu).astype(bf16)

    def mixer_forward(x, tails):
        x_load = [loading(m, v["tokens"].at[m], x.at[m * local : (m + 1) * local]) for m in range(MICRO)]
        for copy in [x_load[0]] + projections[:2] + [x_load[1]] + projections[2:] + cot_load + weights(0, 0):
            copy.start()
        x_load[0].wait()
        for q in range(spans):
            _, unit = normal(x[(q + 1) * SPAN - 16 : (q + 1) * SPAN, :].astype(f32))
            tails[q * 16 : (q + 1) * 16, :] = (unit * gain_row(mix_gain)).astype(bf16)
        projections[0].wait()
        projections[1].wait()
        ends = (dot_nn(tails[...], pb[...]) * dot_nn(tails[...], px[...])).astype(bf16)
        for q in range(spans):
            v["halo_out"][0, q] = ends[q * 16 : (q + 1) * 16]
        pl.semaphore_wait(barrier, 5 + line - 1)
        halo(0).start()
        mixer_half(0, x)
        x_load[1].wait()
        mixer_rest(0)
        mixer_half(1, x)
        halo(1).start()
        mixer_rest(1)
        masked(0)
        branch.relay(pieces - 1)
        masked(1)
        for m in range(MICRO):
            for p in range(m * spans, (m + 1) * spans):
                middle(p, x)
            for p in range(m * spans, (m + 1) * spans):
                branch.spread(p, n2).wait()
                branch.settle(p)
            if m == 0:
                for copy in weights(0, 0):
                    copy.wait()
                front(0, 0)

    pl.run_scoped(mixer_forward, pltpu.VMEM((tokens, width), bf16), pltpu.VMEM((16 * spans, width), bf16))

    def feed_forward(oacc, dacc):
        oacc[...] = jnp.zeros_like(oacc)
        dacc[...] = jnp.zeros_like(dacc)

        @pl.loop(0, n_ffn)
        def _(j):
            slot = lax.rem(j, 2)

            @pl.when(jnp.logical_and(j > 0, j < full))
            def _():
                for copy in weights(jnp.minimum(j, full - 1), slot):
                    copy.wait()

            if rest:

                @pl.when(j == full)
                def _():
                    for copy in rest_weights():
                        copy.wait()

            @pl.when(j + 1 < full)
            def _():
                for copy in weights(jnp.minimum(j + 1, full - 1), 1 - slot):
                    copy.start()

            if rest:

                @pl.when(j + 1 == full)
                def _():
                    blank = jnp.zeros((TILE - rest, width), bf16)
                    wgu[full % 2, rest:TILE, :] = blank
                    wgu[full % 2, TILE + rest :, :] = blank
                    wdb[full % 2, rest:, :] = blank
                    for copy in rest_weights():
                        copy.start()

            @pl.when(j > 0)
            def _():
                front(slot, 0)
                front(slot, 1)

            @pl.when(j == 0)
            def _():
                front(0, 1)

            rs.produce(3 * j, [(0, g, lambda: hb[...])])
            oacc[...] += dot_nn(hb[...], wdb[slot])
            rs.flush(3 * j)
            rs.start_halving(j)
            rs.produce(3 * j + 1, [(0, n2, lambda: dgu[:, :TILE])], flushed=True)
            rs.produce(3 * j + 2, [(0, n2, lambda: dgu[:, TILE:])])
            rs.begin(j)
            dacc[...] += dot_nn(dgu[...], wgu[slot])
            rs.complete(j)

        rs.flush(3 * n_ffn - 1)
        for p in range(pieces):
            at = pl.ds(p * SPAN, SPAN)
            term1[at, :] = dacc[at, :].astype(bf16)
            second.start(p)
            if p > 1:
                second.relay(p - 2)
        for p in range(pieces):
            at = pl.ds(p * SPAN, SPAN)
            term0[at, :] = oacc[at, :].astype(bf16)
            feed.start(p)
            if p < 2:
                second.relay(pieces - 2 + p)

    pl.run_scoped(
        feed_forward,
        pltpu.VMEM((tokens, width), f32),
        pltpu.VMEM((tokens, width), f32),
    )
    taken = [n_ffn]

    def pump(count):
        rs.pump(taken[0], taken[0] + count)
        taken[0] += count

    def backward(dr1, xh, dym, dbx, gain_one, gain_two, tap_rows):
        x_load = [
            loading(
                8 + p,
                v["tokens"].at[p // spans, rows_at(p % spans * SPAN + place.h * half, half)],
                xh.at[p * half : (p + 1) * half],
            )
            for p in range(pieces)
        ]
        for copy in x_load:
            copy.start()
        gain_one[...] = jnp.zeros_like(gain_one)
        gain_two[...] = jnp.zeros_like(gain_two)
        pump(2)
        for p in range(pieces):
            feed.relay(p)
        pump(1)

        for p in range(pieces):
            second.ready(p)

            @pl.loop(0, half // BLOCK)
            def _(r):
                at = rows_at((2 * p + place.h) * half + r * BLOCK, BLOCK)
                here = rows_at(p * half + r * BLOCK, BLOCK)
                grad = second.total(p, r)
                scale, unit = normal(r1h[here, :])
                gain_two[...] += fold(grad * unit)
                weighted = grad * gain_row(ffn_gain)
                inner = jnp.mean(weighted * unit, axis=-1, keepdims=True)
                value = g[at, :].astype(f32) + scale * (weighted - unit * inner)
                dr1[here, :] = value
                n2[at, :] = value.astype(bf16)

            second.spread(p, n2).start()
            if p == 2:
                pump(2)

        for p in range(pieces):
            second.spread(p, n2).wait()
            second.settle(p)
        dym[...] = dot_nt(n2[...], po[...])
        tap_sums = [jnp.zeros((8, chan), f32) for _ in range(3)]
        for m in range(MICRO):
            for q in range(spans):
                rows_q = pl.ds(m * local + q * SPAN, SPAN)
                mine, near, far = span_facts(m, q)
                far_term, near_term, here = terms(m, q, near, far, mine)
                grad = dym[rows_q, :]
                cat[rows_q, chan : 2 * chan] = (
                    grad * (tap[0] * far_term + tap[1] * near_term + tap[2] * here)
                ).astype(bf16)
                grad = grad * cs[rows_q, :]
                for k, other in enumerate((far_term, near_term, here)):
                    tap_sums[k] = tap_sums[k] + fold(grad * other)
                old = jnp.where(far, tap[0] * grad, 0.0)
                mid = jnp.where(near, tap[1] * grad, 0.0)
                dbx[rows_q, :] = (
                    tap[2] * grad
                    + jnp.where(row_ids < SPAN - 1, pltpu.roll(mid, SPAN - 1, 0), 0.0)
                    + jnp.where(row_ids < SPAN - 2, pltpu.roll(old, SPAN - 2, 0), 0.0)
                )
                top_ids = row_ids[:8]
                v["back_out"][m, q] = jnp.where(top_ids < 2, old[:8], 0.0) + jnp.where(
                    top_ids == 1, mid[0:1], 0.0
                )
            halo_back(m).start()
        pump(2)
        for k in range(3):
            tap_rows[k] = tap_sums[k]
        for m in range(MICRO):
            halo_back(m).wait_recv()
            for q in range(spans):
                rows_q = pl.ds(m * local + q * SPAN, SPAN)
                mine = order[m, place.s * spans + q]
                from_next = jnp.zeros((8, chan), f32)
                for k in range(spans):
                    took = order[m, place.after * spans + k] == mine + 1
                    from_next = from_next + jnp.where(took, v["back_in"][m, k], 0.0)
                value = dbx[rows_q, :]
                value = (
                    value
                    + jnp.where(row_ids == SPAN - 2, from_next[0:1], 0.0)
                    + jnp.where(row_ids == SPAN - 1, from_next[1:2], 0.0)
                )
                cat[rows_q, 0:chan] = (value * xs[rows_q, :]).astype(bf16)
                cat[rows_q, 2 * chan :] = (value * bs[rows_q, :]).astype(bf16)
        k0 = 3 * n_ffn
        wide = 3 * chan
        whole = wide // TILE
        for k in range(whole):
            rs.produce(k0 + k, [(0, n1, lambda k=k: cat[:, k * TILE : (k + 1) * TILE])])
            if k % 2 == 1:
                pump(1)
        left = wide - whole * TILE
        rs.produce(
            k0 + whole,
            [
                (0, n1, lambda: cat[:, whole * TILE :]),
                (left, n2, lambda: ym[:, 0 : TILE - left]),
            ],
        )
        rs.produce(k0 + whole + 1, [(0, n2, lambda: ym[:, TILE - left :])])
        rs.flush(k0 + whole + 1)
        assert taken[0] < rs.AHEAD + 13
        pump(1)

        for p in range(pieces):
            feed.ready(p)

            @pl.loop(0, half // BLOCK)
            def _(r):
                here = rows_at(p * half + r * BLOCK, BLOCK)
                at = rows_at(r * BLOCK, BLOCK)
                across2[p, at, :] = (r1h[here, :] + feed.total(p, r)).astype(bf16)

            for copy in feed.publish(p, across2, v["block_out"]):
                copy.start()
            feed.settle(p)
        pump(1)
        for m in range(MICRO):
            at = pl.ds(m * local, local)
            term0[at, :] = (
                dot_nt(cat[at, 0:chan], pb[...])
                + dot_nt(cat[at, chan : 2 * chan], pc[...])
                + dot_nt(cat[at, 2 * chan :], px[...])
            ).astype(bf16)
            for p in range(m * spans, (m + 1) * spans):
                first.start(p)
        for p in range(pieces):
            first.relay(p)
        pump(2)
        for p in range(pieces):
            x_load[p].wait()
            first.ready(p)

            @pl.loop(0, half // BLOCK)
            def _(r):
                here = rows_at(p * half + r * BLOCK, BLOCK)
                at = rows_at(r * BLOCK, BLOCK)
                grad = first.total(p, r)
                scale, unit = normal(xh[here, :].astype(f32))
                gain_one[...] += fold(grad * unit)
                weighted = grad * gain_row(mix_gain)
                inner = jnp.mean(weighted * unit, axis=-1, keepdims=True)
                across0[p, at, :] = (dr1[here, :] + scale * (weighted - unit * inner)).astype(bf16)

            for copy in first.publish(p, across0, v["d_tokens"]):
                copy.start()
            if p % 2 == 1:
                pump(1)

        small, gather = v["small"], v["gather"]
        ssem = v["ssem"]
        side = width // 2
        small[0] = jnp.zeros((8, side), f32)
        for n, gain in enumerate((gain_one, gain_two)):
            row = jnp.sum(gain[...], axis=0, keepdims=True)
            small[0, 2 * n : 2 * n + 1, :] = row[:, :side]
            small[0, 2 * n + 1 : 2 * n + 2, :] = row[:, side:]
        for k in range(3):
            at = k % 2 * chan
            small[0, 4 + k // 2 : 5 + k // 2, at : at + chan] = jnp.sum(tap_rows[k], axis=0, keepdims=True)
        core = send_to(small.at[0], gather.at[0], ssem.at[0], ssem.at[1], place.core)
        core.start()
        pump(1)
        core.wait_recv()
        small[1] = small[0] + jnp.where(lax.broadcasted_iota(jnp.int32, (8, 1), 0) < 4, gather[0], 0.0)
        pair = send_to(small.at[1], gather.at[1], ssem.at[2], ssem.at[3], place.pair)
        pair.start()
        pump(3)
        pair.wait_recv()
        small[2] = small[1] + gather[1]

        def along(c, slot):
            return send_to(
                small.at[2], gather.at[2 + slot], ssem.at[4 + c], ssem.at[4 + line + slot], (c * 2 + place.b, place.t)
            )

        @pl.loop(0, line)
        def _(c):
            @pl.when(c != place.a)
            def _():
                along(c, place.a).start()

        gather[2 + place.a] = small[2]

        rs.pump(taken[0], rs.steps)

        @pl.loop(0, line)
        def _(c):
            @pl.when(c != place.a)
            def _():
                along(c, c).wait_recv()
                along(c, place.a).wait_send()

        total = gather[2]
        for c in range(1, line):
            total = total + gather[2 + c]
        v["small_out"][...] = total
        core.wait_send()
        pair.wait_send()
        for m in range(MICRO):
            halo(m).wait_send()
            halo_back(m).wait_send()
        for m in range(pieces):
            first.settle(m)
            for each, staged, out in ((feed, across2, v["block_out"]), (first, across0, v["d_tokens"])):
                for copy in each.publish(m, staged, out):
                    copy.wait()
        rs.finish()

    pl.run_scoped(
        backward,
        pltpu.VMEM((tokens // 2, width), f32),
        pltpu.VMEM((tokens // 2, width), bf16),
        pltpu.VMEM((tokens, chan), f32),
        pltpu.VMEM((tokens, chan), f32),
        pltpu.VMEM((8, width), f32),
        pltpu.VMEM((8, width), f32),
        pltpu.VMEM((3, 8, chan), f32),
    )


def body(
    seq_count,
    tokens,
    mix_gain,
    proj_b,
    proj_c,
    proj_x,
    conv_taps,
    proj_out,
    ffn_gain,
    w_gate,
    w_up,
    w_down,
    cotangent,
    seq_lengths,
    span_order,
    keep_mask,
):
    local, width = tokens.shape[1:]
    total = MICRO * local
    half = SPAN // 2
    chan = proj_b.shape[1]
    units = w_gate.shape[1]
    n_ffn = pl.cdiv(units, TILE)
    line = seq_count // 2
    rows = width // seq_count
    n_tiles = 3 * n_ffn + 6
    spans = local // SPAN
    pieces = MICRO * spans
    dma = pltpu.SemaphoreType.DMA
    vmem = pl.BlockSpec(memory_space=pltpu.VMEM)
    smem = pl.BlockSpec(memory_space=pltpu.SMEM)
    hbm = pl.BlockSpec(memory_space=pl.ANY)
    shape = jax.ShapeDtypeStruct
    inputs = [
        ("lengths", seq_lengths, smem),
        ("order", span_order, smem),
        ("mask", keep_mask, vmem),
        ("mix_gain", mix_gain, vmem),
        ("ffn_gain", ffn_gain, vmem),
        ("taps", conv_taps, vmem),
        ("tokens", tokens, hbm),
        ("cotangent", cotangent, hbm),
        ("proj_b", proj_b, hbm),
        ("proj_c", proj_c, hbm),
        ("proj_x", proj_x, hbm),
        ("proj_out", proj_out, hbm),
        ("w_gate", w_gate.T, hbm),
        ("w_up", w_up.T, hbm),
        ("w_down", w_down, hbm),
    ]
    outputs = [
        ("block_out", shape((total, width), bf16), hbm),
        ("d_tokens", shape((total, width), bf16), hbm),
        ("grads", shape((4, rows, n_ffn * TILE), f32), hbm),
        ("small_out", shape((8, width // 2), f32), vmem),
        ("wbuf", shape((n_tiles, 2, line, rows, TILE), bf16), hbm),
        ("ybuf", shape((n_tiles, line, rows, TILE), bf16), hbm),
    ]
    scratch = [
        ("n1", pltpu.VMEM((total, width), bf16)),
        ("n2", pltpu.VMEM((total, width), bf16)),
        ("g", pltpu.VMEM((total, width), bf16)),
        ("term0", pltpu.VMEM((total, width), bf16)),
        ("term1", pltpu.VMEM((total, width), bf16)),
        ("r1h", pltpu.VMEM((total // 2, width), f32)),
        ("inbox0", pltpu.VMEM((pieces, half, width), bf16)),
        ("inbox1", pltpu.VMEM((pieces, half, width), bf16)),
        ("across0", pltpu.VMEM((pieces, half, width), bf16)),
        ("across1", pltpu.VMEM((pieces, half, width), bf16)),
        ("across2", pltpu.VMEM((pieces, half, width), bf16)),
        ("pb", pltpu.VMEM((width, chan), bf16)),
        ("pc", pltpu.VMEM((width, chan), bf16)),
        ("px", pltpu.VMEM((width, chan), bf16)),
        ("po", pltpu.VMEM((chan, width), bf16)),
        ("bs", pltpu.VMEM((total, chan), f32)),
        ("cs", pltpu.VMEM((total, chan), f32)),
        ("xs", pltpu.VMEM((total, chan), f32)),
        ("bx", pltpu.VMEM((total, chan), bf16)),
        ("ym", pltpu.VMEM((total, chan), bf16)),
        ("cat", pltpu.VMEM((total, 3 * chan), bf16)),
        ("wgu", pltpu.VMEM((2, 2 * TILE, width), bf16)),
        ("wdb", pltpu.VMEM((2, TILE, width), bf16)),
        ("hb", pltpu.VMEM((total, TILE), bf16)),
        ("dgu", pltpu.VMEM((total, 2 * TILE), bf16)),
        ("halo_out", pltpu.VMEM((MICRO, spans, 16, chan), bf16)),
        ("halo_in", pltpu.VMEM((MICRO, spans, 16, chan), bf16)),
        ("back_out", pltpu.VMEM((MICRO, spans, 8, chan), f32)),
        ("back_in", pltpu.VMEM((MICRO, spans, 8, chan), f32)),
        ("small", pltpu.VMEM((3, 8, width // 2), f32)),
        ("gather", pltpu.VMEM((2 + line, 8, width // 2), f32)),
        ("load", dma((8 + pieces,))),
        ("wsem", dma((2, 3))),
        ("sums", dma((4, pieces, 7))),
        ("hsem", dma((4, MICRO))),
        ("ssem", dma((4 + 2 * line,))),
    ]
    scratch += list(zip(Scatter.NAMES, Scatter.scratch(n_tiles, line, rows)))
    names = [n for n, _, _ in inputs] + [n for n, _, _ in outputs] + [n for n, _ in scratch]
    results = pl.pallas_call(
        functools.partial(kernel, line, rows, n_ffn, names),
        out_shape=tuple(s for _, s, _ in outputs),
        in_specs=[s for _, _, s in inputs],
        out_specs=tuple(s for _, _, s in outputs),
        scratch_shapes=[s for _, s in scratch],
        compiler_params=pltpu.CompilerParams(
            collective_id=0, has_side_effects=True, vmem_limit_bytes=62 * 2**20 - 2**19
        ),
    )(*[a for _, a, _ in inputs])
    done = finish_call(results[2:4], width, chan, units, rows)
    return (
        results[0].reshape(tokens.shape),
        results[1].reshape(tokens.shape),
        done[0],
        done[1],
        done[2],
        done[3],
        done[4],
        done[5].T,
        done[6],
        done[7],
        done[8],
        done[9].T,
    )


def finish_kernel(
    grads, small, d_mixgain, d_b, d_c, d_x, d_taps, d_out, d_ffngain, d_gate, d_up, d_down
):
    chan, units = d_b.shape[1], d_gate.shape[1]
    side = small.shape[1]
    for n, out in enumerate((d_b, d_c, d_x, d_out)):
        out[...] = grads[3, :, n * chan : (n + 1) * chan]
    for n, out in enumerate((d_down, d_gate, d_up)):
        out[...] = grads[n, :, :units]

    @pl.when(pl.program_id(0) == 0)
    def _():
        for n, out in enumerate((d_mixgain, d_ffngain)):
            out[0:side] = small[2 * n : 2 * n + 1, :].reshape(side)
            out[side:] = small[2 * n + 1 : 2 * n + 2, :].reshape(side)
        for k in range(3):
            at = k % 2 * chan
            d_taps[k : k + 1, :] = small[4 + k // 2 : 5 + k // 2, at : at + chan]


def finish_call(arrays, width, chan, units, rows):
    cuts = 3
    shape = jax.ShapeDtypeStruct

    def by_rows(count, columns):
        return pl.BlockSpec((count // cuts, columns), lambda i: (i, 0))

    def whole(*sizes):
        return pl.BlockSpec(sizes, lambda i: (0,) * len(sizes))

    return pl.pallas_call(
        finish_kernel,
        grid=(cuts,),
        in_specs=[
            pl.BlockSpec((4, rows // cuts, arrays[0].shape[2]), lambda i: (0, i, 0)),
            whole(*arrays[1].shape),
        ],
        out_shape=(
            shape((width,), f32),
            shape((rows, chan), f32),
            shape((rows, chan), f32),
            shape((rows, chan), f32),
            shape((3, chan), f32),
            shape((rows, chan), f32),
            shape((width,), f32),
            shape((rows, units), f32),
            shape((rows, units), f32),
            shape((rows, units), f32),
        ),
        out_specs=(
            whole(width),
            by_rows(rows, chan),
            by_rows(rows, chan),
            by_rows(rows, chan),
            whole(3, chan),
            by_rows(rows, chan),
            whole(width),
            by_rows(rows, units),
            by_rows(rows, units),
            by_rows(rows, units),
        ),
    )(*arrays)


def solution(mesh):
    placed = (
        P(None, "seq", None),
        P(),
        P(None, "tp"),
        P(None, "tp"),
        P(None, "tp"),
        P(None, "tp"),
        P("tp", None),
        P(),
        P(None, "tp"),
        P(None, "tp"),
        P("tp", None),
        P(None, "seq", None),
        P(),
        P(),
        P(None, "seq"),
    )
    return jax.shard_map(
        functools.partial(body, mesh.shape["seq"]),
        mesh=mesh,
        in_specs=placed,
        out_specs=(
            P(None, "seq", None),
            P(None, "seq", None),
            P(),
            P("seq", "tp"),
            P("seq", "tp"),
            P("seq", "tp"),
            P(None, "tp"),
            P("tp", "seq"),
            P(),
            P("seq", "tp"),
            P("seq", "tp"),
            P("tp", "seq"),
        ),
        check_vma=False,
    )
```
